32 devices in a mesh: groups: 2 (over y), expert: 8 (over z, core), replica: 2 (over x).
Axes of the slice: x: 2, y: 2, z: 4, core: 2. Of those that a mesh axis runs over, the one named last changes fastest.
Arguments:
- hidden_in: bfloat16 [2048, 2048], P(('groups', 'expert'), 'replica'), parts along dimension 0, may hold values from -6 to 6
- routes: int32 [2048, 8], P(('groups', 'expert')), parts along dimension 0, may hold values from 0 to 15, all different within a row; in each aligned block of 128 rows (0 to 127, 128 to 255, ...) at most 128 rows name the same one
- route_gain: float32 [2048, 8], P(('groups', 'expert')), parts along dimension 0, may hold values from 0.1 to 1
- w_in: bfloat16 [16, 2048, 768], P('expert', 'replica'), may hold values from -0.125 to 0.125
- w_out: bfloat16 [16, 384, 2048], P('expert', None, 'replica'), may hold values from -0.3125 to 0.3125
- handoff: bfloat16 [2048, 1024], P('replica'), may hold values from -0.125 to 0.125
- speaking: int32 [2048], P(('groups', 'expert')), parts along dimension 0, may hold values 0 or 1
- talker_routes: int32 [2048, 8], P(('groups', 'expert')), parts along dimension 0, may hold values from 0 to 15, all different within a row; in each aligned block of 128 rows (0 to 127, 128 to 255, ...) at most 96 rows name the same one
- talker_gain: float32 [2048, 8], P(('groups', 'expert')), parts along dimension 0, may hold values from 0.1 to 1
- talker_w_in: bfloat16 [16, 1024, 768], P('expert', 'replica'), may hold values from -0.1875 to 0.1875
- talker_w_out: bfloat16 [16, 384, 1024], P('expert', None, 'replica'), may hold values from -0.3125 to 0.3125
Outputs:
- thinker_out: bfloat16 [2048, 2048], P(('groups', 'expert'), 'replica'), parts along dimension 0
- talker_out: bfloat16 [2048, 1024], P(('groups', 'expert'), 'replica'), parts along dimension 0
The draws below stay inside these ranges and needn't reach their ends.
There are 2 independent parts, one for each index of `groups`. The reference program is written for one: setup_inputs(seed, part) draws one part's arguments, and reference() takes and returns one part's arrays. A program takes and returns all parts, laid end to end along the dimension named above; an argument that names none is the same for every part. Nothing has to cross between parts.
Inputs may be any that keep to these rules, and one draw needn't show every extreme that they name: `routes`: each row names 8 different experts; in the 128 rows of one index of expert no expert is named more than 128 times, a bound that some block reaches. `talker_routes`: each row names 8 different experts; in the 128 rows of one index of expert no expert is named more than 96 times, a bound that some block reaches.
All inputs are finite; a program needn't handle non-finite values. No bound on the sum of `speaking` on one device may be relied on, other than what follows from the above.
Results may differ from the reference program's by a relative error of at most 0.04.
Values may be sent and summed in bfloat16 or wider, within the bound.
No kernel may reach another device: no remote copies, remote signals or barrier semaphores. Data moves between devices by JAX's collectives and lax.ppermute only.
A program may use at most 64 MiB of HBM per device.

```python
import math
import jax
import jax.numpy as jnp
import numpy as np
from jax import lax

D = 2048
FF = 384
DK = 1024
FK = 384
TOP = 8
TOK_DEV = 128
E = 16
CAP = 128
CAPK = 96
TOKENS = 1024
N_EXPERT = 8
N_REPLICA = 2


def with_ends(drawn, key, low, top_value):
    longest = drawn.shape.index(max(drawn.shape))
    spots = []
    for shift in (0, 1):
        where = [jax.random.randint(jax.random.fold_in(key, axis), (), 0, length) for axis, length in enumerate(drawn.shape)]
        where[longest] = (where[longest] + shift) % drawn.shape[longest]
        spots.append(tuple(where))
    return drawn.at[spots[0]].set(low).at[spots[1]].set(top_value)


def block_scale(own_key, shape, shards, least, largest):
    def one(axis_at, parts):
        draws = jax.random.uniform(jax.random.fold_in(jax.random.fold_in(own_key, 6), axis_at), (parts,), jnp.float32, least / len(shards), largest / len(shards))
        return jnp.repeat(jnp.exp(draws), shape[axis_at] // parts).reshape((-1,) + (1,) * (len(shape) - axis_at - 1))

    factor_of = one(*shards[0])
    for cut in shards[1:]:
        factor_of = factor_of * one(*cut)
    return factor_of


def assign_block(rng, own, number, rows, amount, top, bound, slope):
    sequence = jax.random.permutation(rng, amount)
    crowded, common = portions_of(amount, rows * top, bound, slope, True), portions_of(amount, rows * top, bound, slope, False)
    places = jnp.arange(amount)

    def named(tallies, rotation):
        used = int((tallies > 0).sum())
        fixed = max(1, used // 4)
        passed = fixed + (places - fixed + rotation * (used - fixed)) % max(1, amount - fixed)
        return jnp.zeros((amount,), jnp.int32).at[sequence[jnp.where(places < fixed, places, passed)]].set(jnp.asarray(tallies, jnp.int32))

    tallies = jnp.where(number % 4 == 0, named(crowded, number // 4), named(common, number - number // 4 - 1))
    mixed = jax.random.permutation(jax.random.fold_in(own, 3), amount)
    donor, sink = mixed[0:amount // 2 * 2:2], mixed[1:amount // 2 * 2:2]
    margin = jnp.minimum(tallies[donor] - 1, bound - tallies[sink]) // 2
    margin = jnp.where((donor == sequence[0]) | (sink == sequence[0]) | (tallies[sink] == 0), 0, jnp.maximum(margin, 0))
    passed = jax.random.randint(jax.random.fold_in(own, 4), (amount // 2,), 0, 1 << 20) % (margin + 1)
    tallies = tallies.at[donor].add(-passed).at[sink].add(passed)
    labels = jnp.searchsorted(jnp.cumsum(tallies), jnp.arange(rows * top), side="right").astype(jnp.int32)
    listing = labels.reshape(top, rows).T
    listing = listing[jax.random.permutation(jax.random.fold_in(own, 1), rows)]
    rotation = jax.random.randint(jax.random.fold_in(own, 2), (rows, 1), 0, top)
    return jnp.take_along_axis(listing, (jnp.arange(top)[None, :] + rotation) % top, axis=1)


def portions_of(count, total, limit, lean, full):
    portions = [(1 << 20) // math.isqrt(rank ** lean) + 1 for rank in range(1, count + 1)]
    largest = limit if full else min(limit, max(-(-total // count), total * portions[0] // sum(portions)))
    least = 1 if total - largest >= count - 1 else 0
    holding, surplus = [largest] + [least] * (count - 1), total - largest - least * (count - 1)
    while surplus > 0:
        free = [i for i in range(1, count) if holding[i] < largest] or [i for i in range(1, count) if holding[i] < limit]
        pool, left = sum([portions[i] for i in free]), surplus
        for i in free:
            extra = min(limit - holding[i], max(1, left * portions[i] // pool), surplus)
            holding[i] = holding[i] + extra
            surplus = surplus - extra
    return np.array(holding)


def scatter_about(own_key, dims, scale, reach, pieces=(), kind=jnp.bfloat16):
    factor_of = block_scale(own_key, dims, pieces, -0.22, 0.18) if pieces else 1.0
    array = jax.random.normal(own_key, dims, jnp.float32) * scale * factor_of
    return jnp.minimum(jnp.maximum(array, -reach), reach).astype(kind)


def setup_inputs(seed: int = 0, part: int = 0) -> dict:
    key_of = jax.random.split(jax.random.key(seed), 12)
    own_keys = jax.random.split(jax.random.fold_in(key_of[11], part), 12)
    hidden_in = scatter_about(own_keys[0], (TOKENS, D), 1.0, 6.0, ((0, 8), (1, 2)))
    routes_keys = jax.random.split(jax.random.fold_in(own_keys[1], 1), TOKENS // TOK_DEV)
    routes_turns = jax.random.permutation(jax.random.fold_in(own_keys[1], 3), TOKENS // TOK_DEV)
    routes = jax.vmap(lambda own, number: assign_block(jax.random.fold_in(own_keys[1], 2), own, number, TOK_DEV, E, TOP, CAP, 2))(routes_keys, routes_turns).reshape((TOKENS, TOP))
    route_gain = jnp.clip(jnp.exp(math.log(1.0) - 2.3025851 * jax.random.uniform(own_keys[2], (TOKENS, TOP), jnp.float32) ** block_scale(own_keys[2], (TOKENS, TOP), ((0, 8),), -0.2, 0.2)), 0.1, 1.0)
    w_in = scatter_about(key_of[3], (E, D, 2 * FF), D ** -0.5, 0.125, ((0, 8), (1, 2)))
    w_out = scatter_about(key_of[4], (E, FF, D), FF ** -0.5, 0.3125, ((0, 8), (2, 2)))
    handoff = scatter_about(key_of[5], (D, DK), D ** -0.5, 0.125, ((0, 2),))
    speaking = with_ends((jax.random.randint(own_keys[6], (TOKENS,), 0, 2) < 1).astype(jnp.int32), jax.random.fold_in(own_keys[6], 1), 0, 1)
    talker_routes_keys = jax.random.split(jax.random.fold_in(own_keys[7], 1), TOKENS // TOK_DEV)
    talker_routes_turns = jax.random.permutation(jax.random.fold_in(own_keys[7], 3), TOKENS // TOK_DEV)
    talker_routes = jax.vmap(lambda own, number: assign_block(jax.random.fold_in(own_keys[7], 2), own, number, TOK_DEV, E, TOP, CAPK, 2))(talker_routes_keys, talker_routes_turns).reshape((TOKENS, TOP))
    talker_gain = jnp.clip(jnp.exp(math.log(1.0) - 2.3025851 * jax.random.uniform(own_keys[8], (TOKENS, TOP), jnp.float32) ** block_scale(own_keys[8], (TOKENS, TOP), ((0, 8),), -0.2, 0.2)), 0.1, 1.0)
    talker_w_in = scatter_about(key_of[9], (E, DK, 2 * FK), DK ** -0.5, 0.1875, ((0, 8), (1, 2)))
    talker_w_out = scatter_about(key_of[10], (E, FK, DK), FK ** -0.5, 0.3125, ((0, 8), (2, 2)))
    return dict(hidden_in=hidden_in, routes=routes, route_gain=route_gain, w_in=w_in, w_out=w_out, handoff=handoff, speaking=speaking, talker_routes=talker_routes, talker_gain=talker_gain, talker_w_in=talker_w_in, talker_w_out=talker_w_out)


def mixture(tok_rows, route_ids, live_flags, capacity, first_weights, second_weights):
    row_width = tok_rows.shape[1]
    part_width = row_width // N_REPLICA
    hidden_width = first_weights.shape[2] // 2
    flat_ids = route_ids.reshape(N_EXPERT, TOK_DEV * TOP)
    live_rows = live_flags.reshape(N_EXPERT, TOK_DEV * TOP)
    onehot = (flat_ids[:, :, None] == jnp.arange(E, dtype=jnp.int32)[None, None, :]).astype(jnp.int32) * live_rows[:, :, None]
    before = jnp.cumsum(onehot, axis=1) - onehot
    slot_rank = jnp.sum(before * onehot, axis=2).astype(jnp.int32)
    position = (jnp.arange(N_EXPERT, dtype=jnp.int32)[:, None] * capacity + slot_rank).reshape(-1).astype(jnp.int32)
    target = jnp.where(live_rows.reshape(-1) > 0, flat_ids.reshape(-1), E).astype(jnp.int32)
    spread = jnp.repeat(tok_rows, TOP, axis=0)
    buffer = jnp.zeros((E, N_EXPERT * capacity, row_width), jnp.bfloat16).at[target, position].set(spread, mode="drop")

    def run_expert(operands):
        expert_rows, w_first, w_second = operands
        summed = jnp.zeros((expert_rows.shape[0], 2 * hidden_width), jnp.float32)
        for shard in range(N_REPLICA):
            lower = shard * part_width
            partial_term = jnp.dot(expert_rows[:, lower:lower + part_width], w_first[lower:lower + part_width], preferred_element_type=jnp.float32).astype(jnp.bfloat16)
            summed = summed + lax.optimization_barrier(partial_term).astype(jnp.float32)
        hidden = (jax.nn.silu(summed[:, :hidden_width]) * summed[:, hidden_width:]).astype(jnp.bfloat16)
        return jnp.dot(hidden, w_second, preferred_element_type=jnp.float32).astype(jnp.bfloat16)

    result = lax.map(run_expert, (buffer, first_weights, second_weights))
    picked = result[jnp.minimum(target, E - 1), position].astype(jnp.float32)
    return picked.reshape(TOKENS, TOP, row_width), live_rows.reshape(TOKENS, TOP).astype(jnp.float32)


def reference(hidden_in, routes, route_gain, w_in, w_out, handoff, speaking, talker_routes, talker_gain, talker_w_in, talker_w_out):
    all_rows = jnp.ones((TOKENS * TOP,), jnp.int32)
    thinker_rows, unused_live = mixture(hidden_in, routes, all_rows, CAP, w_in, w_out)
    thinker_out = jnp.sum(thinker_rows * route_gain[:, :, None], axis=1).astype(jnp.bfloat16)
    talker_in = jnp.dot(thinker_out, handoff, preferred_element_type=jnp.float32).astype(jnp.bfloat16)
    speak_rows = jnp.repeat(speaking, TOP)
    talker_rows, live_rows = mixture(talker_in, talker_routes, speak_rows, CAPK, talker_w_in, talker_w_out)
    weights = talker_gain * live_rows
    talker_out = jnp.sum(talker_rows * weights[:, :, None], axis=1).astype(jnp.bfloat16)
    return thinker_out, talker_out
```

```python
import functools

import jax
import jax.numpy as jnp
from jax import lax
from jax.experimental import pallas as pl
from jax.experimental.pallas import tpu as pltpu
from jax.sharding import PartitionSpec as P

LANES = 128
SWAP = [(0, 1), (1, 0)]


def place_rows(tok_rows, flat_ids, live_rows, experts, capacity):
    onehot = (flat_ids[:, None] == lax.iota(jnp.int32, experts)[None, :]).astype(
        jnp.int32
    ) * live_rows[:, None]
    before = jnp.cumsum(onehot, axis=0) - onehot
    slot_rank = jnp.sum(before * onehot, axis=1)
    slot_index = jnp.where(live_rows > 0, flat_ids * capacity + slot_rank, experts * capacity)
    buffer = (
        jnp.zeros((experts * capacity, tok_rows.shape[1]), tok_rows.dtype)
        .at[slot_index]
        .set(tok_rows, mode="drop")
    )
    return (buffer, slot_index)


def activate(gate_sum, up_sum):
    return (jax.nn.silu(gate_sum) * up_sum).astype(jnp.bfloat16)


def down_rows(second_weights, piece):
    return jnp.einsum("lrf,lfd->lrd", piece, second_weights, preferred_element_type=jnp.float32)


def routed_on_device(
    hidden_in,
    routes,
    route_gain,
    w_in,
    w_out,
    handoff,
    speaking,
    talker_routes,
    talker_gain,
    talker_w_in,
    talker_w_out,
):
    owners = lax.axis_size("expert")
    token_count, top_count = routes.shape
    local_experts = w_in.shape[0]
    experts = local_experts * owners
    capacity = max(2, token_count * top_count * 2 // experts)
    talker_capacity = max(2, capacity * 3 // 4)
    flat_ids = routes.reshape(-1)
    all_rows = jnp.ones_like(flat_ids)
    spread = jnp.repeat(hidden_in, top_count, axis=0)
    buffer, slot_index = place_rows(spread, flat_ids, all_rows, experts, capacity)
    arrived = lax.all_to_all(
        buffer.reshape(owners, local_experts, capacity, -1),
        "expert",
        split_axis=0,
        concat_axis=2,
        tiled=True,
    )
    partial_value = jnp.einsum("lrd,ldf->lrf", arrived[0], w_in, preferred_element_type=jnp.float32)
    hidden_width = w_in.shape[2] // 2
    share_sum = lax.psum_scatter(
        partial_value.astype(jnp.bfloat16), "replica", scatter_dimension=1, tiled=True
    ).astype(jnp.float32)
    hidden = activate(share_sum[:, :, :hidden_width], share_sum[:, :, hidden_width:])
    expert_out = down_rows(w_out, lax.all_gather(hidden, "replica", axis=1, tiled=True))
    returned = lax.all_to_all(
        expert_out.astype(jnp.bfloat16)[None], "expert", split_axis=2, concat_axis=0, tiled=True
    )
    returned = returned.reshape(experts * capacity, -1)
    picked = returned[slot_index].astype(jnp.float32).reshape(token_count, top_count, -1)
    thinker_out = jnp.sum(picked * route_gain[:, :, None], axis=1).astype(jnp.bfloat16)
    handoff_terms = jnp.dot(thinker_out, handoff, preferred_element_type=jnp.float32)
    talker_in = lax.psum_scatter(
        handoff_terms.astype(jnp.bfloat16), "replica", scatter_dimension=1, tiled=True
    )
    talker_ids = talker_routes.reshape(-1)
    speak_rows = jnp.repeat(speaking, top_count)
    talker_spread = jnp.repeat(talker_in, top_count, axis=0)
    talker_buffer, talker_slots = place_rows(
        talker_spread, talker_ids, speak_rows, experts, talker_capacity
    )
    talker_arrived = lax.all_to_all(
        talker_buffer.reshape(owners, local_experts, talker_capacity, -1),
        "expert",
        split_axis=0,
        concat_axis=2,
        tiled=True,
    )
    talker_partial = jnp.einsum(
        "lrd,ldf->lrf", talker_arrived[0], talker_w_in, preferred_element_type=jnp.float32
    )
    talker_hidden_width = talker_w_in.shape[2] // 2
    talker_share = lax.psum_scatter(
        talker_partial.astype(jnp.bfloat16), "replica", scatter_dimension=1, tiled=True
    ).astype(jnp.float32)
    talker_hidden = activate(
        talker_share[:, :, :talker_hidden_width], talker_share[:, :, talker_hidden_width:]
    )
    talker_expert_out = down_rows(
        talker_w_out, lax.all_gather(talker_hidden, "replica", axis=1, tiled=True)
    )
    talker_returned = lax.all_to_all(
        talker_expert_out.astype(jnp.bfloat16)[None],
        "expert",
        split_axis=2,
        concat_axis=0,
        tiled=True,
    )
    talker_returned = talker_returned.reshape(experts * talker_capacity, -1)
    safe_slots = jnp.minimum(talker_slots, experts * talker_capacity - 1)
    talker_picked = (
        talker_returned[safe_slots].astype(jnp.float32).reshape(token_count, top_count, -1)
    )
    talker_weights = talker_gain * speak_rows.reshape(token_count, top_count).astype(jnp.float32)
    talker_out = jnp.sum(talker_picked * talker_weights[:, :, None], axis=1).astype(jnp.bfloat16)
    return (thinker_out, talker_out)


def split_gain(ids, gain, experts):
    hits = ids[:, :, None] == lax.iota(jnp.int32, experts)[None, None, :]
    dense = jnp.sum(jnp.where(hits, gain[:, :, None], 0.0), axis=1)
    high = lax.reduce_precision(dense, 8, 7)
    return [high.astype(jnp.bfloat16), (dense - high).astype(jnp.bfloat16)]


def expert_kernel(first_lane, experts, owner_ref, x_ref, gain_ref, first_ref, second_ref, out_ref, total):
    step = pl.program_id(0)
    halves, part = first_ref.shape[0], first_ref.shape[2]
    hidden_width = first_ref.shape[3] // 2
    out_part = second_ref.shape[3]
    lane = lax.broadcasted_iota(jnp.int32, gain_ref.shape, 1) - (
        first_lane + owner_ref[0] * pl.num_programs(0) + step
    )
    gain = jnp.sum(
        jnp.where((lane == 0) | (lane == experts), gain_ref[...].astype(jnp.float32), 0.0),
        axis=1,
        keepdims=True,
    )
    summed = jnp.dot(x_ref[:, :part], first_ref[0, 0], preferred_element_type=jnp.float32)
    for half in range(1, halves):
        summed += jnp.dot(
            x_ref[:, half * part : (half + 1) * part],
            first_ref[half, 0],
            preferred_element_type=jnp.float32,
        )
    hidden = (jax.nn.silu(summed[:, :hidden_width]) * summed[:, hidden_width:] * gain).astype(
        jnp.bfloat16
    )
    for half in range(halves):
        columns = slice(half * out_part, (half + 1) * out_part)
        term = jnp.dot(hidden, second_ref[half, 0], preferred_element_type=jnp.float32)

        @pl.when(step == 0)
        def _():
            total[:, columns] = term

        @pl.when(step > 0)
        def _():
            total[:, columns] += term

    @pl.when(step == pl.num_programs(0) - 1)
    def _():
        out_ref[...] = total[...].astype(jnp.bfloat16)


def run_experts(owner, rows, gain_rows, gain_block, first_lane, first, second, experts):
    count = rows.shape[0]
    halves, local_experts, part, width = first.shape
    hidden_width, out_part = second.shape[2:]
    flops = 2 * count * local_experts * halves * (part * width + hidden_width * out_part)
    return pl.pallas_call(
        functools.partial(expert_kernel, first_lane, experts),
        out_shape=jax.ShapeDtypeStruct((count, halves * out_part), jnp.bfloat16),
        grid_spec=pltpu.PrefetchScalarGridSpec(
            num_scalar_prefetch=1,
            grid=(local_experts,),
            in_specs=[
                pl.BlockSpec((count, halves * part), lambda e, o: (0, 0)),
                pl.BlockSpec((count, LANES), lambda e, o: (0, gain_block)),
                pl.BlockSpec((halves, 1, part, width), lambda e, o: (0, e, 0, 0)),
                pl.BlockSpec((halves, 1, hidden_width, out_part), lambda e, o: (0, e, 0, 0)),
            ],
            out_specs=pl.BlockSpec((count, halves * out_part), lambda e, o: (0, 0)),
            scratch_shapes=[pltpu.VMEM((count, halves * out_part), jnp.float32)],
        ),
        compiler_params=pltpu.CompilerParams(vmem_limit_bytes=48 * 1024 * 1024),
        cost_estimate=pl.CostEstimate(
            flops=flops,
            bytes_accessed=2 * (rows.size + first.size + second.size + count * halves * out_part),
            transcendentals=count * local_experts * hidden_width,
        ),
    )(owner, rows, gain_rows, first, second)


def both_halves(weights):
    mine = lax.dynamic_index_in_dim(weights, lax.axis_index("groups"), 0, keepdims=False)
    whole = lax.all_gather(mine, ("replica", "groups"))
    return whole.reshape((lax.axis_size("replica"), lax.axis_size("groups")) + mine.shape)


def in_order(replica, own, other, axis):
    return jnp.concatenate(
        [jnp.where(replica == 0, own, other), jnp.where(replica == 0, other, own)], axis=axis
    )


def trade(replica, array, axis):
    size = array.shape[axis] // 2
    own = lax.dynamic_slice_in_dim(array, replica * size, size, axis)
    give = lax.dynamic_slice_in_dim(array, (1 - replica) * size, size, axis)
    return own, lax.ppermute(give, "replica", SWAP)


def dense_on_device(
    hidden_in,
    routes,
    route_gain,
    w_in,
    w_out,
    handoff,
    speaking,
    talker_routes,
    talker_gain,
    talker_w_in,
    talker_w_out,
):
    owners = lax.axis_size("expert")
    replica = lax.axis_index("replica")
    owner = lax.axis_index("expert").astype(jnp.int32).reshape(1)
    experts = w_in.shape[0] * owners
    rows = routes.shape[0] // 2
    first, second = both_halves(w_in), both_halves(w_out)
    talker_first, talker_second = both_halves(talker_w_in), both_halves(talker_w_out)

    def my_rows(array):
        return lax.dynamic_slice_in_dim(array, replica * rows, rows, 0)

    live = my_rows(speaking).astype(jnp.float32)[:, None]
    gains = split_gain(my_rows(routes), my_rows(route_gain), experts) + split_gain(
        my_rows(talker_routes), my_rows(talker_gain) * live, experts
    )
    gains.append(jnp.zeros((rows, LANES - 4 * experts), jnp.bfloat16))
    own, other = trade(replica, hidden_in, 0)
    row = jnp.concatenate([in_order(replica, own, other, 1)] + gains, axis=1)
    gathered = lax.all_gather(row, "expert", tiled=True)
    gain_block = row.shape[1] // LANES - 1
    part = run_experts(owner, gathered, gathered, gain_block, 0, first, second, experts)
    summed = lax.psum_scatter(part, "expert", scatter_dimension=0, tiled=True)
    own, other = trade(replica, summed, 1)
    thinker_out = in_order(replica, own, other, 0)
    terms = jnp.dot(thinker_out, handoff, preferred_element_type=jnp.float32)
    own, other = trade(replica, terms.astype(jnp.bfloat16), 0)
    talker_row = (own.astype(jnp.float32) + other.astype(jnp.float32)).astype(jnp.bfloat16)
    talker_gathered = lax.all_gather(talker_row, "expert", tiled=True)
    talker_part = run_experts(
        owner, talker_gathered, gathered, gain_block, 2 * experts, talker_first, talker_second, experts
    )
    talker_sum = lax.psum_scatter(talker_part, "expert", scatter_dimension=0, tiled=True)
    own, other = trade(replica, talker_sum, 1)
    return (thinker_out, in_order(replica, own, other, 0))


def on_device(*arrays):
    token_count, top_count = arrays[1].shape
    local_experts = arrays[3].shape[0]
    experts = local_experts * lax.axis_size("expert")
    dense = (
        token_count * top_count * 2 // experts >= token_count
        and 4 * experts <= LANES
        and lax.axis_size("replica") == 2
        and lax.axis_size("groups") == local_experts
    )
    return (dense_on_device if dense else routed_on_device)(*arrays)


def solution(mesh):
    return jax.shard_map(
        on_device,
        mesh=mesh,
        in_specs=(
            P(("groups", "expert"), "replica"),
            P(("groups", "expert"), None),
            P(("groups", "expert"), None),
            P("expert", "replica", None),
            P("expert", None, "replica"),
            P("replica", None),
            P(("groups", "expert")),
            P(("groups", "expert"), None),
            P(("groups", "expert"), None),
            P("expert", "replica", None),
            P("expert", None, "replica"),
        ),
        out_specs=(P(("groups", "expert"), "replica"), P(("groups", "expert"), "replica")),
        check_vma=False,
    )
```

```python
import functools

import jax
import jax.numpy as jnp
from jax import lax
from jax.experimental import pallas as pl
from jax.experimental.pallas import tpu as pltpu
from jax.sharding import PartitionSpec as P

LANES = 128
SWAP = [(0, 1), (1, 0)]


def place_rows(tok_rows, flat_ids, live_rows, experts, capacity):
    onehot = (flat_ids[:, None] == lax.iota(jnp.int32, experts)[None, :]).astype(
        jnp.int32
    ) * live_rows[:, None]
    before = jnp.cumsum(onehot, axis=0) - onehot
    slot_rank = jnp.sum(before * onehot, axis=1)
    slot_index = jnp.where(live_rows > 0, flat_ids * capacity + slot_rank, experts * capacity)
    buffer = (
        jnp.zeros((experts * capacity, tok_rows.shape[1]), tok_rows.dtype)
        .at[slot_index]
        .set(tok_rows, mode="drop")
    )
    return (buffer, slot_index)


def activate(gate_sum, up_sum):
    return (jax.nn.silu(gate_sum) * up_sum).astype(jnp.bfloat16)


def down_rows(second_weights, piece):
    return jnp.einsum("lrf,lfd->lrd", piece, second_weights, preferred_element_type=jnp.float32)


def routed_on_device(
    hidden_in,
    routes,
    route_gain,
    w_in,
    w_out,
    handoff,
    speaking,
    talker_routes,
    talker_gain,
    talker_w_in,
    talker_w_out,
):
    owners = lax.axis_size("expert")
    token_count, top_count = routes.shape
    local_experts = w_in.shape[0]
    experts = local_experts * owners
    capacity = max(2, token_count * top_count * 2 // experts)
    talker_capacity = max(2, capacity * 3 // 4)
    flat_ids = routes.reshape(-1)
    all_rows = jnp.ones_like(flat_ids)
    spread = jnp.repeat(hidden_in, top_count, axis=0)
    buffer, slot_index = place_rows(spread, flat_ids, all_rows, experts, capacity)
    arrived = lax.all_to_all(
        buffer.reshape(owners, local_experts, capacity, -1),
        "expert",
        split_axis=0,
        concat_axis=2,
        tiled=True,
    )
    partial_value = jnp.einsum("lrd,ldf->lrf", arrived[0], w_in, preferred_element_type=jnp.float32)
    hidden_width = w_in.shape[2] // 2
    share_sum = lax.psum_scatter(
        partial_value.astype(jnp.bfloat16), "replica", scatter_dimension=1, tiled=True
    ).astype(jnp.float32)
    hidden = activate(share_sum[:, :, :hidden_width], share_sum[:, :, hidden_width:])
    expert_out = down_rows(w_out, lax.all_gather(hidden, "replica", axis=1, tiled=True))
    returned = lax.all_to_all(
        expert_out.astype(jnp.bfloat16)[None], "expert", split_axis=2, concat_axis=0, tiled=True
    )
    returned = returned.reshape(experts * capacity, -1)
    picked = returned[slot_index].astype(jnp.float32).reshape(token_count, top_count, -1)
    thinker_out = jnp.sum(picked * route_gain[:, :, None], axis=1).astype(jnp.bfloat16)
    handoff_terms = jnp.dot(thinker_out, handoff, preferred_element_type=jnp.float32)
    talker_in = lax.psum_scatter(
        handoff_terms.astype(jnp.bfloat16), "replica", scatter_dimension=1, tiled=True
    )
    talker_ids = talker_routes.reshape(-1)
    speak_rows = jnp.repeat(speaking, top_count)
    talker_spread = jnp.repeat(talker_in, top_count, axis=0)
    talker_buffer, talker_slots = place_rows(
        talker_spread, talker_ids, speak_rows, experts, talker_capacity
    )
    talker_arrived = lax.all_to_all(
        talker_buffer.reshape(owners, local_experts, talker_capacity, -1),
        "expert",
        split_axis=0,
        concat_axis=2,
        tiled=True,
    )
    talker_partial = jnp.einsum(
        "lrd,ldf->lrf", talker_arrived[0], talker_w_in, preferred_element_type=jnp.float32
    )
    talker_hidden_width = talker_w_in.shape[2] // 2
    talker_share = lax.psum_scatter(
        talker_partial.astype(jnp.bfloat16), "replica", scatter_dimension=1, tiled=True
    ).astype(jnp.float32)
    talker_hidden = activate(
        talker_share[:, :, :talker_hidden_width], talker_share[:, :, talker_hidden_width:]
    )
    talker_expert_out = down_rows(
        talker_w_out, lax.all_gather(talker_hidden, "replica", axis=1, tiled=True)
    )
    talker_returned = lax.all_to_all(
        talker_expert_out.astype(jnp.bfloat16)[None],
        "expert",
        split_axis=2,
        concat_axis=0,
        tiled=True,
    )
    talker_returned = talker_returned.reshape(experts * talker_capacity, -1)
    safe_slots = jnp.minimum(talker_slots, experts * talker_capacity - 1)
    talker_picked = (
        talker_returned[safe_slots].astype(jnp.float32).reshape(token_count, top_count, -1)
    )
    talker_weights = talker_gain * speak_rows.reshape(token_count, top_count).astype(jnp.float32)
    talker_out = jnp.sum(talker_picked * talker_weights[:, :, None], axis=1).astype(jnp.bfloat16)
    return (thinker_out, talker_out)


def split_gain(ids, gain, experts):
    hits = ids[:, :, None] == lax.iota(jnp.int32, experts)[None, None, :]
    dense = jnp.sum(jnp.where(hits, gain[:, :, None], 0.0), axis=1)
    high = lax.reduce_precision(dense, 8, 7)
    return [high.astype(jnp.bfloat16), (dense - high).astype(jnp.bfloat16)]


def load(pairs, sems):
    copies = [
        pltpu.make_async_copy(source, destination, sems.at[index])
        for index, (source, destination) in enumerate(pairs)
    ]
    for copy in copies:
        copy.start()
    return copies


def chunk_pairs(chunks, place, first_row=0):
    pairs, row = [], first_row
    for chunk in chunks:
        pairs.append((chunk, place.at[pl.ds(row, chunk.shape[0])]))
        row += chunk.shape[0]
    return pairs


def hidden_kernel(blocks, gain_blocks, near, far, first_lane, experts, where_ref, *refs):
    refs = list(refs)
    take = lambda count: [refs.pop(0) for _ in range(count)]
    row_refs, gain_refs = take(blocks), take(gain_blocks)
    (own_ref,) = take(1)
    near_refs, far_refs = take(near), take(far)
    (out_ref, rows, gains, weights, sems) = refs
    width = own_ref.shape[1]
    half_hidden = own_ref.shape[2] // 2
    group = where_ref[1]
    lane_refs = [ref.at[:, pl.ds(ref.shape[1] - LANES, LANES)] for ref in gain_refs or row_refs]
    row_refs = [ref.at[:, pl.ds(0, 2 * width)] for ref in row_refs]
    row_copies = load(
        chunk_pairs(row_refs, rows) + chunk_pairs(lane_refs, gains), sems.at[0]
    )
    weight_copies = [
        load(
            [(own_ref.at[(group + order) % 2], weights.at[order, pl.ds(0, width)])]
            + chunk_pairs(parts, weights.at[order], width),
            sems.at[1 + order],
        )
        for order, parts in enumerate((near_refs, far_refs))
    ]
    for copy in row_copies:
        copy.wait()
    lanes = gains[...].astype(jnp.float32)
    place = lax.broadcasted_iota(jnp.int32, lanes.shape, 1) - first_lane
    for order in range(2):
        for copy in weight_copies[order]:
            copy.wait()
        offset = place - (where_ref[0] * 2 + (group + order) % 2)
        gain = jnp.sum(
            jnp.where((offset == 0) | (offset == experts), lanes, 0.0), axis=1, keepdims=True
        )
        summed = jnp.dot(
            rows[...], weights[order], preferred_element_type=jnp.float32
        )
        hidden = jax.nn.silu(summed[:, :half_hidden]) * summed[:, half_hidden:] * gain
        out_ref[:, order * half_hidden : (order + 1) * half_hidden] = hidden.astype(jnp.bfloat16)


def run_hidden(where, row_blocks, gain_blocks, own, near, far, first_lane, experts):
    blocks = len(row_blocks)
    count = blocks * row_blocks[0].shape[0]
    _, width, columns = own.shape
    inputs = [*row_blocks, *gain_blocks, own, *near, *far]
    kernel = functools.partial(
        hidden_kernel, blocks, len(gain_blocks), len(near), len(far), first_lane, experts
    )
    return pl.pallas_call(
        kernel,
        out_shape=jax.ShapeDtypeStruct((count, columns), jnp.bfloat16),
        in_specs=[pl.BlockSpec(memory_space=pltpu.SMEM)]
        + [pl.BlockSpec(memory_space=pl.ANY)] * len(inputs),
        out_specs=pl.BlockSpec(memory_space=pltpu.VMEM),
        scratch_shapes=[
            pltpu.VMEM((count, 2 * width), jnp.bfloat16),
            pltpu.VMEM((count, LANES), jnp.bfloat16),
            pltpu.VMEM((2, 2 * width, columns), jnp.bfloat16),
            pltpu.SemaphoreType.DMA((3, 2 * blocks + 1 + len(near))),
        ],
        compiler_params=pltpu.CompilerParams(vmem_limit_bytes=48 * 1024 * 1024),
        cost_estimate=pl.CostEstimate(
            flops=8 * count * width * columns,
            bytes_accessed=2 * (2 * count * width + 4 * width * columns + count * columns),
            transcendentals=count * columns,
        ),
    )(where, *inputs)


def down_kernel(near, far, where_ref, hidden_ref, *refs):
    refs = list(refs)
    first_refs = [refs.pop(0) for _ in range(near)]
    second_refs = [refs.pop(0) for _ in range(far)]
    mine_ref, away_ref, weights, sems = refs
    depth = weights.shape[0] // 2
    if near == 1 and far == 0:
        (local_ref,) = first_refs
        first_refs = [local_ref.at[where_ref[1]]]
        second_refs = [local_ref.at[1 - where_ref[1]]]
    copies = load(
        chunk_pairs(first_refs, weights) + chunk_pairs(second_refs, weights, depth), sems
    )
    for copy in copies:
        copy.wait()
    rows = mine_ref.shape[0]
    for half, out_ref in enumerate((mine_ref, away_ref)):
        out_ref[...] = jnp.dot(
            hidden_ref[half * rows : (half + 1) * rows, :],
            weights[...],
            preferred_element_type=jnp.float32,
        ).astype(jnp.bfloat16)


def run_down(where, hidden, near, far):
    count, depth = hidden.shape
    columns = near[0].shape[-1]
    inputs = [*near, *far]
    shape = jax.ShapeDtypeStruct((count // 2, columns), jnp.bfloat16)
    return pl.pallas_call(
        functools.partial(down_kernel, len(near), len(far)),
        out_shape=(shape, shape),
        in_specs=[
            pl.BlockSpec(memory_space=pltpu.SMEM),
            pl.BlockSpec(memory_space=pltpu.VMEM),
        ]
        + [pl.BlockSpec(memory_space=pl.ANY)] * len(inputs),
        out_specs=(pl.BlockSpec(memory_space=pltpu.VMEM),) * 2,
        scratch_shapes=[
            pltpu.VMEM((depth, columns), jnp.bfloat16),
            pltpu.SemaphoreType.DMA((max(2, len(inputs)),)),
        ],
        compiler_params=pltpu.CompilerParams(vmem_limit_bytes=48 * 1024 * 1024),
        cost_estimate=pl.CostEstimate(
            flops=2 * count * depth * columns,
            bytes_accessed=2 * (count * depth + depth * columns + count * columns),
            transcendentals=0,
        ),
    )(where, hidden, *inputs)


def over_replica(array):
    return lax.ppermute(array, "replica", SWAP)


def over_groups(array):
    return lax.ppermute(array, "groups", SWAP)


def over_expert(array, distance):
    return lax.ppermute(
        array, "expert", [(at, at ^ distance) for at in range(lax.axis_size("expert"))]
    )


def fetch_halves(named, chunk_rows):
    group = lax.axis_index("groups")
    arrived, result = [], []
    for weights in named:
        near, far = [], []
        for row in range(0, weights.shape[1], chunk_rows(weights)):
            piece = lax.dynamic_slice(
                weights, (group, row, 0), (1, chunk_rows(weights), weights.shape[2])
            )[0]
            if len(arrived) > 1:
                piece, _ = lax.optimization_barrier((piece, arrived[-2]))
            near.append(over_replica(piece))
            arrived.append(near[-1])
            far.append(over_groups(near[-1]))
        result.append((near, far))
    return result


def gather_rows(row):
    owners = lax.axis_size("expert")
    same = [row] + [over_expert(row, distance) for distance in range(2, owners, 2)]
    return same + [over_expert(block, 1) for block in same]


def scatter_sums(mine, away):
    owners = lax.axis_size("expert")
    rows = mine.shape[0] // (owners // 2)
    other = over_expert(away, 1)
    total = None
    for index in range(owners // 2 - 1, -1, -1):
        part = slice(index * rows, (index + 1) * rows)
        chip = mine[part].astype(jnp.float32) + other[part].astype(jnp.float32)
        if index:
            chip = over_expert(chip.astype(jnp.bfloat16), 2 * index).astype(jnp.float32)
        total = chip if total is None else total + chip
    return total.astype(jnp.bfloat16)


def in_order(replica, own, other, axis):
    return jnp.concatenate(
        [jnp.where(replica == 0, own, other), jnp.where(replica == 0, other, own)], axis=axis
    )


def dense_on_device(
    hidden_in,
    routes,
    route_gain,
    w_in,
    w_out,
    handoff,
    speaking,
    talker_routes,
    talker_gain,
    talker_w_in,
    talker_w_out,
):
    replica = lax.axis_index("replica")
    where = jnp.stack([lax.axis_index("expert"), lax.axis_index("groups")]).astype(jnp.int32)
    experts = w_in.shape[0] * lax.axis_size("expert")
    rows = routes.shape[0] // 2

    def my_rows(array):
        return lax.dynamic_slice_in_dim(array, replica * rows, rows, 0)

    other = over_replica(lax.dynamic_slice_in_dim(hidden_in, (1 - replica) * rows, rows, 0))
    chunk_rows = lambda weights: min(weights.shape[1], 384 * 512 // weights.shape[2])
    fetched = fetch_halves((w_in, w_out, talker_w_in, talker_w_out), chunk_rows)
    live = my_rows(speaking).astype(jnp.float32)[:, None]
    gains = split_gain(my_rows(routes), my_rows(route_gain), experts) + split_gain(
        my_rows(talker_routes), my_rows(talker_gain) * live, experts
    )
    gains.append(jnp.zeros((rows, LANES - 4 * experts), jnp.bfloat16))
    blocks = gather_rows(jnp.concatenate([my_rows(hidden_in), other] + gains, axis=1))
    hidden = run_hidden(where, blocks, [], w_in, *fetched[0], 0, experts)
    own = scatter_sums(*run_down(where, hidden, [w_out], []))
    give = scatter_sums(*run_down(where, hidden, *fetched[1]))
    got = over_replica(give)
    thinker_out = in_order(replica, own, got, 0)

    def handed(array):
        return jnp.dot(array, handoff, preferred_element_type=jnp.float32)

    term = over_replica(handed(got).astype(jnp.bfloat16))
    talker_row = (handed(own) + term.astype(jnp.float32)).astype(jnp.bfloat16)
    parts = jnp.split(talker_row, 2, axis=1)
    talker_row = in_order(replica, parts[0], parts[1], 1)
    talker_blocks = gather_rows(talker_row)
    hidden = run_hidden(
        where, talker_blocks, blocks, talker_w_in, *fetched[2], 2 * experts, experts
    )
    own = scatter_sums(*run_down(where, hidden, [talker_w_out], []))
    give = scatter_sums(*run_down(where, hidden, *fetched[3]))
    return (thinker_out, in_order(replica, own, over_replica(give), 0))


def on_device(*arrays):
    token_count, top_count = arrays[1].shape
    local_experts = arrays[3].shape[0]
    experts = local_experts * lax.axis_size("expert")
    dense = (
        token_count * top_count * 2 // experts >= token_count
        and 4 * experts <= LANES
        and lax.axis_size("replica") == lax.axis_size("groups") == local_experts == 2
        and lax.axis_size("expert") in (2, 4, 8, 16)
    )
    return (dense_on_device if dense else routed_on_device)(*arrays)


def solution(mesh):
    return jax.shard_map(
        on_device,
        mesh=mesh,
        in_specs=(
            P(("groups", "expert"), "replica"),
            P(("groups", "expert"), None),
            P(("groups", "expert"), None),
            P("expert", "replica", None),
            P("expert", None, "replica"),
            P("replica", None),
            P(("groups", "expert")),
            P(("groups", "expert"), None),
            P(("groups", "expert"), None),
            P("expert", "replica", None),
            P("expert", None, "replica"),
        ),
        out_specs=(P(("groups", "expert"), "replica"), P(("groups", "expert"), "replica")),
        check_vma=False,
    )
```

```python
import functools

import jax
import jax.numpy as jnp
from jax import lax
from jax.experimental import pallas as pl
from jax.experimental.pallas import tpu as pltpu
from jax.sharding import PartitionSpec as P

LANES = 128
SWAP = [(0, 1), (1, 0)]


def place_rows(tok_rows, flat_ids, live_rows, experts, capacity):
    onehot = (flat_ids[:, None] == lax.iota(jnp.int32, experts)[None, :]).astype(
        jnp.int32
    ) * live_rows[:, None]
    before = jnp.cumsum(onehot, axis=0) - onehot
    slot_rank = jnp.sum(before * onehot, axis=1)
    slot_index = jnp.where(live_rows > 0, flat_ids * capacity + slot_rank, experts * capacity)
    buffer = (
        jnp.zeros((experts * capacity, tok_rows.shape[1]), tok_rows.dtype)
        .at[slot_index]
        .set(tok_rows, mode="drop")
    )
    return (buffer, slot_index)


def activate(gate_sum, up_sum):
    return (jax.nn.silu(gate_sum) * up_sum).astype(jnp.bfloat16)


def down_rows(second_weights, piece):
    return jnp.einsum("lrf,lfd->lrd", piece, second_weights, preferred_element_type=jnp.float32)


def routed_on_device(
    hidden_in,
    routes,
    route_gain,
    w_in,
    w_out,
    handoff,
    speaking,
    talker_routes,
    talker_gain,
    talker_w_in,
    talker_w_out,
):
    owners = lax.axis_size("expert")
    token_count, top_count = routes.shape
    local_experts = w_in.shape[0]
    experts = local_experts * owners
    capacity = max(2, token_count * top_count * 2 // experts)
    talker_capacity = max(2, capacity * 3 // 4)
    flat_ids = routes.reshape(-1)
    all_rows = jnp.ones_like(flat_ids)
    spread = jnp.repeat(hidden_in, top_count, axis=0)
    buffer, slot_index = place_rows(spread, flat_ids, all_rows, experts, capacity)
    arrived = lax.all_to_all(
        buffer.reshape(owners, local_experts, capacity, -1),
        "expert",
        split_axis=0,
        concat_axis=2,
        tiled=True,
    )
    partial_value = jnp.einsum("lrd,ldf->lrf", arrived[0], w_in, preferred_element_type=jnp.float32)
    hidden_width = w_in.shape[2] // 2
    share_sum = lax.psum_scatter(
        partial_value.astype(jnp.bfloat16), "replica", scatter_dimension=1, tiled=True
    ).astype(jnp.float32)
    hidden = activate(share_sum[:, :, :hidden_width], share_sum[:, :, hidden_width:])
    expert_out = down_rows(w_out, lax.all_gather(hidden, "replica", axis=1, tiled=True))
    returned = lax.all_to_all(
        expert_out.astype(jnp.bfloat16)[None], "expert", split_axis=2, concat_axis=0, tiled=True
    )
    returned = returned.reshape(experts * capacity, -1)
    picked = returned[slot_index].astype(jnp.float32).reshape(token_count, top_count, -1)
    thinker_out = jnp.sum(picked * route_gain[:, :, None], axis=1).astype(jnp.bfloat16)
    handoff_terms = jnp.dot(thinker_out, handoff, preferred_element_type=jnp.float32)
    talker_in = lax.psum_scatter(
        handoff_terms.astype(jnp.bfloat16), "replica", scatter_dimension=1, tiled=True
    )
    talker_ids = talker_routes.reshape(-1)
    speak_rows = jnp.repeat(speaking, top_count)
    talker_spread = jnp.repeat(talker_in, top_count, axis=0)
    talker_buffer, talker_slots = place_rows(
        talker_spread, talker_ids, speak_rows, experts, talker_capacity
    )
    talker_arrived = lax.all_to_all(
        talker_buffer.reshape(owners, local_experts, talker_capacity, -1),
        "expert",
        split_axis=0,
        concat_axis=2,
        tiled=True,
    )
    talker_partial = jnp.einsum(
        "lrd,ldf->lrf", talker_arrived[0], talker_w_in, preferred_element_type=jnp.float32
    )
    talker_hidden_width = talker_w_in.shape[2] // 2
    talker_share = lax.psum_scatter(
        talker_partial.astype(jnp.bfloat16), "replica", scatter_dimension=1, tiled=True
    ).astype(jnp.float32)
    talker_hidden = activate(
        talker_share[:, :, :talker_hidden_width], talker_share[:, :, talker_hidden_width:]
    )
    talker_expert_out = down_rows(
        talker_w_out, lax.all_gather(talker_hidden, "replica", axis=1, tiled=True)
    )
    talker_returned = lax.all_to_all(
        talker_expert_out.astype(jnp.bfloat16)[None],
        "expert",
        split_axis=2,
        concat_axis=0,
        tiled=True,
    )
    talker_returned = talker_returned.reshape(experts * talker_capacity, -1)
    safe_slots = jnp.minimum(talker_slots, experts * talker_capacity - 1)
    talker_picked = (
        talker_returned[safe_slots].astype(jnp.float32).reshape(token_count, top_count, -1)
    )
    talker_weights = talker_gain * speak_rows.reshape(token_count, top_count).astype(jnp.float32)
    talker_out = jnp.sum(talker_picked * talker_weights[:, :, None], axis=1).astype(jnp.bfloat16)
    return (thinker_out, talker_out)


def row_kernel(experts, where_ref, hidden_ref, other_ref, *refs):
    routes_ref, gain_ref, live_ref, talker_routes_ref, talker_gain_ref = refs[:5]
    out_ref, lanes = refs[-2:]
    rows, width = other_ref.shape
    first = pl.multiple_of(where_ref[2] * rows, rows)
    out_ref[:, :width] = hidden_ref[pl.ds(first, rows), :]
    out_ref[:, width : 2 * width] = other_ref[...]
    stack = []
    live = live_ref[...].astype(jnp.float32)
    for ids, gains in ((routes_ref, gain_ref[...]), (talker_routes_ref, talker_gain_ref[...] * live)):
        expert = lax.broadcasted_iota(jnp.int32, (experts, ids.shape[1]), 0)
        dense = jnp.zeros(expert.shape, jnp.float32)
        for choice in range(ids.shape[0]):
            dense += jnp.where(
                ids[choice : choice + 1, :] == expert, gains[choice : choice + 1, :], 0.0
            )
        high = dense.astype(jnp.bfloat16).astype(jnp.float32)
        stack += [high, dense - high]
    stack.append(jnp.zeros((LANES - 4 * experts, live.shape[1]), jnp.float32))
    lanes[...] = jnp.concatenate(stack, axis=0).T
    out_ref[:, 2 * width :] = lanes[pl.ds(first, rows), :].astype(jnp.bfloat16)


def build_row(before, where, hidden_in, other, experts, routes, gain, live, talker_routes, talker_gain):
    count = hidden_in.shape[0]
    rows, width = other.shape
    inputs = [hidden_in, other, routes.T, gain.T, live[None], talker_routes.T, talker_gain.T]
    return pl.pallas_call(
        functools.partial(row_kernel, experts),
        out_shape=jax.ShapeDtypeStruct((rows, 2 * width + LANES), jnp.bfloat16),
        in_specs=[pl.BlockSpec(memory_space=pltpu.SMEM)]
        + [pl.BlockSpec(memory_space=pltpu.VMEM)] * len(inputs)
        + [pl.BlockSpec(memory_space=pl.ANY)] * len(before),
        out_specs=pl.BlockSpec(memory_space=pltpu.VMEM),
        scratch_shapes=[pltpu.VMEM((count, LANES), jnp.float32)],
        compiler_params=pltpu.CompilerParams(vmem_limit_bytes=4 * 1024 * 1024),
        cost_estimate=pl.CostEstimate(
            flops=64 * count * experts, bytes_accessed=8 * rows * width, transcendentals=0
        ),
    )(where, *inputs, *before)


def load(pairs, sems):
    copies = [
        pltpu.make_async_copy(source, destination, sems.at[index])
        for index, (source, destination) in enumerate(pairs)
    ]
    for copy in copies:
        copy.start()
    return copies


def chunk_pairs(chunks, place, first_row=0):
    pairs, row = [], first_row
    for chunk in chunks:
        pairs.append((chunk, place.at[pl.ds(row, chunk.shape[0])]))
        row += chunk.shape[0]
    return pairs


def hidden_kernel(owners, chunks, orders, first_lane, experts, where_ref, *refs):
    refs = list(refs)
    take = lambda count: [refs.pop(0) for _ in range(count)]
    rows_ref, gains_ref, own_ref = take(3)
    chunk_refs = [take(count) for count in chunks]
    (out_ref, rows, gains, weights, sems) = refs[-5:]
    width = own_ref.shape[1]
    half_hidden = own_ref.shape[2] // 2
    size = rows.shape[0] // owners
    distances = [*range(0, owners, 2), *range(1, owners, 2)]

    def blocks(ref, first_column, columns):
        for distance in distances:
            start = pl.multiple_of((where_ref[0] ^ distance) * size, size)
            yield ref.at[pl.ds(start, size), pl.ds(first_column, columns)]

    row_copies = load(
        chunk_pairs(blocks(rows_ref, 0, 2 * width), rows)
        + chunk_pairs(blocks(gains_ref, gains_ref.shape[1] - LANES, LANES), gains),
        sems.at[0],
    )
    weight_copies = []
    for place, order in enumerate(orders):
        own = (own_ref.at[(where_ref[1] + order) % 2], weights.at[place, pl.ds(0, width)])
        others = chunk_pairs(chunk_refs[place], weights.at[place], width)
        weight_copies.append(load([own] + others, sems.at[1 + place]))
    for copy in row_copies:
        copy.wait()
    lanes = gains[...].astype(jnp.float32)
    lane = lax.broadcasted_iota(jnp.int32, lanes.shape, 1) - first_lane
    for place, order in enumerate(orders):
        for copy in weight_copies[place]:
            copy.wait()
        offset = lane - (where_ref[0] * 2 + (where_ref[1] + order) % 2)
        gain = jnp.sum(
            jnp.where((offset == 0) | (offset == experts), lanes, 0.0), axis=1, keepdims=True
        )
        summed = jnp.dot(rows[...], weights[place], preferred_element_type=jnp.float32)
        hidden = jax.nn.silu(summed[:, :half_hidden]) * summed[:, half_hidden:] * gain
        out_ref[:, place * half_hidden : (place + 1) * half_hidden] = hidden.astype(jnp.bfloat16)


def run_hidden(before, where, rows, gains, own, chunks, orders, first_lane, experts):
    count = rows.shape[0]
    _, width, columns = own.shape
    places = len(orders)
    owners = experts // own.shape[0]
    inputs = [rows, gains, own] + [part for parts in chunks for part in parts] + before
    kernel = functools.partial(
        hidden_kernel, owners, [len(parts) for parts in chunks], orders, first_lane, experts
    )
    return pl.pallas_call(
        kernel,
        out_shape=jax.ShapeDtypeStruct((count, places * columns // 2), jnp.bfloat16),
        in_specs=[pl.BlockSpec(memory_space=pltpu.SMEM)]
        + [pl.BlockSpec(memory_space=pl.ANY)] * len(inputs),
        out_specs=pl.BlockSpec(memory_space=pltpu.VMEM),
        scratch_shapes=[
            pltpu.VMEM((count, 2 * width), jnp.bfloat16),
            pltpu.VMEM((count, LANES), jnp.bfloat16),
            pltpu.VMEM((places, 2 * width, columns), jnp.bfloat16),
            pltpu.SemaphoreType.DMA((1 + places, max([2 * owners] + [1 + len(c) for c in chunks]))),
        ],
        compiler_params=pltpu.CompilerParams(vmem_limit_bytes=16 * 1024 * 1024),
        cost_estimate=pl.CostEstimate(
            flops=4 * places * count * width * columns,
            bytes_accessed=4 * width * (count + places * columns),
            transcendentals=places * count * columns // 2,
        ),
    )(where, *inputs)


def down_kernel(pieces, near, far, where_ref, *refs):
    refs = list(refs)
    take = lambda count: [refs.pop(0) for _ in range(count)]
    hidden_refs, first_refs, second_refs = take(pieces), take(near), take(far)
    mine_ref, away_ref, weights, sems = refs
    depth = weights.shape[0] // 2
    if far == 0:
        (local_ref,) = first_refs
        first_refs = [local_ref.at[where_ref[1]]]
        second_refs = [local_ref.at[1 - where_ref[1]]]
    copies = load(
        chunk_pairs(first_refs, weights) + chunk_pairs(second_refs, weights, depth), sems
    )
    for copy in copies:
        copy.wait()
    rows = mine_ref.shape[0]
    for half, out_ref in enumerate((mine_ref, away_ref)):
        total, row = None, 0
        for ref in hidden_refs:
            term = jnp.dot(
                ref[half * rows : (half + 1) * rows, :],
                weights[row : row + ref.shape[1], :],
                preferred_element_type=jnp.float32,
            )
            total = term if total is None else total + term
            row += ref.shape[1]
        out_ref[...] = total.astype(jnp.bfloat16)


def run_down(where, hidden, near, far):
    count, depth = hidden[0].shape[0], sum(part.shape[1] for part in hidden)
    columns = near[0].shape[-1]
    inputs = [*near, *far]
    shape = jax.ShapeDtypeStruct((count // 2, columns), jnp.bfloat16)
    return pl.pallas_call(
        functools.partial(down_kernel, len(hidden), len(near), len(far)),
        out_shape=(shape, shape),
        in_specs=[pl.BlockSpec(memory_space=pltpu.SMEM)]
        + [pl.BlockSpec(memory_space=pltpu.VMEM)] * len(hidden)
        + [pl.BlockSpec(memory_space=pl.ANY)] * len(inputs),
        out_specs=(pl.BlockSpec(memory_space=pltpu.VMEM),) * 2,
        scratch_shapes=[
            pltpu.VMEM((depth, columns), jnp.bfloat16),
            pltpu.SemaphoreType.DMA((max(2, len(inputs)),)),
        ],
        compiler_params=pltpu.CompilerParams(vmem_limit_bytes=16 * 1024 * 1024),
        cost_estimate=pl.CostEstimate(
            flops=2 * count * depth * columns,
            bytes_accessed=2 * (count * depth + depth * columns + count * columns),
            transcendentals=0,
        ),
    )(where, *hidden, *inputs)


def over_replica(array):
    return lax.ppermute(array, "replica", SWAP)


def over_groups(array):
    return lax.ppermute(array, "groups", SWAP)


def over_expert(array, distance):
    return lax.ppermute(
        array, "expert", [(at, at ^ distance) for at in range(lax.axis_size("expert"))]
    )


def after(array, *others):
    return lax.optimization_barrier((array, *others))[0] if others else array


def send(weights, group, first_row, rows, *before):
    piece = lax.dynamic_slice(weights, (group, first_row, 0), (1, rows, weights.shape[2]))[0]
    return over_replica(after(piece, *before))


def scatter_sums(mine, away, *before):
    owners = lax.axis_size("expert")
    rows = mine.shape[0] // (owners // 2)
    other = over_expert(away, 1)
    total = None
    for index in range(owners // 2 - 1, -1, -1):
        part = slice(index * rows, (index + 1) * rows)
        chip = mine[part].astype(jnp.float32) + other[part].astype(jnp.float32)
        if index:
            chip = after(chip.astype(jnp.bfloat16), *before)
            chip = over_expert(chip, 2 * index).astype(jnp.float32)
        total = chip if total is None else total + chip
    return total.astype(jnp.bfloat16)


def in_order(replica, own, other, axis):
    return jnp.concatenate(
        [jnp.where(replica == 0, own, other), jnp.where(replica == 0, other, own)], axis=axis
    )


def dense_on_device(
    hidden_in,
    routes,
    route_gain,
    w_in,
    w_out,
    handoff,
    speaking,
    talker_routes,
    talker_gain,
    talker_w_in,
    talker_w_out,
):
    replica, group = lax.axis_index("replica"), lax.axis_index("groups")
    where = jnp.stack([lax.axis_index("expert"), group, replica]).astype(jnp.int32)
    owners = lax.axis_size("expert")
    experts = w_in.shape[0] * owners
    rows = routes.shape[0] // 2

    give = lax.dynamic_slice_in_dim(hidden_in, (1 - replica) * rows, rows, 0)
    other = over_replica(give)
    chunk, out_chunk = w_in.shape[1] // 4, w_out.shape[1] // 2
    near_in = [send(w_in, group, 0, chunk, give), send(w_in, group, chunk, chunk, give)]
    row = build_row(
        [near_in[0]],
        where,
        hidden_in,
        other,
        experts,
        routes,
        route_gain,
        speaking,
        talker_routes,
        talker_gain,
    )
    gathered = lax.all_gather(row, "expert", tiled=True)
    far_in = [over_groups(near_in[0])]
    near_in.append(send(w_in, group, 2 * chunk, chunk, near_in[0]))
    far_in.append(over_groups(near_in[1]))
    near_in.append(send(w_in, group, 3 * chunk, chunk, near_in[1]))
    far_in.append(over_groups(near_in[2]))
    near_out = [send(w_out, group, 0, out_chunk, near_in[2], far_in[0])]
    far_in.append(over_groups(near_in[3]))
    near_out.append(send(w_out, group, out_chunk, out_chunk, near_in[3], far_in[1]))
    far_out = [over_groups(near_out[0])]
    before = [near_out[0], far_in[2]]
    near_hidden = run_hidden(before, where, gathered, gathered, w_in, [near_in], [0], 0, experts)
    near_talker_in = send(talker_w_in, group, 0, talker_w_in.shape[1], near_out[0], far_in[2])
    before = [near_hidden]
    far_hidden = run_hidden(before, where, gathered, gathered, w_in, [far_in], [1], 0, experts)
    far_out.append(over_groups(after(near_out[1], far_hidden)))
    hidden = [near_hidden, far_hidden]
    own = scatter_sums(*run_down(where, hidden, [w_out], []))
    give = run_down(where, hidden, near_out, far_out)
    far_talker_in = over_groups(near_talker_in)
    near_talker_out = send(talker_w_out, group, 0, talker_w_out.shape[1], near_talker_in)
    give = after(scatter_sums(*give, near_talker_in), near_talker_out)
    far_talker_out = over_groups(near_talker_out)
    got = over_replica(give)
    thinker_out = in_order(replica, own, got, 0)

    def handed(array):
        return jnp.dot(array, handoff, preferred_element_type=jnp.float32)

    term = over_replica(handed(got).astype(jnp.bfloat16))
    talker_row = (handed(own) + term.astype(jnp.float32)).astype(jnp.bfloat16)
    parts = jnp.split(talker_row, 2, axis=1)
    talker_row = in_order(replica, parts[0], parts[1], 1)
    hidden = run_hidden(
        [],
        where,
        lax.all_gather(talker_row, "expert", tiled=True),
        gathered,
        talker_w_in,
        [[near_talker_in], [far_talker_in]],
        [0, 1],
        2 * experts,
        experts,
    )
    give = run_down(where, [hidden], [near_talker_out], [far_talker_out])
    got = over_replica(scatter_sums(*give))
    own = scatter_sums(*run_down(where, [after(hidden, *give)], [talker_w_out], []))
    return (thinker_out, in_order(replica, own, got, 0))


def on_device(*arrays):
    token_count, top_count = arrays[1].shape
    local_experts = arrays[3].shape[0]
    experts = local_experts * lax.axis_size("expert")
    dense = (
        token_count * top_count * 2 // experts >= token_count
        and 4 * experts <= LANES
        and lax.axis_size("replica") == lax.axis_size("groups") == local_experts == 2
        and lax.axis_size("expert") in (2, 4, 8, 16)
    )
    return (dense_on_device if dense else routed_on_device)(*arrays)


def solution(mesh):
    return jax.shard_map(
        on_device,
        mesh=mesh,
        in_specs=(
            P(("groups", "expert"), "replica"),
            P(("groups", "expert"), None),
            P(("groups", "expert"), None),
            P("expert", "replica", None),
            P("expert", None, "replica"),
            P("replica", None),
            P(("groups", "expert")),
            P(("groups", "expert"), None),
            P(("groups", "expert"), None),
            P("expert", "replica", None),
            P("expert", None, "replica"),
        ),
        out_specs=(P(("groups", "expert"), "replica"), P(("groups", "expert"), "replica")),
        check_vma=False,
    )
```

```python
import functools

import jax
import jax.numpy as jnp
from jax import lax
from jax.experimental import pallas as pl
from jax.experimental.pallas import tpu as pltpu
from jax.sharding import PartitionSpec as P

LANES = 128
SWAP = [(0, 1), (1, 0)]


def place_rows(tok_rows, flat_ids, live_rows, experts, capacity):
    onehot = (flat_ids[:, None] == lax.iota(jnp.int32, experts)[None, :]).astype(
        jnp.int32
    ) * live_rows[:, None]
    before = jnp.cumsum(onehot, axis=0) - onehot
    slot_rank = jnp.sum(before * onehot, axis=1)
    slot_index = jnp.where(live_rows > 0, flat_ids * capacity + slot_rank, experts * capacity)
    buffer = (
        jnp.zeros((experts * capacity, tok_rows.shape[1]), tok_rows.dtype)
        .at[slot_index]
        .set(tok_rows, mode="drop")
    )
    return (buffer, slot_index)


def activate(gate_sum, up_sum):
    return (jax.nn.silu(gate_sum) * up_sum).astype(jnp.bfloat16)


def down_rows(second_weights, piece):
    return jnp.einsum("lrf,lfd->lrd", piece, second_weights, preferred_element_type=jnp.float32)


def routed_on_device(
    hidden_in,
    routes,
    route_gain,
    w_in,
    w_out,
    handoff,
    speaking,
    talker_routes,
    talker_gain,
    talker_w_in,
    talker_w_out,
):
    owners = lax.axis_size("expert")
    token_count, top_count = routes.shape
    local_experts = w_in.shape[0]
    experts = local_experts * owners
    capacity = max(2, token_count * top_count * 2 // experts)
    talker_capacity = max(2, capacity * 3 // 4)
    flat_ids = routes.reshape(-1)
    all_rows = jnp.ones_like(flat_ids)
    spread = jnp.repeat(hidden_in, top_count, axis=0)
    buffer, slot_index = place_rows(spread, flat_ids, all_rows, experts, capacity)
    arrived = lax.all_to_all(
        buffer.reshape(owners, local_experts, capacity, -1),
        "expert",
        split_axis=0,
        concat_axis=2,
        tiled=True,
    )
    partial_value = jnp.einsum("lrd,ldf->lrf", arrived[0], w_in, preferred_element_type=jnp.float32)
    hidden_width = w_in.shape[2] // 2
    share_sum = lax.psum_scatter(
        partial_value.astype(jnp.bfloat16), "replica", scatter_dimension=1, tiled=True
    ).astype(jnp.float32)
    hidden = activate(share_sum[:, :, :hidden_width], share_sum[:, :, hidden_width:])
    expert_out = down_rows(w_out, lax.all_gather(hidden, "replica", axis=1, tiled=True))
    returned = lax.all_to_all(
        expert_out.astype(jnp.bfloat16)[None], "expert", split_axis=2, concat_axis=0, tiled=True
    )
    returned = returned.reshape(experts * capacity, -1)
    picked = returned[slot_index].astype(jnp.float32).reshape(token_count, top_count, -1)
    thinker_out = jnp.sum(picked * route_gain[:, :, None], axis=1).astype(jnp.bfloat16)
    handoff_terms = jnp.dot(thinker_out, handoff, preferred_element_type=jnp.float32)
    talker_in = lax.psum_scatter(
        handoff_terms.astype(jnp.bfloat16), "replica", scatter_dimension=1, tiled=True
    )
    talker_ids = talker_routes.reshape(-1)
    speak_rows = jnp.repeat(speaking, top_count)
    talker_spread = jnp.repeat(talker_in, top_count, axis=0)
    talker_buffer, talker_slots = place_rows(
        talker_spread, talker_ids, speak_rows, experts, talker_capacity
    )
    talker_arrived = lax.all_to_all(
        talker_buffer.reshape(owners, local_experts, talker_capacity, -1),
        "expert",
        split_axis=0,
        concat_axis=2,
        tiled=True,
    )
    talker_partial = jnp.einsum(
        "lrd,ldf->lrf", talker_arrived[0], talker_w_in, preferred_element_type=jnp.float32
    )
    talker_hidden_width = talker_w_in.shape[2] // 2
    talker_share = lax.psum_scatter(
        talker_partial.astype(jnp.bfloat16), "replica", scatter_dimension=1, tiled=True
    ).astype(jnp.float32)
    talker_hidden = activate(
        talker_share[:, :, :talker_hidden_width], talker_share[:, :, talker_hidden_width:]
    )
    talker_expert_out = down_rows(
        talker_w_out, lax.all_gather(talker_hidden, "replica", axis=1, tiled=True)
    )
    talker_returned = lax.all_to_all(
        talker_expert_out.astype(jnp.bfloat16)[None],
        "expert",
        split_axis=2,
        concat_axis=0,
        tiled=True,
    )
    talker_returned = talker_returned.reshape(experts * talker_capacity, -1)
    safe_slots = jnp.minimum(talker_slots, experts * talker_capacity - 1)
    talker_picked = (
        talker_returned[safe_slots].astype(jnp.float32).reshape(token_count, top_count, -1)
    )
    talker_weights = talker_gain * speak_rows.reshape(token_count, top_count).astype(jnp.float32)
    talker_out = jnp.sum(talker_picked * talker_weights[:, :, None], axis=1).astype(jnp.bfloat16)
    return (thinker_out, talker_out)


def lanes_kernel(experts, where_ref, *refs):
    routes_ref, gain_ref, live_ref, talker_routes_ref, talker_gain_ref, out_ref, lanes = refs
    rows = out_ref.shape[0]
    stack = []
    live = live_ref[...].astype(jnp.float32)
    for ids, gains in ((routes_ref, gain_ref[...]), (talker_routes_ref, talker_gain_ref[...] * live)):
        expert = lax.broadcasted_iota(jnp.int32, (experts, ids.shape[1]), 0)
        dense = jnp.zeros(expert.shape, jnp.float32)
        for choice in range(ids.shape[0]):
            dense += jnp.where(
                ids[choice : choice + 1, :] == expert, gains[choice : choice + 1, :], 0.0
            )
        high = dense.astype(jnp.bfloat16).astype(jnp.float32)
        stack += [high, dense - high]
    stack.append(jnp.zeros((LANES - 4 * experts, live.shape[1]), jnp.float32))
    lanes[...] = jnp.concatenate(stack, axis=0).T
    first = pl.multiple_of(where_ref[2] * rows, rows)
    out_ref[...] = lanes[pl.ds(first, rows), :].astype(jnp.bfloat16)


def gain_lanes(where, experts, routes, gain, live, talker_routes, talker_gain):
    count = routes.shape[0]
    inputs = [routes.T, gain.T, live[None], talker_routes.T, talker_gain.T]
    return pl.pallas_call(
        functools.partial(lanes_kernel, experts),
        out_shape=jax.ShapeDtypeStruct((count // 2, LANES), jnp.bfloat16),
        in_specs=[pl.BlockSpec(memory_space=pltpu.SMEM)]
        + [pl.BlockSpec(memory_space=pltpu.VMEM)] * len(inputs),
        out_specs=pl.BlockSpec(memory_space=pltpu.VMEM),
        scratch_shapes=[pltpu.VMEM((count, LANES), jnp.float32)],
        compiler_params=pltpu.CompilerParams(vmem_limit_bytes=4 * 1024 * 1024),
        cost_estimate=pl.CostEstimate(
            flops=1 << 30, bytes_accessed=64 * count * LANES, transcendentals=0
        ),
    )(where, *inputs)


def row_kernel(where_ref, hidden_ref, other_ref, lanes_ref, out_ref):
    rows, width = other_ref.shape
    first = pl.multiple_of(where_ref[2] * rows, rows)
    out_ref[:, :width] = hidden_ref[pl.ds(first, rows), :]
    out_ref[:, width : 2 * width] = other_ref[...]
    out_ref[:, 2 * width :] = lanes_ref[...]


def build_row(where, hidden_in, other, lanes):
    rows, width = other.shape
    return pl.pallas_call(
        row_kernel,
        out_shape=jax.ShapeDtypeStruct((rows, 2 * width + LANES), jnp.bfloat16),
        in_specs=[pl.BlockSpec(memory_space=pltpu.SMEM)]
        + [pl.BlockSpec(memory_space=pltpu.VMEM)] * 3,
        out_specs=pl.BlockSpec(memory_space=pltpu.VMEM),
        compiler_params=pltpu.CompilerParams(vmem_limit_bytes=4 * 1024 * 1024),
        cost_estimate=pl.CostEstimate(flops=0, bytes_accessed=8 * rows * width, transcendentals=0),
    )(where, hidden_in, other, lanes)


def load(pairs, sems):
    copies = [
        pltpu.make_async_copy(source, destination, sems.at[index])
        for index, (source, destination) in enumerate(pairs)
    ]
    for copy in copies:
        copy.start()
    return copies


def chunk_pairs(chunks, place, first_row=0):
    pairs, row = [], first_row
    for chunk in chunks:
        pairs.append((chunk, place.at[pl.ds(row, chunk.shape[0])]))
        row += chunk.shape[0]
    return pairs


def hidden_kernel(blocks, gain_blocks, chunks, first_lane, experts, where_ref, *refs):
    refs = list(refs)
    take = lambda count: [refs.pop(0) for _ in range(count)]
    row_refs, gain_refs = take(blocks), take(gain_blocks)
    (own_ref,) = take(1)
    chunk_refs = [take(chunks), take(chunks)]
    direct_ref = refs.pop(0) if len(refs) > 5 else None
    (out_ref, rows, gains, weights, sems) = refs
    width = own_ref.shape[1]
    half_hidden = own_ref.shape[2] // 2
    lane_refs = [ref.at[:, pl.ds(ref.shape[1] - LANES, LANES)] for ref in gain_refs or row_refs]
    row_refs = [ref.at[:, pl.ds(0, 2 * width)] for ref in row_refs]
    row_copies = load(chunk_pairs(row_refs, rows) + chunk_pairs(lane_refs, gains), sems.at[0])
    weight_copies = []
    for order in range(2):
        expert = (where_ref[1] + order) % 2
        parts = [own_ref.at[expert], *chunk_refs[order]]
        if direct_ref is not None:
            parts.append(direct_ref.at[expert])
        weight_copies.append(load(chunk_pairs(parts, weights.at[order]), sems.at[1 + order]))
    for copy in row_copies:
        copy.wait()
    lanes = gains[...].astype(jnp.float32)
    lane = lax.broadcasted_iota(jnp.int32, lanes.shape, 1) - first_lane
    for order in range(2):
        for copy in weight_copies[order]:
            copy.wait()
        offset = lane - (where_ref[0] * 2 + (where_ref[1] + order) % 2)
        gain = jnp.sum(
            jnp.where((offset == 0) | (offset == experts), lanes, 0.0), axis=1, keepdims=True
        )
        summed = jnp.dot(rows[...], weights[order], preferred_element_type=jnp.float32)
        hidden = jax.nn.silu(summed[:, :half_hidden]) * summed[:, half_hidden:] * gain
        out_ref[:, order * half_hidden : (order + 1) * half_hidden] = hidden.astype(jnp.bfloat16)


def run_hidden(where, row_blocks, gain_blocks, own, near, far, direct, first_lane, experts):
    blocks = len(row_blocks)
    count = sum(block.shape[0] for block in row_blocks)
    _, width, columns = own.shape
    inputs = [*row_blocks, *gain_blocks, own, *near, *far, *direct]
    return pl.pallas_call(
        functools.partial(
            hidden_kernel, blocks, len(gain_blocks), len(near), first_lane, experts
        ),
        out_shape=jax.ShapeDtypeStruct((count, columns), jnp.bfloat16),
        in_specs=[pl.BlockSpec(memory_space=pltpu.SMEM)]
        + [pl.BlockSpec(memory_space=pltpu.HBM)] * len(inputs),
        out_specs=pl.BlockSpec(memory_space=pltpu.VMEM),
        scratch_shapes=[
            pltpu.VMEM((count, 2 * width), jnp.bfloat16),
            pltpu.VMEM((count, LANES), jnp.bfloat16),
            pltpu.VMEM((2, 2 * width, columns), jnp.bfloat16),
            pltpu.SemaphoreType.DMA((3, max(2 * blocks, 2 + len(near)))),
        ],
        compiler_params=pltpu.CompilerParams(vmem_limit_bytes=20 * 1024 * 1024),
        cost_estimate=pl.CostEstimate(
            flops=8 * count * width * columns,
            bytes_accessed=4 * width * (count + 2 * columns),
            transcendentals=count * columns,
        ),
    )(where, *inputs)


def down_kernel(chunks, where_ref, hidden_ref, *refs):
    refs = list(refs)
    take = lambda count: [refs.pop(0) for _ in range(count)]
    chunk_refs = [take(chunks), take(chunks)]
    whole_refs = refs[:-4]
    mine_ref, away_ref, weights, sems = refs[-4:]
    depth = weights.shape[0] // 2
    pairs = []
    for order in range(2):
        expert = (where_ref[1] + order) % 2
        parts = chunk_refs[order] + [ref.at[expert] for ref in whole_refs]
        pairs += chunk_pairs(parts, weights, order * depth)
    for copy in load(pairs, sems):
        copy.wait()
    rows = mine_ref.shape[0]
    for half, out_ref in enumerate((mine_ref, away_ref)):
        out_ref[...] = jnp.dot(
            hidden_ref[half * rows : (half + 1) * rows, :],
            weights[...],
            preferred_element_type=jnp.float32,
        ).astype(jnp.bfloat16)


def run_down(where, hidden, near, far, whole):
    count, depth = hidden.shape
    inputs = [*near, *far, *whole]
    columns = inputs[0].shape[-1]
    shape = jax.ShapeDtypeStruct((count // 2, columns), jnp.bfloat16)
    return pl.pallas_call(
        functools.partial(down_kernel, len(near)),
        out_shape=(shape, shape),
        in_specs=[pl.BlockSpec(memory_space=pltpu.SMEM), pl.BlockSpec(memory_space=pltpu.VMEM)]
        + [pl.BlockSpec(memory_space=pltpu.HBM)] * len(inputs),
        out_specs=(pl.BlockSpec(memory_space=pltpu.VMEM),) * 2,
        scratch_shapes=[
            pltpu.VMEM((depth, columns), jnp.bfloat16),
            pltpu.SemaphoreType.DMA((2 * (len(near) + len(whole)),)),
        ],
        compiler_params=pltpu.CompilerParams(vmem_limit_bytes=16 * 1024 * 1024),
        cost_estimate=pl.CostEstimate(
            flops=2 * count * depth * columns,
            bytes_accessed=2 * (count * depth + depth * columns + count * columns),
            transcendentals=0,
        ),
    )(where, hidden, *inputs)


def over_replica(array):
    return lax.ppermute(array, "replica", SWAP)


def over_groups(array):
    return lax.ppermute(array, "groups", SWAP)


def over_expert(array, distance):
    return lax.ppermute(
        array, "expert", [(at, at ^ distance) for at in range(lax.axis_size("expert"))]
    )


def after(array, *others):
    return lax.optimization_barrier((array, *others))[0] if others else array


def send(weights, group, first_row, rows, *before):
    piece = lax.dynamic_slice(weights, (group, first_row, 0), (1, rows, weights.shape[2]))[0]
    return over_replica(after(piece, *before))


def spread_sums(mine, away, *before):
    owners = lax.axis_size("expert")
    rows = mine.shape[0] // (owners // 2)
    other = over_expert(away, 1)
    terms = []
    for index in range(owners // 2):
        part = slice(index * rows, (index + 1) * rows)
        chip = mine[part].astype(jnp.float32) + other[part].astype(jnp.float32)
        if index:
            chip = over_expert(after(chip.astype(jnp.bfloat16), *before), 2 * index)
        terms.append(chip)
    return terms


def add_up(terms):
    return sum(term.astype(jnp.float32) for term in terms).astype(jnp.bfloat16)


def in_order(replica, own, other, axis):
    return jnp.concatenate(
        [jnp.where(replica == 0, own, other), jnp.where(replica == 0, other, own)], axis=axis
    )


def dense_on_device(
    hidden_in,
    routes,
    route_gain,
    w_in,
    w_out,
    handoff,
    speaking,
    talker_routes,
    talker_gain,
    talker_w_in,
    talker_w_out,
):
    replica, group = lax.axis_index("replica"), lax.axis_index("groups")
    where = jnp.stack([lax.axis_index("expert"), group, replica]).astype(jnp.int32)
    owners = lax.axis_size("expert")
    experts = w_in.shape[0] * owners
    rows = routes.shape[0] // 2
    distances = range(2, owners, 2)

    chunk, out_chunk = w_in.shape[1] * 21 // 32, w_out.shape[1] * 2 // 3

    lanes = gain_lanes(
        where, experts, routes, route_gain, speaking, talker_routes, talker_gain
    )
    give = lax.dynamic_slice_in_dim(hidden_in, (1 - replica) * rows, rows, 0)
    other = over_replica(give)
    near_in = send(w_in, group, 0, chunk, other)
    row = build_row(where, hidden_in, other, lanes)
    same = [row] + [over_expert(row, distance) for distance in distances]
    far_in = over_groups(after(near_in, same[2]))
    direct_in = over_replica(after(w_in[:, chunk:], near_in, same[2]))
    across = [over_expert(row, 1), over_expert(jnp.concatenate(same[1:]), 1)]
    near_out = send(w_out, group, 0, out_chunk, *same)
    direct_out = over_replica(after(w_out[:, out_chunk:], direct_in))
    blocks = same + across
    hidden = run_hidden(where, blocks, [], w_in, [near_in], [far_in], [direct_in], 0, experts)
    own = run_down(where, hidden, [], [], [w_out])
    far_out = over_groups(after(near_out, *own))
    own = spread_sums(*own)
    near_talker_in = send(talker_w_in, group, 0, talker_w_in.shape[1], direct_out, hidden)
    late_hidden = after(hidden, *own[1:3])
    give = run_down(where, late_hidden, [near_out], [far_out], [direct_out])
    near_talker_out = send(talker_w_out, group, 0, talker_w_out.shape[1], near_talker_in)
    far_talker_in = over_groups(near_talker_in)
    give = after(add_up(spread_sums(*give, near_talker_in, own[3])), near_talker_out)
    own = add_up(own)
    far_talker_out = over_groups(near_talker_out)
    got = over_replica(give)
    thinker_out = in_order(replica, own, got, 0)

    def handed(array):
        return jnp.dot(array, handoff, preferred_element_type=jnp.float32)

    term = over_replica(handed(got).astype(jnp.bfloat16))
    talker_row = (handed(own) + term.astype(jnp.float32)).astype(jnp.bfloat16)
    parts = jnp.split(talker_row, 2, axis=1)
    talker_row = in_order(replica, parts[0], parts[1], 1)
    same = [talker_row] + [over_expert(talker_row, distance) for distance in distances]
    talker_blocks = same + [over_expert(talker_row, 1), over_expert(jnp.concatenate(same[1:]), 1)]
    hidden = run_hidden(
        where,
        talker_blocks,
        blocks,
        talker_w_in,
        [near_talker_in],
        [far_talker_in],
        [],
        2 * experts,
        experts,
    )
    give = run_down(where, hidden, [near_talker_out], [far_talker_out], [])
    got = over_replica(add_up(spread_sums(*give)))
    own = run_down(where, after(hidden, *give), [], [], [talker_w_out])
    own = add_up(spread_sums(*own))
    return (thinker_out, in_order(replica, own, got, 0))


def on_device(*arrays):
    token_count, top_count = arrays[1].shape
    local_experts = arrays[3].shape[0]
    experts = local_experts * lax.axis_size("expert")
    dense = (
        token_count * top_count * 2 // experts >= token_count
        and 4 * experts <= LANES
        and lax.axis_size("replica") == lax.axis_size("groups") == local_experts == 2
        and lax.axis_size("expert") in (2, 4, 8, 16)
    )
    return (dense_on_device if dense else routed_on_device)(*arrays)


def solution(mesh):
    return jax.shard_map(
        on_device,
        mesh=mesh,
        in_specs=(
            P(("groups", "expert"), "replica"),
            P(("groups", "expert"), None),
            P(("groups", "expert"), None),
            P("expert", "replica", None),
            P("expert", None, "replica"),
            P("replica", None),
            P(("groups", "expert")),
            P(("groups", "expert"), None),
            P(("groups", "expert"), None),
            P("expert", "replica", None),
            P("expert", None, "replica"),
        ),
        out_specs=(P(("groups", "expert"), "replica"), P(("groups", "expert"), "replica")),
        check_vma=False,
    )
```

```python
import functools

import jax
import jax.numpy as jnp
from jax import lax
from jax.experimental import pallas as pl
from jax.experimental.pallas import tpu as pltpu
from jax.sharding import PartitionSpec as P

LANES = 128
SWAP = [(0, 1), (1, 0)]


def place_rows(tok_rows, flat_ids, live_rows, experts, capacity):
    onehot = (flat_ids[:, None] == lax.iota(jnp.int32, experts)[None, :]).astype(
        jnp.int32
    ) * live_rows[:, None]
    before = jnp.cumsum(onehot, axis=0) - onehot
    slot_rank = jnp.sum(before * onehot, axis=1)
    slot_index = jnp.where(live_rows > 0, flat_ids * capacity + slot_rank, experts * capacity)
    buffer = (
        jnp.zeros((experts * capacity, tok_rows.shape[1]), tok_rows.dtype)
        .at[slot_index]
        .set(tok_rows, mode="drop")
    )
    return (buffer, slot_index)


def activate(gate_sum, up_sum):
    return (jax.nn.silu(gate_sum) * up_sum).astype(jnp.bfloat16)


def down_rows(second_weights, piece):
    return jnp.einsum("lrf,lfd->lrd", piece, second_weights, preferred_element_type=jnp.float32)


def routed_on_device(
    hidden_in,
    routes,
    route_gain,
    w_in,
    w_out,
    handoff,
    speaking,
    talker_routes,
    talker_gain,
    talker_w_in,
    talker_w_out,
):
    owners = lax.axis_size("expert")
    token_count, top_count = routes.shape
    local_experts = w_in.shape[0]
    experts = local_experts * owners
    capacity = max(2, token_count * top_count * 2 // experts)
    talker_capacity = max(2, capacity * 3 // 4)
    flat_ids = routes.reshape(-1)
    all_rows = jnp.ones_like(flat_ids)
    spread = jnp.repeat(hidden_in, top_count, axis=0)
    buffer, slot_index = place_rows(spread, flat_ids, all_rows, experts, capacity)
    arrived = lax.all_to_all(
        buffer.reshape(owners, local_experts, capacity, -1),
        "expert",
        split_axis=0,
        concat_axis=2,
        tiled=True,
    )
    partial_value = jnp.einsum("lrd,ldf->lrf", arrived[0], w_in, preferred_element_type=jnp.float32)
    hidden_width = w_in.shape[2] // 2
    share_sum = lax.psum_scatter(
        partial_value.astype(jnp.bfloat16), "replica", scatter_dimension=1, tiled=True
    ).astype(jnp.float32)
    hidden = activate(share_sum[:, :, :hidden_width], share_sum[:, :, hidden_width:])
    expert_out = down_rows(w_out, lax.all_gather(hidden, "replica", axis=1, tiled=True))
    returned = lax.all_to_all(
        expert_out.astype(jnp.bfloat16)[None], "expert", split_axis=2, concat_axis=0, tiled=True
    )
    returned = returned.reshape(experts * capacity, -1)
    picked = returned[slot_index].astype(jnp.float32).reshape(token_count, top_count, -1)
    thinker_out = jnp.sum(picked * route_gain[:, :, None], axis=1).astype(jnp.bfloat16)
    handoff_terms = jnp.dot(thinker_out, handoff, preferred_element_type=jnp.float32)
    talker_in = lax.psum_scatter(
        handoff_terms.astype(jnp.bfloat16), "replica", scatter_dimension=1, tiled=True
    )
    talker_ids = talker_routes.reshape(-1)
    speak_rows = jnp.repeat(speaking, top_count)
    talker_spread = jnp.repeat(talker_in, top_count, axis=0)
    talker_buffer, talker_slots = place_rows(
        talker_spread, talker_ids, speak_rows, experts, talker_capacity
    )
    talker_arrived = lax.all_to_all(
        talker_buffer.reshape(owners, local_experts, talker_capacity, -1),
        "expert",
        split_axis=0,
        concat_axis=2,
        tiled=True,
    )
    talker_partial = jnp.einsum(
        "lrd,ldf->lrf", talker_arrived[0], talker_w_in, preferred_element_type=jnp.float32
    )
    talker_hidden_width = talker_w_in.shape[2] // 2
    talker_share = lax.psum_scatter(
        talker_partial.astype(jnp.bfloat16), "replica", scatter_dimension=1, tiled=True
    ).astype(jnp.float32)
    talker_hidden = activate(
        talker_share[:, :, :talker_hidden_width], talker_share[:, :, talker_hidden_width:]
    )
    talker_expert_out = down_rows(
        talker_w_out, lax.all_gather(talker_hidden, "replica", axis=1, tiled=True)
    )
    talker_returned = lax.all_to_all(
        talker_expert_out.astype(jnp.bfloat16)[None],
        "expert",
        split_axis=2,
        concat_axis=0,
        tiled=True,
    )
    talker_returned = talker_returned.reshape(experts * talker_capacity, -1)
    safe_slots = jnp.minimum(talker_slots, experts * talker_capacity - 1)
    talker_picked = (
        talker_returned[safe_slots].astype(jnp.float32).reshape(token_count, top_count, -1)
    )
    talker_weights = talker_gain * speak_rows.reshape(token_count, top_count).astype(jnp.float32)
    talker_out = jnp.sum(talker_picked * talker_weights[:, :, None], axis=1).astype(jnp.bfloat16)
    return (thinker_out, talker_out)


def lanes_kernel(experts, where_ref, *refs):
    routes_ref, gain_ref, live_ref, talker_routes_ref, talker_gain_ref, out_ref, lanes = refs
    rows = out_ref.shape[0]
    stack = []
    live = live_ref[...].astype(jnp.float32)
    for ids, gains in ((routes_ref, gain_ref[...]), (talker_routes_ref, talker_gain_ref[...] * live)):
        expert = lax.broadcasted_iota(jnp.int32, (experts, ids.shape[1]), 0)
        dense = jnp.zeros(expert.shape, jnp.float32)
        for choice in range(ids.shape[0]):
            dense += jnp.where(
                ids[choice : choice + 1, :] == expert, gains[choice : choice + 1, :], 0.0
            )
        high = dense.astype(jnp.bfloat16).astype(jnp.float32)
        stack += [high, dense - high]
    stack.append(jnp.zeros((LANES - 4 * experts, live.shape[1]), jnp.float32))
    lanes[...] = jnp.concatenate(stack, axis=0).T
    first = pl.multiple_of(where_ref[2] * rows, rows)
    out_ref[...] = lanes[pl.ds(first, rows), :].astype(jnp.bfloat16)


def gain_lanes(where, experts, routes, gain, live, talker_routes, talker_gain):
    count = routes.shape[0]
    inputs = [routes.T, gain.T, live[None], talker_routes.T, talker_gain.T]
    return pl.pallas_call(
        functools.partial(lanes_kernel, experts),
        out_shape=jax.ShapeDtypeStruct((count // 2, LANES), jnp.bfloat16),
        in_specs=[pl.BlockSpec(memory_space=pltpu.SMEM)]
        + [pl.BlockSpec(memory_space=pltpu.VMEM)] * len(inputs),
        out_specs=pl.BlockSpec(memory_space=pltpu.VMEM),
        scratch_shapes=[pltpu.VMEM((count, LANES), jnp.float32)],
        compiler_params=pltpu.CompilerParams(vmem_limit_bytes=4 * 1024 * 1024),
        cost_estimate=pl.CostEstimate(
            flops=1 << 30, bytes_accessed=64 * count * LANES, transcendentals=0
        ),
    )(where, *inputs)


def row_kernel(where_ref, hidden_ref, other_ref, lanes_ref, out_ref):
    rows, width = other_ref.shape
    first = pl.multiple_of(where_ref[2] * rows, rows)
    out_ref[:, :width] = hidden_ref[pl.ds(first, rows), :]
    out_ref[:, width : 2 * width] = other_ref[...]
    out_ref[:, 2 * width :] = lanes_ref[...]


def build_row(where, hidden_in, other, lanes):
    rows, width = other.shape
    return pl.pallas_call(
        row_kernel,
        out_shape=jax.ShapeDtypeStruct((rows, 2 * width + LANES), jnp.bfloat16),
        in_specs=[pl.BlockSpec(memory_space=pltpu.SMEM)]
        + [pl.BlockSpec(memory_space=pltpu.VMEM)] * 3,
        out_specs=pl.BlockSpec(memory_space=pltpu.VMEM),
        compiler_params=pltpu.CompilerParams(vmem_limit_bytes=4 * 1024 * 1024),
        cost_estimate=pl.CostEstimate(flops=0, bytes_accessed=8 * rows * width, transcendentals=0),
    )(where, hidden_in, other, lanes)


def load(pairs, sems):
    copies = [
        pltpu.make_async_copy(source, destination, sems.at[index])
        for index, (source, destination) in enumerate(pairs)
    ]
    for copy in copies:
        copy.start()
    return copies


def chunk_pairs(chunks, place, first_row=0):
    pairs, row = [], first_row
    for chunk in chunks:
        pairs.append((chunk, place.at[pl.ds(row, chunk.shape[0])]))
        row += chunk.shape[0]
    return pairs


def hidden_kernel(blocks, gain_blocks, chunks, direct, first_lane, experts, where_ref, *refs):
    refs = list(refs)
    take = lambda count: [refs.pop(0) for _ in range(count)]
    row_refs, gain_refs = take(blocks), take(gain_blocks)
    (own_ref,) = take(1)
    chunk_refs = [take(chunks), take(chunks)]
    direct_refs = take(direct)
    out_ref, rows, gains, weights, sems = refs[-5:]
    width = own_ref.shape[1]
    half_hidden = own_ref.shape[2] // 2
    lane_refs = [ref.at[:, pl.ds(ref.shape[1] - LANES, LANES)] for ref in gain_refs or row_refs]
    row_refs = [ref.at[:, pl.ds(0, 2 * width)] for ref in row_refs]
    row_copies = load(chunk_pairs(row_refs, rows) + chunk_pairs(lane_refs, gains), sems.at[0])
    weight_copies = []
    for order in range(2):
        expert = (where_ref[1] + order) % 2
        parts = [own_ref.at[expert], *chunk_refs[order]]
        parts += [ref.at[expert] for ref in direct_refs]
        weight_copies.append(load(chunk_pairs(parts, weights.at[order]), sems.at[1 + order]))
    for copy in row_copies:
        copy.wait()
    lanes = gains[...].astype(jnp.float32)
    lane = lax.broadcasted_iota(jnp.int32, lanes.shape, 1) - first_lane
    for order in range(2):
        for copy in weight_copies[order]:
            copy.wait()
        offset = lane - (where_ref[0] * 2 + (where_ref[1] + order) % 2)
        gain = jnp.sum(
            jnp.where((offset == 0) | (offset == experts), lanes, 0.0), axis=1, keepdims=True
        )
        summed = jnp.dot(rows[...], weights[order], preferred_element_type=jnp.float32)
        hidden = jax.nn.silu(summed[:, :half_hidden]) * summed[:, half_hidden:] * gain
        out_ref[:, order * half_hidden : (order + 1) * half_hidden] = hidden.astype(jnp.bfloat16)


def run_hidden(where, row_blocks, gain_blocks, own, near, far, direct, before, first_lane, experts):
    blocks = len(row_blocks)
    count = sum(block.shape[0] for block in row_blocks)
    _, width, columns = own.shape
    inputs = [*row_blocks, *gain_blocks, own, *near, *far, *direct, *before]
    return pl.pallas_call(
        functools.partial(
            hidden_kernel, blocks, len(gain_blocks), len(near), len(direct), first_lane, experts
        ),
        out_shape=jax.ShapeDtypeStruct((count, columns), jnp.bfloat16),
        in_specs=[pl.BlockSpec(memory_space=pltpu.SMEM)]
        + [pl.BlockSpec(memory_space=pltpu.HBM)] * len(inputs),
        out_specs=pl.BlockSpec(memory_space=pltpu.VMEM),
        scratch_shapes=[
            pltpu.VMEM((count, 2 * width), jnp.bfloat16),
            pltpu.VMEM((count, LANES), jnp.bfloat16),
            pltpu.VMEM((2, 2 * width, columns), jnp.bfloat16),
            pltpu.SemaphoreType.DMA((3, max(2 * blocks, 2 + len(near)))),
        ],
        compiler_params=pltpu.CompilerParams(vmem_limit_bytes=20 * 1024 * 1024),
        cost_estimate=pl.CostEstimate(
            flops=8 * count * width * columns,
            bytes_accessed=4 * width * (count + 2 * columns),
            transcendentals=count * columns,
        ),
    )(where, *inputs)


def down_kernel(chunks, where_ref, hidden_ref, *refs):
    refs = list(refs)
    take = lambda count: [refs.pop(0) for _ in range(count)]
    chunk_refs = [take(chunks), take(chunks)]
    whole_refs = refs[:-4]
    mine_ref, away_ref, weights, sems = refs[-4:]
    depth = weights.shape[0] // 2
    pairs = []
    for order in range(2):
        expert = (where_ref[1] + order) % 2
        parts = chunk_refs[order] + [ref.at[expert] for ref in whole_refs]
        pairs += chunk_pairs(parts, weights, order * depth)
    for copy in load(pairs, sems):
        copy.wait()
    rows = mine_ref.shape[0]
    for half, out_ref in enumerate((mine_ref, away_ref)):
        out_ref[...] = jnp.dot(
            hidden_ref[half * rows : (half + 1) * rows, :],
            weights[...],
            preferred_element_type=jnp.float32,
        ).astype(jnp.bfloat16)


def run_down(where, hidden, near, far, whole):
    count, depth = hidden.shape
    inputs = [*near, *far, *whole]
    columns = inputs[0].shape[-1]
    shape = jax.ShapeDtypeStruct((count // 2, columns), jnp.bfloat16)
    return pl.pallas_call(
        functools.partial(down_kernel, len(near)),
        out_shape=(shape, shape),
        in_specs=[pl.BlockSpec(memory_space=pltpu.SMEM), pl.BlockSpec(memory_space=pltpu.VMEM)]
        + [pl.BlockSpec(memory_space=pltpu.HBM)] * len(inputs),
        out_specs=(pl.BlockSpec(memory_space=pltpu.VMEM),) * 2,
        scratch_shapes=[
            pltpu.VMEM((depth, columns), jnp.bfloat16),
            pltpu.SemaphoreType.DMA((2 * (len(near) + len(whole)),)),
        ],
        compiler_params=pltpu.CompilerParams(vmem_limit_bytes=16 * 1024 * 1024),
        cost_estimate=pl.CostEstimate(
            flops=2 * count * depth * columns,
            bytes_accessed=2 * (count * depth + depth * columns + count * columns),
            transcendentals=0,
        ),
    )(where, hidden, *inputs)


def over_replica(array):
    return lax.ppermute(array, "replica", SWAP)


def over_groups(array):
    return lax.ppermute(array, "groups", SWAP)


def over_expert(array, distance):
    return lax.ppermute(
        array, "expert", [(at, at ^ distance) for at in range(lax.axis_size("expert"))]
    )


def after(array, *others):
    return lax.optimization_barrier((array, *others))[0] if others else array


def send(weights, group, first_row, rows, *before):
    piece = lax.dynamic_slice(weights, (group, first_row, 0), (1, rows, weights.shape[2]))[0]
    return over_replica(after(piece, *before))


def spread_sums(mine, away, *before):
    owners = lax.axis_size("expert")
    rows = mine.shape[0] // (owners // 2)
    other = over_expert(away, 1)
    terms = []
    for index in range(owners // 2):
        part = slice(index * rows, (index + 1) * rows)
        chip = mine[part].astype(jnp.float32) + other[part].astype(jnp.float32)
        if index:
            chip = over_expert(after(chip.astype(jnp.bfloat16), *before), 2 * index)
        terms.append(chip)
    return terms


def add_up(terms):
    return sum(term.astype(jnp.float32) for term in terms).astype(jnp.bfloat16)


def in_order(replica, own, other, axis):
    return jnp.concatenate(
        [jnp.where(replica == 0, own, other), jnp.where(replica == 0, other, own)], axis=axis
    )


def dense_on_device(
    hidden_in,
    routes,
    route_gain,
    w_in,
    w_out,
    handoff,
    speaking,
    talker_routes,
    talker_gain,
    talker_w_in,
    talker_w_out,
):
    replica, group = lax.axis_index("replica"), lax.axis_index("groups")
    where = jnp.stack([lax.axis_index("expert"), group, replica]).astype(jnp.int32)
    owners = lax.axis_size("expert")
    experts = w_in.shape[0] * owners
    rows = routes.shape[0] // 2
    distances = range(2, owners, 2)

    chunk, out_chunk = w_in.shape[1] * 13 // 32, w_out.shape[1] * 2 // 3

    lanes = gain_lanes(
        where, experts, routes, route_gain, speaking, talker_routes, talker_gain
    )
    give = lax.dynamic_slice_in_dim(hidden_in, (1 - replica) * rows, rows, 0)
    other = over_replica(give)
    near_in = [send(w_in, group, index * chunk, chunk, other) for index in range(2)]
    row = build_row(where, hidden_in, other, lanes)
    same = [row] + [over_expert(row, distance) for distance in distances]
    far_in = [over_groups(after(near_in[0], same[1]))]
    far_in.append(over_groups(after(near_in[1], far_in[0])))
    direct_in = over_replica(after(w_in[:, 2 * chunk :], near_in[0]))
    across = [over_expert(row, 1), over_expert(jnp.concatenate(same[1:]), 1)]
    near_out = send(w_out, group, 0, out_chunk, near_in[1])
    direct_out = over_replica(after(w_out[:, out_chunk:], direct_in))
    blocks = same + across
    hidden = run_hidden(where, blocks, [], w_in, near_in, far_in, [direct_in], [], 0, experts)
    own = run_down(where, hidden, [], [], [w_out])
    far_out = over_groups(after(near_out, *own))
    own = spread_sums(*own)
    late_hidden = after(hidden, own[1])
    give = run_down(where, late_hidden, [near_out], [far_out], [direct_out])
    near_talker_in = send(talker_w_in, group, 0, talker_w_in.shape[1], near_out, hidden)
    give = spread_sums(*give, *own[2:])
    far_talker_in = over_groups(after(near_talker_in, give[1]))
    give, own = add_up(give), add_up(own)
    got = over_replica(give)
    thinker_out = in_order(replica, own, got, 0)

    def handed(array):
        return jnp.dot(array, handoff, preferred_element_type=jnp.float32)

    term = over_replica(handed(got).astype(jnp.bfloat16))
    direct_talker_out = over_replica(after(talker_w_out, term))
    talker_row = (handed(own) + term.astype(jnp.float32)).astype(jnp.bfloat16)
    parts = jnp.split(talker_row, 2, axis=1)
    talker_row = in_order(replica, parts[0], parts[1], 1)
    same = [talker_row] + [over_expert(talker_row, distance) for distance in distances]
    talker_blocks = same + [over_expert(talker_row, 1), over_expert(jnp.concatenate(same[1:]), 1)]
    hidden = run_hidden(
        where,
        talker_blocks,
        blocks,
        talker_w_in,
        [near_talker_in],
        [far_talker_in],
        [],
        [direct_talker_out],
        2 * experts,
        experts,
    )
    give = run_down(where, hidden, [], [], [direct_talker_out])
    got = over_replica(add_up(spread_sums(*give)))
    own = run_down(where, after(hidden, *give), [], [], [talker_w_out])
    own = add_up(spread_sums(*own))
    return (thinker_out, in_order(replica, own, got, 0))


def on_device(*arrays):
    token_count, top_count = arrays[1].shape
    local_experts = arrays[3].shape[0]
    experts = local_experts * lax.axis_size("expert")
    dense = (
        token_count * top_count * 2 // experts >= token_count
        and 4 * experts <= LANES
        and lax.axis_size("replica") == lax.axis_size("groups") == local_experts == 2
        and lax.axis_size("expert") in (2, 4, 8, 16)
    )
    return (dense_on_device if dense else routed_on_device)(*arrays)


def solution(mesh):
    return jax.shard_map(
        on_device,
        mesh=mesh,
        in_specs=(
            P(("groups", "expert"), "replica"),
            P(("groups", "expert"), None),
            P(("groups", "expert"), None),
            P("expert", "replica", None),
            P("expert", None, "replica"),
            P("replica", None),
            P(("groups", "expert")),
            P(("groups", "expert"), None),
            P(("groups", "expert"), None),
            P("expert", "replica", None),
            P("expert", None, "replica"),
        ),
        out_specs=(P(("groups", "expert"), "replica"), P(("groups", "expert"), "replica")),
        check_vma=False,
    )
```

```python
import functools

import jax
import jax.numpy as jnp
from jax import lax
from jax.experimental import pallas as pl
from jax.experimental.pallas import tpu as pltpu
from jax.sharding import PartitionSpec as P

LANES = 128
SWAP = [(0, 1), (1, 0)]


def place_rows(tok_rows, flat_ids, live_rows, experts, capacity):
    onehot = (flat_ids[:, None] == lax.iota(jnp.int32, experts)[None, :]).astype(
        jnp.int32
    ) * live_rows[:, None]
    before = jnp.cumsum(onehot, axis=0) - onehot
    slot_rank = jnp.sum(before * onehot, axis=1)
    slot_index = jnp.where(live_rows > 0, flat_ids * capacity + slot_rank, experts * capacity)
    buffer = (
        jnp.zeros((experts * capacity, tok_rows.shape[1]), tok_rows.dtype)
        .at[slot_index]
        .set(tok_rows, mode="drop")
    )
    return (buffer, slot_index)


def activate(gate_sum, up_sum):
    return (jax.nn.silu(gate_sum) * up_sum).astype(jnp.bfloat16)


def down_rows(second_weights, piece):
    return jnp.einsum("lrf,lfd->lrd", piece, second_weights, preferred_element_type=jnp.float32)


def routed_on_device(
    hidden_in,
    routes,
    route_gain,
    w_in,
    w_out,
    handoff,
    speaking,
    talker_routes,
    talker_gain,
    talker_w_in,
    talker_w_out,
):
    owners = lax.axis_size("expert")
    token_count, top_count = routes.shape
    local_experts = w_in.shape[0]
    experts = local_experts * owners
    capacity = max(2, token_count * top_count * 2 // experts)
    talker_capacity = max(2, capacity * 3 // 4)
    flat_ids = routes.reshape(-1)
    all_rows = jnp.ones_like(flat_ids)
    spread = jnp.repeat(hidden_in, top_count, axis=0)
    buffer, slot_index = place_rows(spread, flat_ids, all_rows, experts, capacity)
    arrived = lax.all_to_all(
        buffer.reshape(owners, local_experts, capacity, -1),
        "expert",
        split_axis=0,
        concat_axis=2,
        tiled=True,
    )
    partial_value = jnp.einsum("lrd,ldf->lrf", arrived[0], w_in, preferred_element_type=jnp.float32)
    hidden_width = w_in.shape[2] // 2
    share_sum = lax.psum_scatter(
        partial_value.astype(jnp.bfloat16), "replica", scatter_dimension=1, tiled=True
    ).astype(jnp.float32)
    hidden = activate(share_sum[:, :, :hidden_width], share_sum[:, :, hidden_width:])
    expert_out = down_rows(w_out, lax.all_gather(hidden, "replica", axis=1, tiled=True))
    returned = lax.all_to_all(
        expert_out.astype(jnp.bfloat16)[None], "expert", split_axis=2, concat_axis=0, tiled=True
    )
    returned = returned.reshape(experts * capacity, -1)
    picked = returned[slot_index].astype(jnp.float32).reshape(token_count, top_count, -1)
    thinker_out = jnp.sum(picked * route_gain[:, :, None], axis=1).astype(jnp.bfloat16)
    handoff_terms = jnp.dot(thinker_out, handoff, preferred_element_type=jnp.float32)
    talker_in = lax.psum_scatter(
        handoff_terms.astype(jnp.bfloat16), "replica", scatter_dimension=1, tiled=True
    )
    talker_ids = talker_routes.reshape(-1)
    speak_rows = jnp.repeat(speaking, top_count)
    talker_spread = jnp.repeat(talker_in, top_count, axis=0)
    talker_buffer, talker_slots = place_rows(
        talker_spread, talker_ids, speak_rows, experts, talker_capacity
    )
    talker_arrived = lax.all_to_all(
        talker_buffer.reshape(owners, local_experts, talker_capacity, -1),
        "expert",
        split_axis=0,
        concat_axis=2,
        tiled=True,
    )
    talker_partial = jnp.einsum(
        "lrd,ldf->lrf", talker_arrived[0], talker_w_in, preferred_element_type=jnp.float32
    )
    talker_hidden_width = talker_w_in.shape[2] // 2
    talker_share = lax.psum_scatter(
        talker_partial.astype(jnp.bfloat16), "replica", scatter_dimension=1, tiled=True
    ).astype(jnp.float32)
    talker_hidden = activate(
        talker_share[:, :, :talker_hidden_width], talker_share[:, :, talker_hidden_width:]
    )
    talker_expert_out = down_rows(
        talker_w_out, lax.all_gather(talker_hidden, "replica", axis=1, tiled=True)
    )
    talker_returned = lax.all_to_all(
        talker_expert_out.astype(jnp.bfloat16)[None],
        "expert",
        split_axis=2,
        concat_axis=0,
        tiled=True,
    )
    talker_returned = talker_returned.reshape(experts * talker_capacity, -1)
    safe_slots = jnp.minimum(talker_slots, experts * talker_capacity - 1)
    talker_picked = (
        talker_returned[safe_slots].astype(jnp.float32).reshape(token_count, top_count, -1)
    )
    talker_weights = talker_gain * speak_rows.reshape(token_count, top_count).astype(jnp.float32)
    talker_out = jnp.sum(talker_picked * talker_weights[:, :, None], axis=1).astype(jnp.bfloat16)
    return (thinker_out, talker_out)


def lanes_kernel(experts, where_ref, *refs):
    routes_ref, gain_ref, live_ref, talker_routes_ref, talker_gain_ref, out_ref, lanes = refs
    rows = out_ref.shape[0]
    stack = []
    live = live_ref[...].astype(jnp.float32)
    for ids, gains in ((routes_ref, gain_ref[...]), (talker_routes_ref, talker_gain_ref[...] * live)):
        expert = lax.broadcasted_iota(jnp.int32, (experts, ids.shape[1]), 0)
        dense = jnp.zeros(expert.shape, jnp.float32)
        for choice in range(ids.shape[0]):
            dense += jnp.where(
                ids[choice : choice + 1, :] == expert, gains[choice : choice + 1, :], 0.0
            )
        high = dense.astype(jnp.bfloat16).astype(jnp.float32)
        stack += [high, dense - high]
    stack.append(jnp.zeros((LANES - 4 * experts, live.shape[1]), jnp.float32))
    lanes[...] = jnp.concatenate(stack, axis=0).T
    first = pl.multiple_of(where_ref[2] * rows, rows)
    out_ref[...] = lanes[pl.ds(first, rows), :].astype(jnp.bfloat16)


def gain_lanes(where, experts, routes, gain, live, talker_routes, talker_gain):
    count = routes.shape[0]
    inputs = [routes.T, gain.T, live[None], talker_routes.T, talker_gain.T]
    return pl.pallas_call(
        functools.partial(lanes_kernel, experts),
        out_shape=jax.ShapeDtypeStruct((count // 2, LANES), jnp.bfloat16),
        in_specs=[pl.BlockSpec(memory_space=pltpu.SMEM)]
        + [pl.BlockSpec(memory_space=pltpu.VMEM)] * len(inputs),
        out_specs=pl.BlockSpec(memory_space=pltpu.VMEM),
        scratch_shapes=[pltpu.VMEM((count, LANES), jnp.float32)],
        compiler_params=pltpu.CompilerParams(vmem_limit_bytes=4 * 1024 * 1024),
        cost_estimate=pl.CostEstimate(
            flops=1 << 30, bytes_accessed=64 * count * LANES, transcendentals=0
        ),
    )(where, *inputs)


def row_kernel(where_ref, hidden_ref, other_ref, lanes_ref, out_ref):
    rows, width = other_ref.shape
    first = pl.multiple_of(where_ref[2] * rows, rows)
    out_ref[:, :width] = hidden_ref[pl.ds(first, rows), :]
    out_ref[:, width : 2 * width] = other_ref[...]
    out_ref[:, 2 * width :] = lanes_ref[...]


def build_row(where, hidden_in, other, lanes):
    rows, width = other.shape
    return pl.pallas_call(
        row_kernel,
        out_shape=jax.ShapeDtypeStruct((rows, 2 * width + LANES), jnp.bfloat16),
        in_specs=[pl.BlockSpec(memory_space=pltpu.SMEM)]
        + [pl.BlockSpec(memory_space=pltpu.VMEM)] * 3,
        out_specs=pl.BlockSpec(memory_space=pltpu.VMEM),
        compiler_params=pltpu.CompilerParams(vmem_limit_bytes=4 * 1024 * 1024),
        cost_estimate=pl.CostEstimate(flops=0, bytes_accessed=8 * rows * width, transcendentals=0),
    )(where, hidden_in, other, lanes)


def load(pairs, sems):
    copies = [
        pltpu.make_async_copy(source, destination, sems.at[index])
        for index, (source, destination) in enumerate(pairs)
    ]
    for copy in copies:
        copy.start()
    return copies


def chunk_pairs(chunks, place, first_row=0):
    pairs, row = [], first_row
    for chunk in chunks:
        pairs.append((chunk, place.at[pl.ds(row, chunk.shape[0])]))
        row += chunk.shape[0]
    return pairs


def hidden_kernel(blocks, gain_blocks, chunks, direct, first_lane, experts, where_ref, *refs):
    refs = list(refs)
    take = lambda count: [refs.pop(0) for _ in range(count)]
    row_refs, gain_refs = take(blocks), take(gain_blocks)
    (own_ref,) = take(1)
    chunk_refs = [take(chunks), take(chunks)]
    direct_refs = take(direct)
    out_ref, rows, gains, weights, sems = refs[-5:]
    width = own_ref.shape[1]
    half_hidden = own_ref.shape[2] // 2
    lane_refs = [ref.at[:, pl.ds(ref.shape[1] - LANES, LANES)] for ref in gain_refs or row_refs]
    row_refs = [ref.at[:, pl.ds(0, 2 * width)] for ref in row_refs]
    row_copies = load(chunk_pairs(row_refs, rows) + chunk_pairs(lane_refs, gains), sems.at[0])
    weight_copies = []
    for order in range(2):
        expert = (where_ref[1] + order) % 2
        parts = [own_ref.at[expert], *chunk_refs[order]]
        parts += [ref.at[expert] for ref in direct_refs]
        weight_copies.append(load(chunk_pairs(parts, weights.at[order]), sems.at[1 + order]))
    for copy in row_copies:
        copy.wait()
    lanes = gains[...].astype(jnp.float32)
    lane = lax.broadcasted_iota(jnp.int32, lanes.shape, 1) - first_lane
    for order in range(2):
        for copy in weight_copies[order]:
            copy.wait()
        offset = lane - (where_ref[0] * 2 + (where_ref[1] + order) % 2)
        gain = jnp.sum(
            jnp.where((offset == 0) | (offset == experts), lanes, 0.0), axis=1, keepdims=True
        )
        summed = jnp.dot(rows[...], weights[order], preferred_element_type=jnp.float32)
        hidden = jax.nn.silu(summed[:, :half_hidden]) * summed[:, half_hidden:] * gain
        out_ref[:, order * half_hidden : (order + 1) * half_hidden] = hidden.astype(jnp.bfloat16)


def run_hidden(where, row_blocks, gain_blocks, own, near, far, direct, before, first_lane, experts):
    blocks = len(row_blocks)
    count = sum(block.shape[0] for block in row_blocks)
    _, width, columns = own.shape
    inputs = [*row_blocks, *gain_blocks, own, *near, *far, *direct, *before]
    return pl.pallas_call(
        functools.partial(
            hidden_kernel, blocks, len(gain_blocks), len(near), len(direct), first_lane, experts
        ),
        out_shape=jax.ShapeDtypeStruct((count, columns), jnp.bfloat16),
        in_specs=[pl.BlockSpec(memory_space=pltpu.SMEM)]
        + [pl.BlockSpec(memory_space=pltpu.HBM)] * len(inputs),
        out_specs=pl.BlockSpec(memory_space=pltpu.VMEM),
        scratch_shapes=[
            pltpu.VMEM((count, 2 * width), jnp.bfloat16),
            pltpu.VMEM((count, LANES), jnp.bfloat16),
            pltpu.VMEM((2, 2 * width, columns), jnp.bfloat16),
            pltpu.SemaphoreType.DMA((3, max(2 * blocks, 2 + len(near)))),
        ],
        compiler_params=pltpu.CompilerParams(vmem_limit_bytes=20 * 1024 * 1024),
        cost_estimate=pl.CostEstimate(
            flops=8 * count * width * columns,
            bytes_accessed=4 * width * (count + 2 * columns),
            transcendentals=count * columns,
        ),
    )(where, *inputs)


def down_kernel(chunks, where_ref, hidden_ref, *refs):
    refs = list(refs)
    take = lambda count: [refs.pop(0) for _ in range(count)]
    chunk_refs = [take(chunks), take(chunks)]
    whole_refs = refs[:-4]
    mine_ref, away_ref, weights, sems = refs[-4:]
    depth = weights.shape[0] // 2
    pairs = []
    for order in range(2):
        expert = (where_ref[1] + order) % 2
        parts = chunk_refs[order] + [ref.at[expert] for ref in whole_refs]
        pairs += chunk_pairs(parts, weights, order * depth)
    for copy in load(pairs, sems):
        copy.wait()
    rows = mine_ref.shape[0]
    for half, out_ref in enumerate((mine_ref, away_ref)):
        out_ref[...] = jnp.dot(
            hidden_ref[half * rows : (half + 1) * rows, :],
            weights[...],
            preferred_element_type=jnp.float32,
        ).astype(jnp.bfloat16)


def run_down(where, hidden, near, far, whole):
    count, depth = hidden.shape
    inputs = [*near, *far, *whole]
    columns = inputs[0].shape[-1]
    shape = jax.ShapeDtypeStruct((count // 2, columns), jnp.bfloat16)
    return pl.pallas_call(
        functools.partial(down_kernel, len(near)),
        out_shape=(shape, shape),
        in_specs=[pl.BlockSpec(memory_space=pltpu.SMEM), pl.BlockSpec(memory_space=pltpu.VMEM)]
        + [pl.BlockSpec(memory_space=pltpu.HBM)] * len(inputs),
        out_specs=(pl.BlockSpec(memory_space=pltpu.VMEM),) * 2,
        scratch_shapes=[
            pltpu.VMEM((depth, columns), jnp.bfloat16),
            pltpu.SemaphoreType.DMA((2 * (len(near) + len(whole)),)),
        ],
        compiler_params=pltpu.CompilerParams(vmem_limit_bytes=16 * 1024 * 1024),
        cost_estimate=pl.CostEstimate(
            flops=2 * count * depth * columns,
            bytes_accessed=2 * (count * depth + depth * columns + count * columns),
            transcendentals=0,
        ),
    )(where, hidden, *inputs)


def over_replica(array):
    return lax.ppermute(array, "replica", SWAP)


def over_groups(array):
    return lax.ppermute(array, "groups", SWAP)


def over_expert(array, distance):
    return lax.ppermute(
        array, "expert", [(at, at ^ distance) for at in range(lax.axis_size("expert"))]
    )


def after(array, *others):
    return lax.optimization_barrier((array, *others))[0] if others else array


def send(weights, group, first_row, rows, *before):
    piece = lax.dynamic_slice(weights, (group, first_row, 0), (1, rows, weights.shape[2]))[0]
    return over_replica(after(piece, *before))


def over_both(array, distance):
    owners = lax.axis_size("expert")
    pairs = [
        (2 * at + replica, 2 * (at ^ distance) + 1 - replica)
        for at in range(owners)
        for replica in range(2)
    ]
    return lax.ppermute(array, ("expert", "replica"), pairs)


def spread_sums(mine, away, before=(), hold=(), cross=False):
    owners = lax.axis_size("expert")
    rows = mine.shape[0] // (owners // 2)
    other = over_expert(after(away, *hold), 1)
    terms = []
    for index in range(owners // 2):
        part = slice(index * rows, (index + 1) * rows)
        chip = mine[part].astype(jnp.float32) + other[part].astype(jnp.float32)
        if cross or index:
            chip = after(chip.astype(jnp.bfloat16), *before)
            chip = (over_both if cross else over_expert)(chip, 2 * index)
        terms.append(chip)
    return terms


def add_up(terms):
    return sum(term.astype(jnp.float32) for term in terms).astype(jnp.bfloat16)


def in_order(replica, own, other, axis):
    return jnp.concatenate(
        [jnp.where(replica == 0, own, other), jnp.where(replica == 0, other, own)], axis=axis
    )


def dense_on_device(
    hidden_in,
    routes,
    route_gain,
    w_in,
    w_out,
    handoff,
    speaking,
    talker_routes,
    talker_gain,
    talker_w_in,
    talker_w_out,
):
    replica, group = lax.axis_index("replica"), lax.axis_index("groups")
    where = jnp.stack([lax.axis_index("expert"), group, replica]).astype(jnp.int32)
    owners = lax.axis_size("expert")
    experts = w_in.shape[0] * owners
    rows = routes.shape[0] // 2
    distances = range(2, owners, 2)

    width, chunk, out_chunk = w_in.shape[1], w_in.shape[1] * 11 // 32, w_out.shape[1] * 2 // 3

    lanes = gain_lanes(
        where, experts, routes, route_gain, speaking, talker_routes, talker_gain
    )
    give = lax.dynamic_slice_in_dim(hidden_in, (1 - replica) * rows, rows, 0)
    other = over_replica(give)
    near_in = [
        send(w_in, group, first, min(chunk, width - first), other)
        for first in range(0, width, chunk)
    ]
    row = build_row(where, hidden_in, other, lanes)
    same = [row] + [over_expert(row, distance) for distance in distances]
    far_in = [over_groups(after(near_in[0], same[1]))]
    for part in near_in[1:]:
        far_in.append(over_groups(after(part, far_in[-1])))
    across = [over_expert(row, 1), over_expert(jnp.concatenate(same[1:]), 1)]
    near_out = send(w_out, group, 0, out_chunk, near_in[1])
    direct_out = over_replica(after(w_out[:, out_chunk:], near_out))
    far_out = over_groups(near_out)
    blocks = same + across
    hidden = run_hidden(where, blocks, [], w_in, near_in, far_in, [], [near_out], 0, experts)
    own = run_down(where, hidden, [], [], [w_out])
    own = spread_sums(*own, hold=[direct_out, far_out])
    near_talker_in = send(talker_w_in, group, 0, talker_w_in.shape[1], near_out, hidden)
    give = run_down(where, hidden, [near_out], [far_out], [direct_out])
    got = spread_sums(*give, before=[own[2], near_talker_in], cross=True)
    far_talker_in = over_groups(near_talker_in)
    got, own = add_up(got), add_up(own)
    thinker_out = in_order(replica, own, got, 0)

    def handed(array):
        return jnp.dot(array, handoff, preferred_element_type=jnp.float32)

    term = over_replica(handed(got).astype(jnp.bfloat16))
    direct_talker_out = over_replica(after(talker_w_out, term))
    talker_row = (handed(own) + term.astype(jnp.float32)).astype(jnp.bfloat16)
    parts = jnp.split(talker_row, 2, axis=1)
    talker_row = in_order(replica, parts[0], parts[1], 1)
    same = [talker_row] + [over_expert(talker_row, distance) for distance in distances]
    rest = after(jnp.concatenate(same[1:]), far_talker_in)
    talker_blocks = same + [over_expert(talker_row, 1), over_expert(rest, 1)]
    hidden = run_hidden(
        where,
        talker_blocks,
        blocks,
        talker_w_in,
        [near_talker_in],
        [far_talker_in],
        [],
        [direct_talker_out],
        2 * experts,
        experts,
    )
    give = run_down(where, hidden, [], [], [direct_talker_out])
    got = add_up(spread_sums(*give, cross=True))
    own = run_down(where, after(hidden, *give), [], [], [talker_w_out])
    own = add_up(spread_sums(*own))
    return (thinker_out, in_order(replica, own, got, 0))


def on_device(*arrays):
    token_count, top_count = arrays[1].shape
    local_experts = arrays[3].shape[0]
    experts = local_experts * lax.axis_size("expert")
    dense = (
        token_count * top_count * 2 // experts >= token_count
        and 4 * experts <= LANES
        and lax.axis_size("replica") == lax.axis_size("groups") == local_experts == 2
        and lax.axis_size("expert") in (2, 4, 8, 16)
    )
    return (dense_on_device if dense else routed_on_device)(*arrays)


def solution(mesh):
    return jax.shard_map(
        on_device,
        mesh=mesh,
        in_specs=(
            P(("groups", "expert"), "replica"),
            P(("groups", "expert"), None),
            P(("groups", "expert"), None),
            P("expert", "replica", None),
            P("expert", None, "replica"),
            P("replica", None),
            P(("groups", "expert")),
            P(("groups", "expert"), None),
            P(("groups", "expert"), None),
            P("expert", "replica", None),
            P("expert", None, "replica"),
        ),
        out_specs=(P(("groups", "expert"), "replica"), P(("groups", "expert"), "replica")),
        check_vma=False,
    )
```

```python
import functools

import jax
import jax.numpy as jnp
from jax import lax
from jax.experimental import pallas as pl
from jax.experimental.pallas import tpu as pltpu
from jax.sharding import PartitionSpec as P

LANES = 128
SWAP = [(0, 1), (1, 0)]


def place_rows(tok_rows, flat_ids, live_rows, experts, capacity):
    onehot = (flat_ids[:, None] == lax.iota(jnp.int32, experts)[None, :]).astype(
        jnp.int32
    ) * live_rows[:, None]
    before = jnp.cumsum(onehot, axis=0) - onehot
    slot_rank = jnp.sum(before * onehot, axis=1)
    slot_index = jnp.where(live_rows > 0, flat_ids * capacity + slot_rank, experts * capacity)
    buffer = (
        jnp.zeros((experts * capacity, tok_rows.shape[1]), tok_rows.dtype)
        .at[slot_index]
        .set(tok_rows, mode="drop")
    )
    return (buffer, slot_index)


def activate(gate_sum, up_sum):
    return (jax.nn.silu(gate_sum) * up_sum).astype(jnp.bfloat16)


def down_rows(second_weights, piece):
    return jnp.einsum("lrf,lfd->lrd", piece, second_weights, preferred_element_type=jnp.float32)


def routed_on_device(
    hidden_in,
    routes,
    route_gain,
    w_in,
    w_out,
    handoff,
    speaking,
    talker_routes,
    talker_gain,
    talker_w_in,
    talker_w_out,
):
    owners = lax.axis_size("expert")
    token_count, top_count = routes.shape
    local_experts = w_in.shape[0]
    experts = local_experts * owners
    capacity = max(2, token_count * top_count * 2 // experts)
    talker_capacity = max(2, capacity * 3 // 4)
    flat_ids = routes.reshape(-1)
    all_rows = jnp.ones_like(flat_ids)
    spread = jnp.repeat(hidden_in, top_count, axis=0)
    buffer, slot_index = place_rows(spread, flat_ids, all_rows, experts, capacity)
    arrived = lax.all_to_all(
        buffer.reshape(owners, local_experts, capacity, -1),
        "expert",
        split_axis=0,
        concat_axis=2,
        tiled=True,
    )
    partial_value = jnp.einsum("lrd,ldf->lrf", arrived[0], w_in, preferred_element_type=jnp.float32)
    hidden_width = w_in.shape[2] // 2
    share_sum = lax.psum_scatter(
        partial_value.astype(jnp.bfloat16), "replica", scatter_dimension=1, tiled=True
    ).astype(jnp.float32)
    hidden = activate(share_sum[:, :, :hidden_width], share_sum[:, :, hidden_width:])
    expert_out = down_rows(w_out, lax.all_gather(hidden, "replica", axis=1, tiled=True))
    returned = lax.all_to_all(
        expert_out.astype(jnp.bfloat16)[None], "expert", split_axis=2, concat_axis=0, tiled=True
    )
    returned = returned.reshape(experts * capacity, -1)
    picked = returned[slot_index].astype(jnp.float32).reshape(token_count, top_count, -1)
    thinker_out = jnp.sum(picked * route_gain[:, :, None], axis=1).astype(jnp.bfloat16)
    handoff_terms = jnp.dot(thinker_out, handoff, preferred_element_type=jnp.float32)
    talker_in = lax.psum_scatter(
        handoff_terms.astype(jnp.bfloat16), "replica", scatter_dimension=1, tiled=True
    )
    talker_ids = talker_routes.reshape(-1)
    speak_rows = jnp.repeat(speaking, top_count)
    talker_spread = jnp.repeat(talker_in, top_count, axis=0)
    talker_buffer, talker_slots = place_rows(
        talker_spread, talker_ids, speak_rows, experts, talker_capacity
    )
    talker_arrived = lax.all_to_all(
        talker_buffer.reshape(owners, local_experts, talker_capacity, -1),
        "expert",
        split_axis=0,
        concat_axis=2,
        tiled=True,
    )
    talker_partial = jnp.einsum(
        "lrd,ldf->lrf", talker_arrived[0], talker_w_in, preferred_element_type=jnp.float32
    )
    talker_hidden_width = talker_w_in.shape[2] // 2
    talker_share = lax.psum_scatter(
        talker_partial.astype(jnp.bfloat16), "replica", scatter_dimension=1, tiled=True
    ).astype(jnp.float32)
    talker_hidden = activate(
        talker_share[:, :, :talker_hidden_width], talker_share[:, :, talker_hidden_width:]
    )
    talker_expert_out = down_rows(
        talker_w_out, lax.all_gather(talker_hidden, "replica", axis=1, tiled=True)
    )
    talker_returned = lax.all_to_all(
        talker_expert_out.astype(jnp.bfloat16)[None],
        "expert",
        split_axis=2,
        concat_axis=0,
        tiled=True,
    )
    talker_returned = talker_returned.reshape(experts * talker_capacity, -1)
    safe_slots = jnp.minimum(talker_slots, experts * talker_capacity - 1)
    talker_picked = (
        talker_returned[safe_slots].astype(jnp.float32).reshape(token_count, top_count, -1)
    )
    talker_weights = talker_gain * speak_rows.reshape(token_count, top_count).astype(jnp.float32)
    talker_out = jnp.sum(talker_picked * talker_weights[:, :, None], axis=1).astype(jnp.bfloat16)
    return (thinker_out, talker_out)


def lanes_kernel(experts, where_ref, *refs):
    routes_ref, gain_ref, live_ref, talker_routes_ref, talker_gain_ref, out_ref, lanes = refs
    rows = out_ref.shape[0]
    stack = []
    live = live_ref[...].astype(jnp.float32)
    for ids, gains in ((routes_ref, gain_ref[...]), (talker_routes_ref, talker_gain_ref[...] * live)):
        expert = lax.broadcasted_iota(jnp.int32, (experts, ids.shape[1]), 0)
        dense = jnp.zeros(expert.shape, jnp.float32)
        for choice in range(ids.shape[0]):
            dense += jnp.where(
                ids[choice : choice + 1, :] == expert, gains[choice : choice + 1, :], 0.0
            )
        high = dense.astype(jnp.bfloat16).astype(jnp.float32)
        stack += [high, dense - high]
    stack.append(jnp.zeros((LANES - 4 * experts, live.shape[1]), jnp.float32))
    lanes[...] = jnp.concatenate(stack, axis=0).T
    first = pl.multiple_of(where_ref[2] * rows, rows)
    out_ref[...] = lanes[pl.ds(first, rows), :].astype(jnp.bfloat16)


def gain_lanes(where, experts, routes, gain, live, talker_routes, talker_gain):
    count = routes.shape[0]
    inputs = [routes.T, gain.T, live[None], talker_routes.T, talker_gain.T]
    return pl.pallas_call(
        functools.partial(lanes_kernel, experts),
        out_shape=jax.ShapeDtypeStruct((count // 2, LANES), jnp.bfloat16),
        in_specs=[pl.BlockSpec(memory_space=pltpu.SMEM)]
        + [pl.BlockSpec(memory_space=pltpu.VMEM)] * len(inputs),
        out_specs=pl.BlockSpec(memory_space=pltpu.VMEM),
        scratch_shapes=[pltpu.VMEM((count, LANES), jnp.float32)],
        compiler_params=pltpu.CompilerParams(vmem_limit_bytes=4 * 1024 * 1024),
        cost_estimate=pl.CostEstimate(
            flops=1 << 30, bytes_accessed=64 * count * LANES, transcendentals=0
        ),
    )(where, *inputs)


def row_kernel(where_ref, hidden_ref, other_ref, lanes_ref, out_ref):
    rows, width = other_ref.shape
    first = pl.multiple_of(where_ref[2] * rows, rows)
    out_ref[:, :width] = hidden_ref[pl.ds(first, rows), :]
    out_ref[:, width : 2 * width] = other_ref[...]
    out_ref[:, 2 * width :] = lanes_ref[...]


def build_row(where, hidden_in, other, lanes):
    rows, width = other.shape
    return pl.pallas_call(
        row_kernel,
        out_shape=jax.ShapeDtypeStruct((rows, 2 * width + LANES), jnp.bfloat16),
        in_specs=[pl.BlockSpec(memory_space=pltpu.SMEM)]
        + [pl.BlockSpec(memory_space=pltpu.VMEM)] * 3,
        out_specs=pl.BlockSpec(memory_space=pltpu.VMEM),
        compiler_params=pltpu.CompilerParams(vmem_limit_bytes=4 * 1024 * 1024),
        cost_estimate=pl.CostEstimate(flops=0, bytes_accessed=8 * rows * width, transcendentals=0),
    )(where, hidden_in, other, lanes)


def load(pairs, sems):
    copies = [
        pltpu.make_async_copy(source, destination, sems.at[index])
        for index, (source, destination) in enumerate(pairs)
    ]
    for copy in copies:
        copy.start()
    return copies


def chunk_pairs(chunks, place, first_row=0):
    pairs, row = [], first_row
    for chunk in chunks:
        pairs.append((chunk, place.at[pl.ds(row, chunk.shape[0])]))
        row += chunk.shape[0]
    return pairs


def hidden_kernel(blocks, gain_blocks, chunks, direct, first_lane, experts, where_ref, *refs):
    refs = list(refs)
    take = lambda count: [refs.pop(0) for _ in range(count)]
    row_refs, gain_refs = take(blocks), take(gain_blocks)
    (own_ref,) = take(1)
    chunk_refs = [take(chunks), take(chunks)]
    direct_refs = take(direct)
    out_ref, rows, gains, weights, sems = refs[-5:]
    width = own_ref.shape[1]
    half_hidden = own_ref.shape[2] // 2
    lane_refs = [ref.at[:, pl.ds(ref.shape[1] - LANES, LANES)] for ref in gain_refs or row_refs]
    row_refs = [ref.at[:, pl.ds(0, 2 * width)] for ref in row_refs]
    row_copies = load(chunk_pairs(row_refs, rows) + chunk_pairs(lane_refs, gains), sems.at[0])
    weight_copies = []
    for order in range(2):
        expert = (where_ref[1] + order) % 2
        parts = [own_ref.at[expert], *chunk_refs[order]]
        parts += [ref.at[expert] for ref in direct_refs]
        weight_copies.append(load(chunk_pairs(parts, weights.at[order]), sems.at[1 + order]))
    for copy in row_copies:
        copy.wait()
    lanes = gains[...].astype(jnp.float32)
    lane = lax.broadcasted_iota(jnp.int32, lanes.shape, 1) - first_lane
    for order in range(2):
        for copy in weight_copies[order]:
            copy.wait()
        offset = lane - (where_ref[0] * 2 + (where_ref[1] + order) % 2)
        gain = jnp.sum(
            jnp.where((offset == 0) | (offset == experts), lanes, 0.0), axis=1, keepdims=True
        )
        summed = jnp.dot(rows[...], weights[order], preferred_element_type=jnp.float32)
        hidden = jax.nn.silu(summed[:, :half_hidden]) * summed[:, half_hidden:] * gain
        out_ref[:, order * half_hidden : (order + 1) * half_hidden] = hidden.astype(jnp.bfloat16)


def run_hidden(where, row_blocks, gain_blocks, own, near, far, direct, before, first_lane, experts):
    blocks = len(row_blocks)
    count = sum(block.shape[0] for block in row_blocks)
    _, width, columns = own.shape
    inputs = [*row_blocks, *gain_blocks, own, *near, *far, *direct, *before]
    return pl.pallas_call(
        functools.partial(
            hidden_kernel, blocks, len(gain_blocks), len(near), len(direct), first_lane, experts
        ),
        out_shape=jax.ShapeDtypeStruct((count, columns), jnp.bfloat16),
        in_specs=[pl.BlockSpec(memory_space=pltpu.SMEM)]
        + [pl.BlockSpec(memory_space=pltpu.HBM)] * len(inputs),
        out_specs=pl.BlockSpec(memory_space=pltpu.VMEM),
        scratch_shapes=[
            pltpu.VMEM((count, 2 * width), jnp.bfloat16),
            pltpu.VMEM((count, LANES), jnp.bfloat16),
            pltpu.VMEM((2, 2 * width, columns), jnp.bfloat16),
            pltpu.SemaphoreType.DMA((3, max(2 * blocks, 2 + len(near)))),
        ],
        compiler_params=pltpu.CompilerParams(vmem_limit_bytes=20 * 1024 * 1024),
        cost_estimate=pl.CostEstimate(
            flops=8 * count * width * columns,
            bytes_accessed=4 * width * (count + 2 * columns),
            transcendentals=count * columns,
        ),
    )(where, *inputs)


def down_kernel(chunks, where_ref, hidden_ref, *refs):
    refs = list(refs)
    take = lambda count: [refs.pop(0) for _ in range(count)]
    chunk_refs = [take(chunks), take(chunks)]
    whole_refs = refs[:-4]
    mine_ref, away_ref, weights, sems = refs[-4:]
    depth = weights.shape[0] // 2
    pairs = []
    for order in range(2):
        expert = (where_ref[1] + order) % 2
        parts = chunk_refs[order] + [ref.at[expert] for ref in whole_refs]
        pairs += chunk_pairs(parts, weights, order * depth)
    for copy in load(pairs, sems):
        copy.wait()
    rows = mine_ref.shape[0]
    for half, out_ref in enumerate((mine_ref, away_ref)):
        out_ref[...] = jnp.dot(
            hidden_ref[half * rows : (half + 1) * rows, :],
            weights[...],
            preferred_element_type=jnp.float32,
        ).astype(jnp.bfloat16)


def run_down(where, hidden, near, far, whole):
    count, depth = hidden.shape
    inputs = [*near, *far, *whole]
    columns = inputs[0].shape[-1]
    shape = jax.ShapeDtypeStruct((count // 2, columns), jnp.bfloat16)
    return pl.pallas_call(
        functools.partial(down_kernel, len(near)),
        out_shape=(shape, shape),
        in_specs=[pl.BlockSpec(memory_space=pltpu.SMEM), pl.BlockSpec(memory_space=pltpu.VMEM)]
        + [pl.BlockSpec(memory_space=pltpu.HBM)] * len(inputs),
        out_specs=(pl.BlockSpec(memory_space=pltpu.VMEM),) * 2,
        scratch_shapes=[
            pltpu.VMEM((depth, columns), jnp.bfloat16),
            pltpu.SemaphoreType.DMA((2 * (len(near) + len(whole)),)),
        ],
        compiler_params=pltpu.CompilerParams(vmem_limit_bytes=16 * 1024 * 1024),
        cost_estimate=pl.CostEstimate(
            flops=2 * count * depth * columns,
            bytes_accessed=2 * (count * depth + depth * columns + count * columns),
            transcendentals=0,
        ),
    )(where, hidden, *inputs)


def over_replica(array):
    return lax.ppermute(array, "replica", SWAP)


def over_groups(array):
    return lax.ppermute(array, "groups", SWAP)


def over_expert(array, distance):
    return lax.ppermute(
        array, "expert", [(at, at ^ distance) for at in range(lax.axis_size("expert"))]
    )


def after(array, *others):
    return lax.optimization_barrier((array, *others))[0] if others else array


def send(weights, group, first_row, rows, *before):
    piece = lax.dynamic_slice(weights, (group, first_row, 0), (1, rows, weights.shape[2]))[0]
    return over_replica(after(piece, *before))


def over_both(array, distance):
    owners = lax.axis_size("expert")
    pairs = [
        (2 * at + replica, 2 * (at ^ distance) + 1 - replica)
        for at in range(owners)
        for replica in range(2)
    ]
    return lax.ppermute(array, ("expert", "replica"), pairs)


def spread_sums(mine, away, before=(), hold=(), cross=False):
    owners = lax.axis_size("expert")
    rows = mine.shape[0] // (owners // 2)
    other = over_expert(after(away, *hold), 1)
    terms = []
    for index in range(owners // 2):
        part = slice(index * rows, (index + 1) * rows)
        chip = mine[part].astype(jnp.float32) + other[part].astype(jnp.float32)
        if cross or index:
            chip = after(chip.astype(jnp.bfloat16), *before)
            chip = (over_both if cross else over_expert)(chip, 2 * index)
        terms.append(chip)
    return terms


def add_up(terms):
    return sum(term.astype(jnp.float32) for term in terms).astype(jnp.bfloat16)


def in_order(replica, own, other, axis):
    return jnp.concatenate(
        [jnp.where(replica == 0, own, other), jnp.where(replica == 0, other, own)], axis=axis
    )


def dense_on_device(
    hidden_in,
    routes,
    route_gain,
    w_in,
    w_out,
    handoff,
    speaking,
    talker_routes,
    talker_gain,
    talker_w_in,
    talker_w_out,
):
    replica, group = lax.axis_index("replica"), lax.axis_index("groups")
    where = jnp.stack([lax.axis_index("expert"), group, replica]).astype(jnp.int32)
    owners = lax.axis_size("expert")
    experts = w_in.shape[0] * owners
    rows = routes.shape[0] // 2
    distances = range(2, owners, 2)

    width, chunk, out_chunk = w_in.shape[1], w_in.shape[1] * 11 // 32, w_out.shape[1] * 2 // 3

    lanes = gain_lanes(
        where, experts, routes, route_gain, speaking, talker_routes, talker_gain
    )
    give = lax.dynamic_slice_in_dim(hidden_in, (1 - replica) * rows, rows, 0)
    other = over_replica(give)
    near_in = [
        send(w_in, group, first, min(chunk, width - first), other)
        for first in range(0, width, chunk)
    ]
    row = build_row(where, hidden_in, other, lanes)
    same = [row] + [over_expert(row, distance) for distance in distances]
    far_in = [over_groups(after(near_in[0], same[2]))]
    for part in near_in[1:]:
        far_in.append(over_groups(after(part, far_in[-1])))
    across = [over_expert(row, 1), over_expert(jnp.concatenate(same[1:]), 1)]
    near_out = send(w_out, group, 0, out_chunk, near_in[1])
    direct_out = over_replica(after(w_out[:, out_chunk:], near_out))
    far_out = over_groups(near_out)
    blocks = same + across
    hidden = run_hidden(where, blocks, [], w_in, near_in, far_in, [], [near_out], 0, experts)
    own = run_down(where, hidden, [], [], [w_out])
    own = spread_sums(*own, hold=[direct_out, far_out])
    near_talker_in = send(talker_w_in, group, 0, talker_w_in.shape[1], near_out, hidden)
    give = run_down(where, hidden, [near_out], [far_out], [direct_out])
    got = spread_sums(*give, before=[own[2], near_talker_in], cross=True)
    far_talker_in = over_groups(near_talker_in)
    got, own = add_up(got), add_up(own)
    thinker_out = in_order(replica, own, got, 0)

    def handed(array):
        return jnp.dot(array, handoff, preferred_element_type=jnp.float32)

    term = over_replica(handed(got).astype(jnp.bfloat16))
    direct_talker_out = over_replica(after(talker_w_out, term))
    talker_row = (handed(own) + term.astype(jnp.float32)).astype(jnp.bfloat16)
    parts = jnp.split(talker_row, 2, axis=1)
    talker_row = in_order(replica, parts[0], parts[1], 1)
    same = [talker_row] + [over_expert(talker_row, distance) for distance in distances]
    rest = after(jnp.concatenate(same[1:]), far_talker_in)
    talker_blocks = same + [over_expert(talker_row, 1), over_expert(rest, 1)]
    hidden = run_hidden(
        where,
        talker_blocks,
        blocks,
        talker_w_in,
        [near_talker_in],
        [far_talker_in],
        [],
        [direct_talker_out],
        2 * experts,
        experts,
    )
    give = run_down(where, hidden, [], [], [direct_talker_out])
    got = add_up(spread_sums(*give, cross=True))
    own = run_down(where, after(hidden, *give), [], [], [talker_w_out])
    own = add_up(spread_sums(*own))
    return (thinker_out, in_order(replica, own, got, 0))


def on_device(*arrays):
    token_count, top_count = arrays[1].shape
    local_experts = arrays[3].shape[0]
    experts = local_experts * lax.axis_size("expert")
    dense = (
        token_count * top_count * 2 // experts >= token_count
        and 4 * experts <= LANES
        and lax.axis_size("replica") == lax.axis_size("groups") == local_experts == 2
        and lax.axis_size("expert") in (2, 4, 8, 16)
    )
    return (dense_on_device if dense else routed_on_device)(*arrays)


def solution(mesh):
    return jax.shard_map(
        on_device,
        mesh=mesh,
        in_specs=(
            P(("groups", "expert"), "replica"),
            P(("groups", "expert"), None),
            P(("groups", "expert"), None),
            P("expert", "replica", None),
            P("expert", None, "replica"),
            P("replica", None),
            P(("groups", "expert")),
            P(("groups", "expert"), None),
            P(("groups", "expert"), None),
            P("expert", "replica", None),
            P("expert", None, "replica"),
        ),
        out_specs=(P(("groups", "expert"), "replica"), P(("groups", "expert"), "replica")),
        check_vma=False,
    )
```

```python
import functools

import jax
import jax.numpy as jnp
from jax import lax
from jax.experimental import pallas as pl
from jax.experimental.pallas import tpu as pltpu
from jax.sharding import PartitionSpec as P

LANES = 128
SWAP = [(0, 1), (1, 0)]


def place_rows(tok_rows, flat_ids, live_rows, experts, capacity):
    onehot = (flat_ids[:, None] == lax.iota(jnp.int32, experts)[None, :]).astype(
        jnp.int32
    ) * live_rows[:, None]
    before = jnp.cumsum(onehot, axis=0) - onehot
    slot_rank = jnp.sum(before * onehot, axis=1)
    slot_index = jnp.where(live_rows > 0, flat_ids * capacity + slot_rank, experts * capacity)
    buffer = (
        jnp.zeros((experts * capacity, tok_rows.shape[1]), tok_rows.dtype)
        .at[slot_index]
        .set(tok_rows, mode="drop")
    )
    return (buffer, slot_index)


def activate(gate_sum, up_sum):
    return (jax.nn.silu(gate_sum) * up_sum).astype(jnp.bfloat16)


def down_rows(second_weights, piece):
    return jnp.einsum("lrf,lfd->lrd", piece, second_weights, preferred_element_type=jnp.float32)


def routed_on_device(
    hidden_in,
    routes,
    route_gain,
    w_in,
    w_out,
    handoff,
    speaking,
    talker_routes,
    talker_gain,
    talker_w_in,
    talker_w_out,
):
    owners = lax.axis_size("expert")
    token_count, top_count = routes.shape
    local_experts = w_in.shape[0]
    experts = local_experts * owners
    capacity = max(2, token_count * top_count * 2 // experts)
    talker_capacity = max(2, capacity * 3 // 4)
    flat_ids = routes.reshape(-1)
    all_rows = jnp.ones_like(flat_ids)
    spread = jnp.repeat(hidden_in, top_count, axis=0)
    buffer, slot_index = place_rows(spread, flat_ids, all_rows, experts, capacity)
    arrived = lax.all_to_all(
        buffer.reshape(owners, local_experts, capacity, -1),
        "expert",
        split_axis=0,
        concat_axis=2,
        tiled=True,
    )
    partial_value = jnp.einsum("lrd,ldf->lrf", arrived[0], w_in, preferred_element_type=jnp.float32)
    hidden_width = w_in.shape[2] // 2
    share_sum = lax.psum_scatter(
        partial_value.astype(jnp.bfloat16), "replica", scatter_dimension=1, tiled=True
    ).astype(jnp.float32)
    hidden = activate(share_sum[:, :, :hidden_width], share_sum[:, :, hidden_width:])
    expert_out = down_rows(w_out, lax.all_gather(hidden, "replica", axis=1, tiled=True))
    returned = lax.all_to_all(
        expert_out.astype(jnp.bfloat16)[None], "expert", split_axis=2, concat_axis=0, tiled=True
    )
    returned = returned.reshape(experts * capacity, -1)
    picked = returned[slot_index].astype(jnp.float32).reshape(token_count, top_count, -1)
    thinker_out = jnp.sum(picked * route_gain[:, :, None], axis=1).astype(jnp.bfloat16)
    handoff_terms = jnp.dot(thinker_out, handoff, preferred_element_type=jnp.float32)
    talker_in = lax.psum_scatter(
        handoff_terms.astype(jnp.bfloat16), "replica", scatter_dimension=1, tiled=True
    )
    talker_ids = talker_routes.reshape(-1)
    speak_rows = jnp.repeat(speaking, top_count)
    talker_spread = jnp.repeat(talker_in, top_count, axis=0)
    talker_buffer, talker_slots = place_rows(
        talker_spread, talker_ids, speak_rows, experts, talker_capacity
    )
    talker_arrived = lax.all_to_all(
        talker_buffer.reshape(owners, local_experts, talker_capacity, -1),
        "expert",
        split_axis=0,
        concat_axis=2,
        tiled=True,
    )
    talker_partial = jnp.einsum(
        "lrd,ldf->lrf", talker_arrived[0], talker_w_in, preferred_element_type=jnp.float32
    )
    talker_hidden_width = talker_w_in.shape[2] // 2
    talker_share = lax.psum_scatter(
        talker_partial.astype(jnp.bfloat16), "replica", scatter_dimension=1, tiled=True
    ).astype(jnp.float32)
    talker_hidden = activate(
        talker_share[:, :, :talker_hidden_width], talker_share[:, :, talker_hidden_width:]
    )
    talker_expert_out = down_rows(
        talker_w_out, lax.all_gather(talker_hidden, "replica", axis=1, tiled=True)
    )
    talker_returned = lax.all_to_all(
        talker_expert_out.astype(jnp.bfloat16)[None],
        "expert",
        split_axis=2,
        concat_axis=0,
        tiled=True,
    )
    talker_returned = talker_returned.reshape(experts * talker_capacity, -1)
    safe_slots = jnp.minimum(talker_slots, experts * talker_capacity - 1)
    talker_picked = (
        talker_returned[safe_slots].astype(jnp.float32).reshape(token_count, top_count, -1)
    )
    talker_weights = talker_gain * speak_rows.reshape(token_count, top_count).astype(jnp.float32)
    talker_out = jnp.sum(talker_picked * talker_weights[:, :, None], axis=1).astype(jnp.bfloat16)
    return (thinker_out, talker_out)


def lanes_kernel(experts, where_ref, *refs):
    routes_ref, gain_ref, live_ref, talker_routes_ref, talker_gain_ref, out_ref, lanes = refs
    rows = out_ref.shape[0]
    stack = []
    live = live_ref[...].astype(jnp.float32)
    for ids, gains in ((routes_ref, gain_ref[...]), (talker_routes_ref, talker_gain_ref[...] * live)):
        expert = lax.broadcasted_iota(jnp.int32, (experts, ids.shape[1]), 0)
        dense = jnp.zeros(expert.shape, jnp.float32)
        for choice in range(ids.shape[0]):
            dense += jnp.where(
                ids[choice : choice + 1, :] == expert, gains[choice : choice + 1, :], 0.0
            )
        high = dense.astype(jnp.bfloat16).astype(jnp.float32)
        stack += [high, dense - high]
    stack.append(jnp.zeros((LANES - 4 * experts, live.shape[1]), jnp.float32))
    lanes[...] = jnp.concatenate(stack, axis=0).T
    first = pl.multiple_of(where_ref[2] * rows, rows)
    out_ref[...] = lanes[pl.ds(first, rows), :].astype(jnp.bfloat16)


def gain_lanes(where, experts, routes, gain, live, talker_routes, talker_gain):
    count = routes.shape[0]
    inputs = [routes.T, gain.T, live[None], talker_routes.T, talker_gain.T]
    return pl.pallas_call(
        functools.partial(lanes_kernel, experts),
        out_shape=jax.ShapeDtypeStruct((count // 2, LANES), jnp.bfloat16),
        in_specs=[pl.BlockSpec(memory_space=pltpu.SMEM)]
        + [pl.BlockSpec(memory_space=pltpu.VMEM)] * len(inputs),
        out_specs=pl.BlockSpec(memory_space=pltpu.VMEM),
        scratch_shapes=[pltpu.VMEM((count, LANES), jnp.float32)],
        compiler_params=pltpu.CompilerParams(vmem_limit_bytes=4 * 1024 * 1024),
        cost_estimate=pl.CostEstimate(
            flops=1 << 30, bytes_accessed=64 * count * LANES, transcendentals=0
        ),
    )(where, *inputs)


def row_kernel(where_ref, hidden_ref, other_ref, lanes_ref, out_ref):
    rows, width = other_ref.shape
    first = pl.multiple_of(where_ref[2] * rows, rows)
    out_ref[:, :width] = hidden_ref[pl.ds(first, rows), :]
    out_ref[:, width : 2 * width] = other_ref[...]
    out_ref[:, 2 * width :] = lanes_ref[...]


def build_row(where, hidden_in, other, lanes):
    rows, width = other.shape
    return pl.pallas_call(
        row_kernel,
        out_shape=jax.ShapeDtypeStruct((rows, 2 * width + LANES), jnp.bfloat16),
        in_specs=[pl.BlockSpec(memory_space=pltpu.SMEM)]
        + [pl.BlockSpec(memory_space=pltpu.VMEM)] * 3,
        out_specs=pl.BlockSpec(memory_space=pltpu.VMEM),
        compiler_params=pltpu.CompilerParams(vmem_limit_bytes=4 * 1024 * 1024),
        cost_estimate=pl.CostEstimate(flops=0, bytes_accessed=8 * rows * width, transcendentals=0),
    )(where, hidden_in, other, lanes)


def load(pairs, sems):
    copies = [
        pltpu.make_async_copy(source, destination, sems.at[index])
        for index, (source, destination) in enumerate(pairs)
    ]
    for copy in copies:
        copy.start()
    return copies


def chunk_pairs(chunks, place, first_row=0):
    pairs, row = [], first_row
    for chunk in chunks:
        pairs.append((chunk, place.at[pl.ds(row, chunk.shape[0])]))
        row += chunk.shape[0]
    return pairs


def hidden_kernel(blocks, gain_blocks, chunks, direct, first_lane, experts, where_ref, *refs):
    refs = list(refs)
    take = lambda count: [refs.pop(0) for _ in range(count)]
    row_refs, gain_refs = take(blocks), take(gain_blocks)
    (own_ref,) = take(1)
    chunk_refs = [take(chunks), take(chunks)]
    direct_refs = take(direct)
    out_ref, rows, gains, weights, sems = refs[-5:]
    width = own_ref.shape[1]
    half_hidden = own_ref.shape[2] // 2
    lane_refs = [ref.at[:, pl.ds(ref.shape[1] - LANES, LANES)] for ref in gain_refs or row_refs]
    row_refs = [ref.at[:, pl.ds(0, 2 * width)] for ref in row_refs]
    row_copies = load(chunk_pairs(row_refs, rows) + chunk_pairs(lane_refs, gains), sems.at[0])
    weight_copies = []
    for order in range(2):
        expert = (where_ref[1] + order) % 2
        parts = [own_ref.at[expert], *chunk_refs[order]]
        parts += [ref.at[expert] for ref in direct_refs]
        weight_copies.append(load(chunk_pairs(parts, weights.at[order]), sems.at[1 + order]))
    for copy in row_copies:
        copy.wait()
    lanes = gains[...].astype(jnp.float32)
    lane = lax.broadcasted_iota(jnp.int32, lanes.shape, 1) - first_lane
    for order in range(2):
        for copy in weight_copies[order]:
            copy.wait()
        offset = lane - (where_ref[0] * 2 + (where_ref[1] + order) % 2)
        gain = jnp.sum(
            jnp.where((offset == 0) | (offset == experts), lanes, 0.0), axis=1, keepdims=True
        )
        summed = jnp.dot(rows[...], weights[order], preferred_element_type=jnp.float32)
        hidden = jax.nn.silu(summed[:, :half_hidden]) * summed[:, half_hidden:] * gain
        out_ref[:, order * half_hidden : (order + 1) * half_hidden] = hidden.astype(jnp.bfloat16)


def run_hidden(where, row_blocks, gain_blocks, own, near, far, direct, before, first_lane, experts):
    blocks = len(row_blocks)
    count = sum(block.shape[0] for block in row_blocks)
    _, width, columns = own.shape
    inputs = [*row_blocks, *gain_blocks, own, *near, *far, *direct, *before]
    return pl.pallas_call(
        functools.partial(
            hidden_kernel, blocks, len(gain_blocks), len(near), len(direct), first_lane, experts
        ),
        out_shape=jax.ShapeDtypeStruct((count, columns), jnp.bfloat16),
        in_specs=[pl.BlockSpec(memory_space=pltpu.SMEM)]
        + [pl.BlockSpec(memory_space=pltpu.HBM)] * len(inputs),
        out_specs=pl.BlockSpec(memory_space=pltpu.VMEM),
        scratch_shapes=[
            pltpu.VMEM((count, 2 * width), jnp.bfloat16),
            pltpu.VMEM((count, LANES), jnp.bfloat16),
            pltpu.VMEM((2, 2 * width, columns), jnp.bfloat16),
            pltpu.SemaphoreType.DMA((3, max(2 * blocks, 2 + len(near)))),
        ],
        compiler_params=pltpu.CompilerParams(vmem_limit_bytes=20 * 1024 * 1024),
        cost_estimate=pl.CostEstimate(
            flops=8 * count * width * columns,
            bytes_accessed=4 * width * (count + 2 * columns),
            transcendentals=count * columns,
        ),
    )(where, *inputs)


def down_kernel(chunks, where_ref, hidden_ref, *refs):
    refs = list(refs)
    take = lambda count: [refs.pop(0) for _ in range(count)]
    chunk_refs = [take(chunks), take(chunks)]
    whole_refs = refs[:-4]
    mine_ref, away_ref, weights, sems = refs[-4:]
    depth = weights.shape[0] // 2
    pairs = []
    for order in range(2):
        expert = (where_ref[1] + order) % 2
        parts = chunk_refs[order] + [ref.at[expert] for ref in whole_refs]
        pairs += chunk_pairs(parts, weights, order * depth)
    for copy in load(pairs, sems):
        copy.wait()
    rows = mine_ref.shape[0]
    for half, out_ref in enumerate((mine_ref, away_ref)):
        out_ref[...] = jnp.dot(
            hidden_ref[half * rows : (half + 1) * rows, :],
            weights[...],
            preferred_element_type=jnp.float32,
        ).astype(jnp.bfloat16)


def run_down(where, hidden, near, far, whole):
    count, depth = hidden.shape
    inputs = [*near, *far, *whole]
    columns = inputs[0].shape[-1]
    shape = jax.ShapeDtypeStruct((count // 2, columns), jnp.bfloat16)
    return pl.pallas_call(
        functools.partial(down_kernel, len(near)),
        out_shape=(shape, shape),
        in_specs=[pl.BlockSpec(memory_space=pltpu.SMEM), pl.BlockSpec(memory_space=pltpu.VMEM)]
        + [pl.BlockSpec(memory_space=pltpu.HBM)] * len(inputs),
        out_specs=(pl.BlockSpec(memory_space=pltpu.VMEM),) * 2,
        scratch_shapes=[
            pltpu.VMEM((depth, columns), jnp.bfloat16),
            pltpu.SemaphoreType.DMA((2 * (len(near) + len(whole)),)),
        ],
        compiler_params=pltpu.CompilerParams(vmem_limit_bytes=16 * 1024 * 1024),
        cost_estimate=pl.CostEstimate(
            flops=2 * count * depth * columns,
            bytes_accessed=2 * (count * depth + depth * columns + count * columns),
            transcendentals=0,
        ),
    )(where, hidden, *inputs)


def over_replica(array):
    return lax.ppermute(array, "replica", SWAP)


def over_groups(array):
    return lax.ppermute(array, "groups", SWAP)


def over_expert(array, distance):
    return lax.ppermute(
        array, "expert", [(at, at ^ distance) for at in range(lax.axis_size("expert"))]
    )


def after(array, *others):
    return lax.optimization_barrier((array, *others))[0] if others else array


def send(weights, group, first_row, rows, *before):
    piece = lax.dynamic_slice(weights, (group, first_row, 0), (1, rows, weights.shape[2]))[0]
    return over_replica(after(piece, *before))


def over_both(array, distance):
    owners = lax.axis_size("expert")
    pairs = [
        (2 * at + replica, 2 * (at ^ distance) + 1 - replica)
        for at in range(owners)
        for replica in range(2)
    ]
    return lax.ppermute(array, ("expert", "replica"), pairs)


def spread_sums(mine, away, before=(), hold=(), cross=False):
    owners = lax.axis_size("expert")
    rows = mine.shape[0] // (owners // 2)
    other = over_expert(after(away, *hold), 1)
    terms = []
    for index in range(owners // 2):
        part = slice(index * rows, (index + 1) * rows)
        chip = mine[part].astype(jnp.float32) + other[part].astype(jnp.float32)
        if cross or index:
            chip = after(chip.astype(jnp.bfloat16), *before)
            chip = (over_both if cross else over_expert)(chip, 2 * index)
        terms.append(chip)
    return terms


def add_up(terms):
    return sum(term.astype(jnp.float32) for term in terms).astype(jnp.bfloat16)


def in_order(replica, own, other, axis):
    return jnp.concatenate(
        [jnp.where(replica == 0, own, other), jnp.where(replica == 0, other, own)], axis=axis
    )


def dense_on_device(
    hidden_in,
    routes,
    route_gain,
    w_in,
    w_out,
    handoff,
    speaking,
    talker_routes,
    talker_gain,
    talker_w_in,
    talker_w_out,
):
    replica, group = lax.axis_index("replica"), lax.axis_index("groups")
    where = jnp.stack([lax.axis_index("expert"), group, replica]).astype(jnp.int32)
    owners = lax.axis_size("expert")
    experts = w_in.shape[0] * owners
    rows = routes.shape[0] // 2
    distances = range(2, owners, 2)

    chunk = w_in.shape[1] * 13 // 32

    lanes = gain_lanes(
        where, experts, routes, route_gain, speaking, talker_routes, talker_gain
    )
    give = lax.dynamic_slice_in_dim(hidden_in, (1 - replica) * rows, rows, 0)
    other = over_replica(give)
    near_in = [send(w_in, group, index * chunk, chunk, other) for index in range(2)]
    row = build_row(where, hidden_in, other, lanes)
    same = [row] + [over_expert(row, distance) for distance in distances]
    far_in = [over_groups(after(near_in[0], same[2]))]
    far_in.append(over_groups(near_in[1]))
    direct_in = over_replica(after(w_in[:, 2 * chunk :], near_in[0]))
    across = [over_expert(after(row, far_in[0]), 1), over_expert(jnp.concatenate(same[1:]), 1)]
    blocks = same + across
    hidden = run_hidden(where, blocks, [], w_in, near_in, far_in, [direct_in], [], 0, experts)
    half = talker_w_in.shape[1] // 2
    near_talker_in = [send(talker_w_in, group, 0, half, direct_in)]
    far_talker_in = [over_groups(near_talker_in[0])]
    other_hidden = over_replica(after(hidden, near_talker_in[0]))
    own = spread_sums(*run_down(where, hidden, [], [], [w_out]))
    got = run_down(where, after(other_hidden, own[2]), [], [], [w_out])
    near_talker_in.append(send(talker_w_in, group, half, half, own[3], *got))
    got = spread_sums(*got, before=[own[1]])
    far_talker_in.append(over_groups(after(near_talker_in[1], far_talker_in[0])))
    got, own = add_up(got), add_up(own)
    thinker_out = in_order(replica, own, got, 0)

    def handed(array):
        return jnp.dot(array, handoff, preferred_element_type=jnp.float32)

    term = over_replica(handed(got).astype(jnp.bfloat16))
    direct_talker_out = over_replica(after(talker_w_out, term))
    talker_row = (handed(own) + term.astype(jnp.float32)).astype(jnp.bfloat16)
    parts = jnp.split(talker_row, 2, axis=1)
    talker_row = in_order(replica, parts[0], parts[1], 1)
    same = [talker_row] + [over_expert(talker_row, distance) for distance in distances]
    rest = after(jnp.concatenate(same[1:]), far_talker_in[1])
    talker_blocks = same + [over_expert(talker_row, 1), over_expert(rest, 1)]
    hidden = run_hidden(
        where,
        talker_blocks,
        blocks,
        talker_w_in,
        near_talker_in,
        far_talker_in,
        [],
        [direct_talker_out],
        2 * experts,
        experts,
    )
    give = run_down(where, hidden, [], [], [direct_talker_out])
    got = add_up(spread_sums(*give, cross=True))
    own = run_down(where, after(hidden, *give), [], [], [talker_w_out])
    own = add_up(spread_sums(*own))
    return (thinker_out, in_order(replica, own, got, 0))


def on_device(*arrays):
    token_count, top_count = arrays[1].shape
    local_experts = arrays[3].shape[0]
    experts = local_experts * lax.axis_size("expert")
    dense = (
        token_count * top_count * 2 // experts >= token_count
        and 4 * experts <= LANES
        and lax.axis_size("replica") == lax.axis_size("groups") == local_experts == 2
        and lax.axis_size("expert") in (2, 4, 8, 16)
    )
    return (dense_on_device if dense else routed_on_device)(*arrays)


def solution(mesh):
    return jax.shard_map(
        on_device,
        mesh=mesh,
        in_specs=(
            P(("groups", "expert"), "replica"),
            P(("groups", "expert"), None),
            P(("groups", "expert"), None),
            P("expert", "replica", None),
            P("expert", None, "replica"),
            P("replica", None),
            P(("groups", "expert")),
            P(("groups", "expert"), None),
            P(("groups", "expert"), None),
            P("expert", "replica", None),
            P("expert", None, "replica"),
        ),
        out_specs=(P(("groups", "expert"), "replica"), P(("groups", "expert"), "replica")),
        check_vma=False,
    )
```

```python
import functools

import jax
import jax.numpy as jnp
from jax import lax
from jax.experimental import pallas as pl
from jax.experimental.pallas import tpu as pltpu
from jax.sharding import PartitionSpec as P

LANES = 128
SWAP = [(0, 1), (1, 0)]


def place_rows(tok_rows, flat_ids, live_rows, experts, capacity):
    onehot = (flat_ids[:, None] == lax.iota(jnp.int32, experts)[None, :]).astype(
        jnp.int32
    ) * live_rows[:, None]
    before = jnp.cumsum(onehot, axis=0) - onehot
    slot_rank = jnp.sum(before * onehot, axis=1)
    slot_index = jnp.where(live_rows > 0, flat_ids * capacity + slot_rank, experts * capacity)
    buffer = (
        jnp.zeros((experts * capacity, tok_rows.shape[1]), tok_rows.dtype)
        .at[slot_index]
        .set(tok_rows, mode="drop")
    )
    return (buffer, slot_index)


def activate(gate_sum, up_sum):
    return (jax.nn.silu(gate_sum) * up_sum).astype(jnp.bfloat16)


def down_rows(second_weights, piece):
    return jnp.einsum("lrf,lfd->lrd", piece, second_weights, preferred_element_type=jnp.float32)


def routed_on_device(
    hidden_in,
    routes,
    route_gain,
    w_in,
    w_out,
    handoff,
    speaking,
    talker_routes,
    talker_gain,
    talker_w_in,
    talker_w_out,
):
    owners = lax.axis_size("expert")
    token_count, top_count = routes.shape
    local_experts = w_in.shape[0]
    experts = local_experts * owners
    capacity = max(2, token_count * top_count * 2 // experts)
    talker_capacity = max(2, capacity * 3 // 4)
    flat_ids = routes.reshape(-1)
    all_rows = jnp.ones_like(flat_ids)
    spread = jnp.repeat(hidden_in, top_count, axis=0)
    buffer, slot_index = place_rows(spread, flat_ids, all_rows, experts, capacity)
    arrived = lax.all_to_all(
        buffer.reshape(owners, local_experts, capacity, -1),
        "expert",
        split_axis=0,
        concat_axis=2,
        tiled=True,
    )
    partial_value = jnp.einsum("lrd,ldf->lrf", arrived[0], w_in, preferred_element_type=jnp.float32)
    hidden_width = w_in.shape[2] // 2
    share_sum = lax.psum_scatter(
        partial_value.astype(jnp.bfloat16), "replica", scatter_dimension=1, tiled=True
    ).astype(jnp.float32)
    hidden = activate(share_sum[:, :, :hidden_width], share_sum[:, :, hidden_width:])
    expert_out = down_rows(w_out, lax.all_gather(hidden, "replica", axis=1, tiled=True))
    returned = lax.all_to_all(
        expert_out.astype(jnp.bfloat16)[None], "expert", split_axis=2, concat_axis=0, tiled=True
    )
    returned = returned.reshape(experts * capacity, -1)
    picked = returned[slot_index].astype(jnp.float32).reshape(token_count, top_count, -1)
    thinker_out = jnp.sum(picked * route_gain[:, :, None], axis=1).astype(jnp.bfloat16)
    handoff_terms = jnp.dot(thinker_out, handoff, preferred_element_type=jnp.float32)
    talker_in = lax.psum_scatter(
        handoff_terms.astype(jnp.bfloat16), "replica", scatter_dimension=1, tiled=True
    )
    talker_ids = talker_routes.reshape(-1)
    speak_rows = jnp.repeat(speaking, top_count)
    talker_spread = jnp.repeat(talker_in, top_count, axis=0)
    talker_buffer, talker_slots = place_rows(
        talker_spread, talker_ids, speak_rows, experts, talker_capacity
    )
    talker_arrived = lax.all_to_all(
        talker_buffer.reshape(owners, local_experts, talker_capacity, -1),
        "expert",
        split_axis=0,
        concat_axis=2,
        tiled=True,
    )
    talker_partial = jnp.einsum(
        "lrd,ldf->lrf", talker_arrived[0], talker_w_in, preferred_element_type=jnp.float32
    )
    talker_hidden_width = talker_w_in.shape[2] // 2
    talker_share = lax.psum_scatter(
        talker_partial.astype(jnp.bfloat16), "replica", scatter_dimension=1, tiled=True
    ).astype(jnp.float32)
    talker_hidden = activate(
        talker_share[:, :, :talker_hidden_width], talker_share[:, :, talker_hidden_width:]
    )
    talker_expert_out = down_rows(
        talker_w_out, lax.all_gather(talker_hidden, "replica", axis=1, tiled=True)
    )
    talker_returned = lax.all_to_all(
        talker_expert_out.astype(jnp.bfloat16)[None],
        "expert",
        split_axis=2,
        concat_axis=0,
        tiled=True,
    )
    talker_returned = talker_returned.reshape(experts * talker_capacity, -1)
    safe_slots = jnp.minimum(talker_slots, experts * talker_capacity - 1)
    talker_picked = (
        talker_returned[safe_slots].astype(jnp.float32).reshape(token_count, top_count, -1)
    )
    talker_weights = talker_gain * speak_rows.reshape(token_count, top_count).astype(jnp.float32)
    talker_out = jnp.sum(talker_picked * talker_weights[:, :, None], axis=1).astype(jnp.bfloat16)
    return (thinker_out, talker_out)


def lanes_kernel(experts, where_ref, *refs):
    routes_ref, gain_ref, live_ref, talker_routes_ref, talker_gain_ref, out_ref, lanes = refs
    rows = out_ref.shape[0]
    stack = []
    live = live_ref[...].astype(jnp.float32)
    for ids, gains in ((routes_ref, gain_ref[...]), (talker_routes_ref, talker_gain_ref[...] * live)):
        expert = lax.broadcasted_iota(jnp.int32, (experts, ids.shape[1]), 0)
        dense = jnp.zeros(expert.shape, jnp.float32)
        for choice in range(ids.shape[0]):
            dense += jnp.where(
                ids[choice : choice + 1, :] == expert, gains[choice : choice + 1, :], 0.0
            )
        high = dense.astype(jnp.bfloat16).astype(jnp.float32)
        stack += [high, dense - high]
    stack.append(jnp.zeros((LANES - 4 * experts, live.shape[1]), jnp.float32))
    lanes[...] = jnp.concatenate(stack, axis=0).T
    first = pl.multiple_of(where_ref[2] * rows, rows)
    out_ref[...] = lanes[pl.ds(first, rows), :].astype(jnp.bfloat16)


def gain_lanes(where, experts, routes, gain, live, talker_routes, talker_gain):
    count = routes.shape[0]
    inputs = [routes.T, gain.T, live[None], talker_routes.T, talker_gain.T]
    return pl.pallas_call(
        functools.partial(lanes_kernel, experts),
        out_shape=jax.ShapeDtypeStruct((count // 2, LANES), jnp.bfloat16),
        in_specs=[pl.BlockSpec(memory_space=pltpu.SMEM)]
        + [pl.BlockSpec(memory_space=pltpu.VMEM)] * len(inputs),
        out_specs=pl.BlockSpec(memory_space=pltpu.VMEM),
        scratch_shapes=[pltpu.VMEM((count, LANES), jnp.float32)],
        compiler_params=pltpu.CompilerParams(vmem_limit_bytes=4 * 1024 * 1024),
        cost_estimate=pl.CostEstimate(
            flops=1 << 30, bytes_accessed=64 * count * LANES, transcendentals=0
        ),
    )(where, *inputs)


def row_kernel(where_ref, hidden_ref, other_ref, lanes_ref, out_ref):
    rows, width = other_ref.shape
    first = pl.multiple_of(where_ref[2] * rows, rows)
    out_ref[:, :width] = hidden_ref[pl.ds(first, rows), :]
    out_ref[:, width : 2 * width] = other_ref[...]
    out_ref[:, 2 * width :] = lanes_ref[...]


def build_row(where, hidden_in, other, lanes):
    rows, width = other.shape
    return pl.pallas_call(
        row_kernel,
        out_shape=jax.ShapeDtypeStruct((rows, 2 * width + LANES), jnp.bfloat16),
        in_specs=[pl.BlockSpec(memory_space=pltpu.SMEM)]
        + [pl.BlockSpec(memory_space=pltpu.VMEM)] * 3,
        out_specs=pl.BlockSpec(memory_space=pltpu.VMEM),
        compiler_params=pltpu.CompilerParams(vmem_limit_bytes=4 * 1024 * 1024),
        cost_estimate=pl.CostEstimate(flops=0, bytes_accessed=8 * rows * width, transcendentals=0),
    )(where, hidden_in, other, lanes)


def load(pairs, sems):
    copies = [
        pltpu.make_async_copy(source, destination, sems.at[index])
        for index, (source, destination) in enumerate(pairs)
    ]
    for copy in copies:
        copy.start()
    return copies


def chunk_pairs(chunks, place, first_row=0):
    pairs, row = [], first_row
    for chunk in chunks:
        pairs.append((chunk, place.at[pl.ds(row, chunk.shape[0])]))
        row += chunk.shape[0]
    return pairs


def hidden_kernel(blocks, gain_blocks, chunks, direct, first_lane, experts, where_ref, *refs):
    refs = list(refs)
    take = lambda count: [refs.pop(0) for _ in range(count)]
    row_refs, gain_refs = take(blocks), take(gain_blocks)
    (own_ref,) = take(1)
    chunk_refs = [take(chunks), take(chunks)]
    direct_refs = take(direct)
    out_ref, rows, gains, weights, sems = refs[-5:]
    width = own_ref.shape[1]
    half_hidden = own_ref.shape[2] // 2
    lane_refs = [ref.at[:, pl.ds(ref.shape[1] - LANES, LANES)] for ref in gain_refs or row_refs]
    row_refs = [ref.at[:, pl.ds(0, 2 * width)] for ref in row_refs]
    row_copies = load(chunk_pairs(row_refs, rows) + chunk_pairs(lane_refs, gains), sems.at[0])
    weight_copies = []
    for order in range(2):
        expert = (where_ref[1] + order) % 2
        parts = [own_ref.at[expert], *chunk_refs[order]]
        parts += [ref.at[expert] for ref in direct_refs]
        weight_copies.append(load(chunk_pairs(parts, weights.at[order]), sems.at[1 + order]))
    for copy in row_copies:
        copy.wait()
    lanes = gains[...].astype(jnp.float32)
    lane = lax.broadcasted_iota(jnp.int32, lanes.shape, 1) - first_lane
    for order in range(2):
        for copy in weight_copies[order]:
            copy.wait()
        offset = lane - (where_ref[0] * 2 + (where_ref[1] + order) % 2)
        gain = jnp.sum(
            jnp.where((offset == 0) | (offset == experts), lanes, 0.0), axis=1, keepdims=True
        )
        summed = jnp.dot(rows[...], weights[order], preferred_element_type=jnp.float32)
        hidden = jax.nn.silu(summed[:, :half_hidden]) * summed[:, half_hidden:] * gain
        out_ref[:, order * half_hidden : (order + 1) * half_hidden] = hidden.astype(jnp.bfloat16)


def run_hidden(where, row_blocks, gain_blocks, own, near, far, direct, before, first_lane, experts):
    blocks = len(row_blocks)
    count = sum(block.shape[0] for block in row_blocks)
    _, width, columns = own.shape
    inputs = [*row_blocks, *gain_blocks, own, *near, *far, *direct, *before]
    return pl.pallas_call(
        functools.partial(
            hidden_kernel, blocks, len(gain_blocks), len(near), len(direct), first_lane, experts
        ),
        out_shape=jax.ShapeDtypeStruct((count, columns), jnp.bfloat16),
        in_specs=[pl.BlockSpec(memory_space=pltpu.SMEM)]
        + [pl.BlockSpec(memory_space=pltpu.HBM)] * len(inputs),
        out_specs=pl.BlockSpec(memory_space=pltpu.VMEM),
        scratch_shapes=[
            pltpu.VMEM((count, 2 * width), jnp.bfloat16),
            pltpu.VMEM((count, LANES), jnp.bfloat16),
            pltpu.VMEM((2, 2 * width, columns), jnp.bfloat16),
            pltpu.SemaphoreType.DMA((3, max(2 * blocks, 2 + len(near)))),
        ],
        compiler_params=pltpu.CompilerParams(vmem_limit_bytes=20 * 1024 * 1024),
        cost_estimate=pl.CostEstimate(
            flops=8 * count * width * columns,
            bytes_accessed=4 * width * (count + 2 * columns),
            transcendentals=count * columns,
        ),
    )(where, *inputs)


def down_kernel(halves, chunks, where_ref, hidden_ref, *refs):
    refs = list(refs)
    take = lambda count: [refs.pop(0) for _ in range(count)]
    chunk_refs = [take(chunks), take(chunks)]
    weights, sems = refs[-2:]
    out_refs, whole_refs = refs[-2 - len(halves) : -2], refs[: -2 - len(halves)]
    depth = weights.shape[0] // 2
    pairs = []
    for order in range(2):
        expert = (where_ref[1] + order) % 2
        parts = chunk_refs[order] + [ref.at[expert] for ref in whole_refs]
        pairs += chunk_pairs(parts, weights, order * depth)
    for copy in load(pairs, sems):
        copy.wait()
    rows = hidden_ref.shape[0] // 2
    for half, out_ref in zip(halves, out_refs):
        out_ref[...] = jnp.dot(
            hidden_ref[half * rows : (half + 1) * rows, :],
            weights[...],
            preferred_element_type=jnp.float32,
        ).astype(jnp.bfloat16)


def run_down(where, hidden, near, far, whole, halves=(0, 1)):
    count, depth = hidden.shape
    inputs = [*near, *far, *whole]
    columns = inputs[0].shape[-1]
    outs = len(halves)
    return pl.pallas_call(
        functools.partial(down_kernel, halves, len(near)),
        out_shape=(jax.ShapeDtypeStruct((count // 2, columns), jnp.bfloat16),) * outs,
        in_specs=[pl.BlockSpec(memory_space=pltpu.SMEM), pl.BlockSpec(memory_space=pltpu.VMEM)]
        + [pl.BlockSpec(memory_space=pltpu.HBM)] * len(inputs),
        out_specs=(pl.BlockSpec(memory_space=pltpu.VMEM),) * outs,
        scratch_shapes=[
            pltpu.VMEM((depth, columns), jnp.bfloat16),
            pltpu.SemaphoreType.DMA((2 * (len(near) + len(whole)),)),
        ],
        compiler_params=pltpu.CompilerParams(vmem_limit_bytes=16 * 1024 * 1024),
        cost_estimate=pl.CostEstimate(
            flops=outs * count * depth * columns,
            bytes_accessed=2 * depth * (count + columns) + outs * count * columns,
            transcendentals=0,
        ),
    )(where, hidden, *inputs)


def over_replica(array):
    return lax.ppermute(array, "replica", SWAP)


def over_groups(array):
    return lax.ppermute(array, "groups", SWAP)


def over_expert(array, distance):
    return lax.ppermute(
        array, "expert", [(at, at ^ distance) for at in range(lax.axis_size("expert"))]
    )


def after(array, *others):
    return lax.optimization_barrier((array, *others))[0] if others else array


def send(weights, group, first_row, rows, *before):
    piece = lax.dynamic_slice(weights, (group, first_row, 0), (1, rows, weights.shape[2]))[0]
    return over_replica(after(piece, *before))


def over_both(array, distance):
    owners = lax.axis_size("expert")
    pairs = [
        (2 * at + replica, 2 * (at ^ distance) + 1 - replica)
        for at in range(owners)
        for replica in range(2)
    ]
    return lax.ppermute(array, ("expert", "replica"), pairs)


def chip_sums(mine, other, cross=False):
    owners = lax.axis_size("expert")
    rows = mine.shape[0] // (owners // 2)
    terms = []
    for index in range(owners // 2):
        part = slice(index * rows, (index + 1) * rows)
        chip = mine[part].astype(jnp.float32) + other[part].astype(jnp.float32)
        if cross or index:
            chip = (over_both if cross else over_expert)(chip.astype(jnp.bfloat16), 2 * index)
        terms.append(chip)
    return terms


def spread_sums(mine, away, cross=False):
    return chip_sums(mine, over_expert(away, 1), cross)


def add_up(terms):
    return sum(term.astype(jnp.float32) for term in terms).astype(jnp.bfloat16)


def in_order(replica, own, other, axis):
    return jnp.concatenate(
        [jnp.where(replica == 0, own, other), jnp.where(replica == 0, other, own)], axis=axis
    )


def dense_on_device(
    hidden_in,
    routes,
    route_gain,
    w_in,
    w_out,
    handoff,
    speaking,
    talker_routes,
    talker_gain,
    talker_w_in,
    talker_w_out,
):
    replica, group = lax.axis_index("replica"), lax.axis_index("groups")
    where = jnp.stack([lax.axis_index("expert"), group, replica]).astype(jnp.int32)
    owners = lax.axis_size("expert")
    experts = w_in.shape[0] * owners
    rows = routes.shape[0] // 2
    distances = range(2, owners, 2)

    chunk = w_in.shape[1] * 13 // 32

    lanes = gain_lanes(
        where, experts, routes, route_gain, speaking, talker_routes, talker_gain
    )
    give = lax.dynamic_slice_in_dim(hidden_in, (1 - replica) * rows, rows, 0)
    other = over_replica(give)
    near_in = [send(w_in, group, index * chunk, chunk, other) for index in range(2)]
    row = build_row(where, hidden_in, other, lanes)
    same = [row] + [over_expert(row, distance) for distance in distances]
    far_in = [over_groups(after(near_in[0], same[2]))]
    far_in.append(over_groups(near_in[1]))
    direct_in = over_replica(after(w_in[:, 2 * chunk :], near_in[0]))
    across = [over_expert(after(row, far_in[0]), 1), over_expert(jnp.concatenate([*same[1:3], after(same[3], near_in[1])]), 1)]
    blocks = same + across
    hidden = run_hidden(where, blocks, [], w_in, near_in, far_in, [direct_in], [], 0, experts)
    other_hidden = over_replica(hidden)
    own = spread_sums(*run_down(where, hidden, [], [], [w_out]))
    other_hidden = after(other_hidden, *own[1:])
    (got_away,) = run_down(where, other_hidden, [], [], [w_out], (1,))
    other_hidden = after(other_hidden, got_away)
    (got_mine,) = run_down(where, other_hidden, [], [], [w_out], (0,))
    got_away = over_expert(got_away, 1)
    half = talker_w_in.shape[1] // 2
    near_talker_in = [send(talker_w_in, group, first, half, got_mine) for first in (0, half)]
    got = chip_sums(got_mine, got_away)
    far_talker_in = [over_groups(near_talker_in[0])]
    far_talker_in.append(over_groups(after(near_talker_in[1], far_talker_in[0])))
    got, own = add_up(got), add_up(own)
    thinker_out = in_order(replica, own, got, 0)

    def handed(array):
        return jnp.dot(array, handoff, preferred_element_type=jnp.float32)

    term = over_replica(handed(got).astype(jnp.bfloat16))
    direct_talker_out = over_replica(after(talker_w_out, term))
    talker_row = (handed(own) + term.astype(jnp.float32)).astype(jnp.bfloat16)
    parts = jnp.split(talker_row, 2, axis=1)
    talker_row = in_order(replica, parts[0], parts[1], 1)
    same = [talker_row] + [over_expert(talker_row, distance) for distance in distances]
    rest = after(jnp.concatenate(same[1:]), far_talker_in[1])
    talker_blocks = same + [over_expert(talker_row, 1), over_expert(rest, 1)]
    hidden = run_hidden(
        where,
        talker_blocks,
        blocks,
        talker_w_in,
        near_talker_in,
        far_talker_in,
        [],
        [direct_talker_out],
        2 * experts,
        experts,
    )
    give = run_down(where, hidden, [], [], [direct_talker_out])
    got = add_up(spread_sums(*give, cross=True))
    own = run_down(where, after(hidden, *give), [], [], [talker_w_out])
    own = add_up(spread_sums(*own))
    return (thinker_out, in_order(replica, own, got, 0))


def on_device(*arrays):
    token_count, top_count = arrays[1].shape
    local_experts = arrays[3].shape[0]
    experts = local_experts * lax.axis_size("expert")
    dense = (
        token_count * top_count * 2 // experts >= token_count
        and 4 * experts <= LANES
        and lax.axis_size("replica") == lax.axis_size("groups") == local_experts == 2
        and lax.axis_size("expert") in (2, 4, 8, 16)
    )
    return (dense_on_device if dense else routed_on_device)(*arrays)


def solution(mesh):
    return jax.shard_map(
        on_device,
        mesh=mesh,
        in_specs=(
            P(("groups", "expert"), "replica"),
            P(("groups", "expert"), None),
            P(("groups", "expert"), None),
            P("expert", "replica", None),
            P("expert", None, "replica"),
            P("replica", None),
            P(("groups", "expert")),
            P(("groups", "expert"), None),
            P(("groups", "expert"), None),
            P("expert", "replica", None),
            P("expert", None, "replica"),
        ),
        out_specs=(P(("groups", "expert"), "replica"), P(("groups", "expert"), "replica")),
        check_vma=False,
    )
```

```python
import functools

import jax
import jax.numpy as jnp
from jax import lax
from jax.experimental import pallas as pl
from jax.experimental.pallas import tpu as pltpu
from jax.sharding import PartitionSpec as P

LANES = 128
SWAP = [(0, 1), (1, 0)]


def place_rows(tok_rows, flat_ids, live_rows, experts, capacity):
    onehot = (flat_ids[:, None] == lax.iota(jnp.int32, experts)[None, :]).astype(
        jnp.int32
    ) * live_rows[:, None]
    before = jnp.cumsum(onehot, axis=0) - onehot
    slot_rank = jnp.sum(before * onehot, axis=1)
    slot_index = jnp.where(live_rows > 0, flat_ids * capacity + slot_rank, experts * capacity)
    buffer = (
        jnp.zeros((experts * capacity, tok_rows.shape[1]), tok_rows.dtype)
        .at[slot_index]
        .set(tok_rows, mode="drop")
    )
    return (buffer, slot_index)


def activate(gate_sum, up_sum):
    return (jax.nn.silu(gate_sum) * up_sum).astype(jnp.bfloat16)


def down_rows(second_weights, piece):
    return jnp.einsum("lrf,lfd->lrd", piece, second_weights, preferred_element_type=jnp.float32)


def routed_on_device(
    hidden_in,
    routes,
    route_gain,
    w_in,
    w_out,
    handoff,
    speaking,
    talker_routes,
    talker_gain,
    talker_w_in,
    talker_w_out,
):
    owners = lax.axis_size("expert")
    token_count, top_count = routes.shape
    local_experts = w_in.shape[0]
    experts = local_experts * owners
    capacity = max(2, token_count * top_count * 2 // experts)
    talker_capacity = max(2, capacity * 3 // 4)
    flat_ids = routes.reshape(-1)
    all_rows = jnp.ones_like(flat_ids)
    spread = jnp.repeat(hidden_in, top_count, axis=0)
    buffer, slot_index = place_rows(spread, flat_ids, all_rows, experts, capacity)
    arrived = lax.all_to_all(
        buffer.reshape(owners, local_experts, capacity, -1),
        "expert",
        split_axis=0,
        concat_axis=2,
        tiled=True,
    )
    partial_value = jnp.einsum("lrd,ldf->lrf", arrived[0], w_in, preferred_element_type=jnp.float32)
    hidden_width = w_in.shape[2] // 2
    share_sum = lax.psum_scatter(
        partial_value.astype(jnp.bfloat16), "replica", scatter_dimension=1, tiled=True
    ).astype(jnp.float32)
    hidden = activate(share_sum[:, :, :hidden_width], share_sum[:, :, hidden_width:])
    expert_out = down_rows(w_out, lax.all_gather(hidden, "replica", axis=1, tiled=True))
    returned = lax.all_to_all(
        expert_out.astype(jnp.bfloat16)[None], "expert", split_axis=2, concat_axis=0, tiled=True
    )
    returned = returned.reshape(experts * capacity, -1)
    picked = returned[slot_index].astype(jnp.float32).reshape(token_count, top_count, -1)
    thinker_out = jnp.sum(picked * route_gain[:, :, None], axis=1).astype(jnp.bfloat16)
    handoff_terms = jnp.dot(thinker_out, handoff, preferred_element_type=jnp.float32)
    talker_in = lax.psum_scatter(
        handoff_terms.astype(jnp.bfloat16), "replica", scatter_dimension=1, tiled=True
    )
    talker_ids = talker_routes.reshape(-1)
    speak_rows = jnp.repeat(speaking, top_count)
    talker_spread = jnp.repeat(talker_in, top_count, axis=0)
    talker_buffer, talker_slots = place_rows(
        talker_spread, talker_ids, speak_rows, experts, talker_capacity
    )
    talker_arrived = lax.all_to_all(
        talker_buffer.reshape(owners, local_experts, talker_capacity, -1),
        "expert",
        split_axis=0,
        concat_axis=2,
        tiled=True,
    )
    talker_partial = jnp.einsum(
        "lrd,ldf->lrf", talker_arrived[0], talker_w_in, preferred_element_type=jnp.float32
    )
    talker_hidden_width = talker_w_in.shape[2] // 2
    talker_share = lax.psum_scatter(
        talker_partial.astype(jnp.bfloat16), "replica", scatter_dimension=1, tiled=True
    ).astype(jnp.float32)
    talker_hidden = activate(
        talker_share[:, :, :talker_hidden_width], talker_share[:, :, talker_hidden_width:]
    )
    talker_expert_out = down_rows(
        talker_w_out, lax.all_gather(talker_hidden, "replica", axis=1, tiled=True)
    )
    talker_returned = lax.all_to_all(
        talker_expert_out.astype(jnp.bfloat16)[None],
        "expert",
        split_axis=2,
        concat_axis=0,
        tiled=True,
    )
    talker_returned = talker_returned.reshape(experts * talker_capacity, -1)
    safe_slots = jnp.minimum(talker_slots, experts * talker_capacity - 1)
    talker_picked = (
        talker_returned[safe_slots].astype(jnp.float32).reshape(token_count, top_count, -1)
    )
    talker_weights = talker_gain * speak_rows.reshape(token_count, top_count).astype(jnp.float32)
    talker_out = jnp.sum(talker_picked * talker_weights[:, :, None], axis=1).astype(jnp.bfloat16)
    return (thinker_out, talker_out)


def lanes_kernel(experts, where_ref, *refs):
    routes_ref, gain_ref, live_ref, talker_routes_ref, talker_gain_ref, out_ref, lanes = refs
    rows = out_ref.shape[0]
    stack = []
    live = live_ref[...].astype(jnp.float32)
    for ids, gains in ((routes_ref, gain_ref[...]), (talker_routes_ref, talker_gain_ref[...] * live)):
        expert = lax.broadcasted_iota(jnp.int32, (experts, ids.shape[1]), 0)
        dense = jnp.zeros(expert.shape, jnp.float32)
        for choice in range(ids.shape[0]):
            dense += jnp.where(
                ids[choice : choice + 1, :] == expert, gains[choice : choice + 1, :], 0.0
            )
        high = dense.astype(jnp.bfloat16).astype(jnp.float32)
        stack += [high, dense - high]
    stack.append(jnp.zeros((LANES - 4 * experts, live.shape[1]), jnp.float32))
    lanes[...] = jnp.concatenate(stack, axis=0).T
    first = pl.multiple_of(where_ref[2] * rows, rows)
    out_ref[...] = lanes[pl.ds(first, rows), :].astype(jnp.bfloat16)


def gain_lanes(where, experts, routes, gain, live, talker_routes, talker_gain):
    count = routes.shape[0]
    inputs = [routes.T, gain.T, live[None], talker_routes.T, talker_gain.T]
    return pl.pallas_call(
        functools.partial(lanes_kernel, experts),
        out_shape=jax.ShapeDtypeStruct((count // 2, LANES), jnp.bfloat16),
        in_specs=[pl.BlockSpec(memory_space=pltpu.SMEM)]
        + [pl.BlockSpec(memory_space=pltpu.VMEM)] * len(inputs),
        out_specs=pl.BlockSpec(memory_space=pltpu.VMEM),
        scratch_shapes=[pltpu.VMEM((count, LANES), jnp.float32)],
        compiler_params=pltpu.CompilerParams(vmem_limit_bytes=4 * 1024 * 1024),
        cost_estimate=pl.CostEstimate(
            flops=1 << 30, bytes_accessed=64 * count * LANES, transcendentals=0
        ),
    )(where, *inputs)


def row_kernel(where_ref, hidden_ref, other_ref, lanes_ref, out_ref):
    rows, width = other_ref.shape
    first = pl.multiple_of(where_ref[2] * rows, rows)
    out_ref[:, :width] = hidden_ref[pl.ds(first, rows), :]
    out_ref[:, width : 2 * width] = other_ref[...]
    out_ref[:, 2 * width :] = lanes_ref[...]


def build_row(where, hidden_in, other, lanes):
    rows, width = other.shape
    return pl.pallas_call(
        row_kernel,
        out_shape=jax.ShapeDtypeStruct((rows, 2 * width + LANES), jnp.bfloat16),
        in_specs=[pl.BlockSpec(memory_space=pltpu.SMEM)]
        + [pl.BlockSpec(memory_space=pltpu.VMEM)] * 3,
        out_specs=pl.BlockSpec(memory_space=pltpu.VMEM),
        compiler_params=pltpu.CompilerParams(vmem_limit_bytes=4 * 1024 * 1024),
        cost_estimate=pl.CostEstimate(flops=0, bytes_accessed=8 * rows * width, transcendentals=0),
    )(where, hidden_in, other, lanes)


def load(pairs, sems):
    copies = [
        pltpu.make_async_copy(source, destination, sems.at[index])
        for index, (source, destination) in enumerate(pairs)
    ]
    for copy in copies:
        copy.start()
    return copies


def chunk_pairs(chunks, place, first_row=0):
    pairs, row = [], first_row
    for chunk in chunks:
        pairs.append((chunk, place.at[pl.ds(row, chunk.shape[0])]))
        row += chunk.shape[0]
    return pairs


def hidden_kernel(blocks, gain_blocks, chunks, direct, first_lane, experts, where_ref, *refs):
    refs = list(refs)
    take = lambda count: [refs.pop(0) for _ in range(count)]
    row_refs, gain_refs = take(blocks), take(gain_blocks)
    (own_ref,) = take(1)
    chunk_refs = [take(chunks), take(chunks)]
    direct_refs = take(direct)
    out_ref, rows, gains, weights, sems = refs[-5:]
    width = own_ref.shape[1]
    half_hidden = own_ref.shape[2] // 2
    lane_refs = [ref.at[:, pl.ds(ref.shape[1] - LANES, LANES)] for ref in gain_refs or row_refs]
    row_refs = [ref.at[:, pl.ds(0, 2 * width)] for ref in row_refs]
    row_copies = load(chunk_pairs(row_refs, rows) + chunk_pairs(lane_refs, gains), sems.at[0])
    weight_copies = []
    for order in range(2):
        expert = (where_ref[1] + order) % 2
        parts = [own_ref.at[expert], *chunk_refs[order]]
        parts += [ref.at[expert] for ref in direct_refs]
        weight_copies.append(load(chunk_pairs(parts, weights.at[order]), sems.at[1 + order]))
    for copy in row_copies:
        copy.wait()
    lanes = gains[...].astype(jnp.float32)
    lane = lax.broadcasted_iota(jnp.int32, lanes.shape, 1) - first_lane
    for order in range(2):
        for copy in weight_copies[order]:
            copy.wait()
        offset = lane - (where_ref[0] * 2 + (where_ref[1] + order) % 2)
        gain = jnp.sum(
            jnp.where((offset == 0) | (offset == experts), lanes, 0.0), axis=1, keepdims=True
        )
        summed = jnp.dot(rows[...], weights[order], preferred_element_type=jnp.float32)
        hidden = jax.nn.silu(summed[:, :half_hidden]) * summed[:, half_hidden:] * gain
        out_ref[:, order * half_hidden : (order + 1) * half_hidden] = hidden.astype(jnp.bfloat16)


def run_hidden(where, row_blocks, gain_blocks, own, near, far, direct, before, first_lane, experts):
    blocks = len(row_blocks)
    count = sum(block.shape[0] for block in row_blocks)
    _, width, columns = own.shape
    inputs = [*row_blocks, *gain_blocks, own, *near, *far, *direct, *before]
    return pl.pallas_call(
        functools.partial(
            hidden_kernel, blocks, len(gain_blocks), len(near), len(direct), first_lane, experts
        ),
        out_shape=jax.ShapeDtypeStruct((count, columns), jnp.bfloat16),
        in_specs=[pl.BlockSpec(memory_space=pltpu.SMEM)]
        + [pl.BlockSpec(memory_space=pltpu.HBM)] * len(inputs),
        out_specs=pl.BlockSpec(memory_space=pltpu.VMEM),
        scratch_shapes=[
            pltpu.VMEM((count, 2 * width), jnp.bfloat16),
            pltpu.VMEM((count, LANES), jnp.bfloat16),
            pltpu.VMEM((2, 2 * width, columns), jnp.bfloat16),
            pltpu.SemaphoreType.DMA((3, max(2 * blocks, 2 + len(near)))),
        ],
        compiler_params=pltpu.CompilerParams(vmem_limit_bytes=20 * 1024 * 1024),
        cost_estimate=pl.CostEstimate(
            flops=8 * count * width * columns,
            bytes_accessed=4 * width * (count + 2 * columns),
            transcendentals=count * columns,
        ),
    )(where, *inputs)


def down_kernel(halves, chunks, where_ref, hidden_ref, *refs):
    refs = list(refs)
    take = lambda count: [refs.pop(0) for _ in range(count)]
    chunk_refs = [take(chunks), take(chunks)]
    weights, sems = refs[-2:]
    out_refs, whole_refs = refs[-2 - len(halves) : -2], refs[: -2 - len(halves)]
    depth = weights.shape[0] // 2
    pairs = []
    for order in range(2):
        expert = (where_ref[1] + order) % 2
        parts = chunk_refs[order] + [ref.at[expert] for ref in whole_refs]
        pairs += chunk_pairs(parts, weights, order * depth)
    for copy in load(pairs, sems):
        copy.wait()
    rows = hidden_ref.shape[0] // 2
    for half, out_ref in zip(halves, out_refs):
        out_ref[...] = jnp.dot(
            hidden_ref[half * rows : (half + 1) * rows, :],
            weights[...],
            preferred_element_type=jnp.float32,
        ).astype(jnp.bfloat16)


def run_down(where, hidden, near, far, whole, halves=(0, 1)):
    count, depth = hidden.shape
    inputs = [*near, *far, *whole]
    columns = inputs[0].shape[-1]
    outs = len(halves)
    return pl.pallas_call(
        functools.partial(down_kernel, halves, len(near)),
        out_shape=(jax.ShapeDtypeStruct((count // 2, columns), jnp.bfloat16),) * outs,
        in_specs=[pl.BlockSpec(memory_space=pltpu.SMEM), pl.BlockSpec(memory_space=pltpu.VMEM)]
        + [pl.BlockSpec(memory_space=pltpu.HBM)] * len(inputs),
        out_specs=(pl.BlockSpec(memory_space=pltpu.VMEM),) * outs,
        scratch_shapes=[
            pltpu.VMEM((depth, columns), jnp.bfloat16),
            pltpu.SemaphoreType.DMA((2 * (len(near) + len(whole)),)),
        ],
        compiler_params=pltpu.CompilerParams(vmem_limit_bytes=16 * 1024 * 1024),
        cost_estimate=pl.CostEstimate(
            flops=outs * count * depth * columns,
            bytes_accessed=2 * depth * (count + columns) + outs * count * columns,
            transcendentals=0,
        ),
    )(where, hidden, *inputs)


def over_replica(array):
    return lax.ppermute(array, "replica", SWAP)


def over_groups(array):
    return lax.ppermute(array, "groups", SWAP)


def over_expert(array, distance):
    return lax.ppermute(
        array, "expert", [(at, at ^ distance) for at in range(lax.axis_size("expert"))]
    )


def after(array, *others):
    return lax.optimization_barrier((array, *others))[0] if others else array


def send(weights, group, first_row, rows, *before):
    piece = lax.dynamic_slice(weights, (group, first_row, 0), (1, rows, weights.shape[2]))[0]
    return over_replica(after(piece, *before))


def over_both(array, distance):
    owners = lax.axis_size("expert")
    pairs = [
        (2 * at + replica, 2 * (at ^ distance) + 1 - replica)
        for at in range(owners)
        for replica in range(2)
    ]
    return lax.ppermute(array, ("expert", "replica"), pairs)


def chip_sums(mine, other, cross=False):
    owners = lax.axis_size("expert")
    rows = mine.shape[0] // (owners // 2)
    terms = []
    for index in range(owners // 2):
        part = slice(index * rows, (index + 1) * rows)
        chip = mine[part].astype(jnp.float32) + other[part].astype(jnp.float32)
        if cross or index:
            chip = (over_both if cross else over_expert)(chip.astype(jnp.bfloat16), 2 * index)
        terms.append(chip)
    return terms


def spread_sums(mine, away, cross=False):
    return chip_sums(mine, over_expert(away, 1), cross)


def add_up(terms):
    return sum(term.astype(jnp.float32) for term in terms).astype(jnp.bfloat16)


def in_order(replica, own, other, axis):
    return jnp.concatenate(
        [jnp.where(replica == 0, own, other), jnp.where(replica == 0, other, own)], axis=axis
    )


def dense_on_device(
    hidden_in,
    routes,
    route_gain,
    w_in,
    w_out,
    handoff,
    speaking,
    talker_routes,
    talker_gain,
    talker_w_in,
    talker_w_out,
):
    replica, group = lax.axis_index("replica"), lax.axis_index("groups")
    where = jnp.stack([lax.axis_index("expert"), group, replica]).astype(jnp.int32)
    owners = lax.axis_size("expert")
    experts = w_in.shape[0] * owners
    rows = routes.shape[0] // 2
    distances = range(2, owners, 2)

    chunk = w_in.shape[1] * 13 // 32

    lanes = gain_lanes(
        where, experts, routes, route_gain, speaking, talker_routes, talker_gain
    )
    give = lax.dynamic_slice_in_dim(hidden_in, (1 - replica) * rows, rows, 0)
    other = over_replica(give)
    near_in = [send(w_in, group, index * chunk, chunk, other) for index in range(2)]
    row = build_row(where, hidden_in, other, lanes)
    same = [row] + [over_expert(row, distance) for distance in distances]
    far_in = [over_groups(after(near_in[0], same[1]))]
    far_in.append(over_groups(near_in[1]))
    direct_in = over_replica(after(w_in[:, 2 * chunk :], near_in[0]))
    across = [over_expert(after(row, far_in[0]), 1), over_expert(jnp.concatenate([*same[1:3], after(same[3], near_in[1])]), 1)]
    blocks = same + across
    hidden = run_hidden(where, blocks, [], w_in, near_in, far_in, [direct_in], [], 0, experts)
    other_hidden = over_replica(hidden)
    own = spread_sums(*run_down(where, hidden, [], [], [w_out]))
    other_hidden = after(other_hidden, *own[1:])
    (got_away,) = run_down(where, other_hidden, [], [], [w_out], (1,))
    other_hidden = after(other_hidden, got_away)
    (got_mine,) = run_down(where, other_hidden, [], [], [w_out], (0,))
    got_away = over_expert(got_away, 1)
    half = talker_w_in.shape[1] // 2
    near_talker_in = [send(talker_w_in, group, first, half, got_mine) for first in (0, half)]
    got = chip_sums(got_mine, got_away)
    far_talker_in = [over_groups(near_talker_in[0])]
    far_talker_in.append(over_groups(after(near_talker_in[1], far_talker_in[0])))
    got, own = add_up(got), add_up(own)
    thinker_out = in_order(replica, own, got, 0)

    def handed(array):
        return jnp.dot(array, handoff, preferred_element_type=jnp.float32)

    term = over_replica(handed(got).astype(jnp.bfloat16))
    direct_talker_out = over_replica(after(talker_w_out, term))
    talker_row = (handed(own) + term.astype(jnp.float32)).astype(jnp.bfloat16)
    parts = jnp.split(talker_row, 2, axis=1)
    talker_row = in_order(replica, parts[0], parts[1], 1)
    same = [talker_row] + [over_expert(talker_row, distance) for distance in distances]
    rest = after(jnp.concatenate(same[1:]), far_talker_in[1])
    talker_blocks = same + [over_expert(talker_row, 1), over_expert(rest, 1)]
    hidden = run_hidden(
        where,
        talker_blocks,
        blocks,
        talker_w_in,
        near_talker_in,
        far_talker_in,
        [],
        [direct_talker_out],
        2 * experts,
        experts,
    )
    give = run_down(where, hidden, [], [], [direct_talker_out])
    got = add_up(spread_sums(*give, cross=True))
    own = run_down(where, after(hidden, *give), [], [], [talker_w_out])
    own = add_up(spread_sums(*own))
    return (thinker_out, in_order(replica, own, got, 0))


def on_device(*arrays):
    token_count, top_count = arrays[1].shape
    local_experts = arrays[3].shape[0]
    experts = local_experts * lax.axis_size("expert")
    dense = (
        token_count * top_count * 2 // experts >= token_count
        and 4 * experts <= LANES
        and lax.axis_size("replica") == lax.axis_size("groups") == local_experts == 2
        and lax.axis_size("expert") in (2, 4, 8, 16)
    )
    return (dense_on_device if dense else routed_on_device)(*arrays)


def solution(mesh):
    return jax.shard_map(
        on_device,
        mesh=mesh,
        in_specs=(
            P(("groups", "expert"), "replica"),
            P(("groups", "expert"), None),
            P(("groups", "expert"), None),
            P("expert", "replica", None),
            P("expert", None, "replica"),
            P("replica", None),
            P(("groups", "expert")),
            P(("groups", "expert"), None),
            P(("groups", "expert"), None),
            P("expert", "replica", None),
            P("expert", None, "replica"),
        ),
        out_specs=(P(("groups", "expert"), "replica"), P(("groups", "expert"), "replica")),
        check_vma=False,
    )
```

```python
import functools

import jax
import jax.numpy as jnp
from jax import lax
from jax.experimental import pallas as pl
from jax.experimental.pallas import tpu as pltpu
from jax.sharding import PartitionSpec as P

LANES = 128
SWAP = [(0, 1), (1, 0)]


def place_rows(tok_rows, flat_ids, live_rows, experts, capacity):
    onehot = (flat_ids[:, None] == lax.iota(jnp.int32, experts)[None, :]).astype(
        jnp.int32
    ) * live_rows[:, None]
    before = jnp.cumsum(onehot, axis=0) - onehot
    slot_rank = jnp.sum(before * onehot, axis=1)
    slot_index = jnp.where(live_rows > 0, flat_ids * capacity + slot_rank, experts * capacity)
    buffer = (
        jnp.zeros((experts * capacity, tok_rows.shape[1]), tok_rows.dtype)
        .at[slot_index]
        .set(tok_rows, mode="drop")
    )
    return (buffer, slot_index)


def activate(gate_sum, up_sum):
    return (jax.nn.silu(gate_sum) * up_sum).astype(jnp.bfloat16)


def down_rows(second_weights, piece):
    return jnp.einsum("lrf,lfd->lrd", piece, second_weights, preferred_element_type=jnp.float32)


def routed_on_device(
    hidden_in,
    routes,
    route_gain,
    w_in,
    w_out,
    handoff,
    speaking,
    talker_routes,
    talker_gain,
    talker_w_in,
    talker_w_out,
):
    owners = lax.axis_size("expert")
    token_count, top_count = routes.shape
    local_experts = w_in.shape[0]
    experts = local_experts * owners
    capacity = max(2, token_count * top_count * 2 // experts)
    talker_capacity = max(2, capacity * 3 // 4)
    flat_ids = routes.reshape(-1)
    all_rows = jnp.ones_like(flat_ids)
    spread = jnp.repeat(hidden_in, top_count, axis=0)
    buffer, slot_index = place_rows(spread, flat_ids, all_rows, experts, capacity)
    arrived = lax.all_to_all(
        buffer.reshape(owners, local_experts, capacity, -1),
        "expert",
        split_axis=0,
        concat_axis=2,
        tiled=True,
    )
    partial_value = jnp.einsum("lrd,ldf->lrf", arrived[0], w_in, preferred_element_type=jnp.float32)
    hidden_width = w_in.shape[2] // 2
    share_sum = lax.psum_scatter(
        partial_value.astype(jnp.bfloat16), "replica", scatter_dimension=1, tiled=True
    ).astype(jnp.float32)
    hidden = activate(share_sum[:, :, :hidden_width], share_sum[:, :, hidden_width:])
    expert_out = down_rows(w_out, lax.all_gather(hidden, "replica", axis=1, tiled=True))
    returned = lax.all_to_all(
        expert_out.astype(jnp.bfloat16)[None], "expert", split_axis=2, concat_axis=0, tiled=True
    )
    returned = returned.reshape(experts * capacity, -1)
    picked = returned[slot_index].astype(jnp.float32).reshape(token_count, top_count, -1)
    thinker_out = jnp.sum(picked * route_gain[:, :, None], axis=1).astype(jnp.bfloat16)
    handoff_terms = jnp.dot(thinker_out, handoff, preferred_element_type=jnp.float32)
    talker_in = lax.psum_scatter(
        handoff_terms.astype(jnp.bfloat16), "replica", scatter_dimension=1, tiled=True
    )
    talker_ids = talker_routes.reshape(-1)
    speak_rows = jnp.repeat(speaking, top_count)
    talker_spread = jnp.repeat(talker_in, top_count, axis=0)
    talker_buffer, talker_slots = place_rows(
        talker_spread, talker_ids, speak_rows, experts, talker_capacity
    )
    talker_arrived = lax.all_to_all(
        talker_buffer.reshape(owners, local_experts, talker_capacity, -1),
        "expert",
        split_axis=0,
        concat_axis=2,
        tiled=True,
    )
    talker_partial = jnp.einsum(
        "lrd,ldf->lrf", talker_arrived[0], talker_w_in, preferred_element_type=jnp.float32
    )
    talker_hidden_width = talker_w_in.shape[2] // 2
    talker_share = lax.psum_scatter(
        talker_partial.astype(jnp.bfloat16), "replica", scatter_dimension=1, tiled=True
    ).astype(jnp.float32)
    talker_hidden = activate(
        talker_share[:, :, :talker_hidden_width], talker_share[:, :, talker_hidden_width:]
    )
    talker_expert_out = down_rows(
        talker_w_out, lax.all_gather(talker_hidden, "replica", axis=1, tiled=True)
    )
    talker_returned = lax.all_to_all(
        talker_expert_out.astype(jnp.bfloat16)[None],
        "expert",
        split_axis=2,
        concat_axis=0,
        tiled=True,
    )
    talker_returned = talker_returned.reshape(experts * talker_capacity, -1)
    safe_slots = jnp.minimum(talker_slots, experts * talker_capacity - 1)
    talker_picked = (
        talker_returned[safe_slots].astype(jnp.float32).reshape(token_count, top_count, -1)
    )
    talker_weights = talker_gain * speak_rows.reshape(token_count, top_count).astype(jnp.float32)
    talker_out = jnp.sum(talker_picked * talker_weights[:, :, None], axis=1).astype(jnp.bfloat16)
    return (thinker_out, talker_out)


def lanes_kernel(experts, where_ref, *refs):
    routes_ref, gain_ref, live_ref, talker_routes_ref, talker_gain_ref, out_ref, lanes = refs
    rows = out_ref.shape[0]
    stack = []
    live = live_ref[...].astype(jnp.float32)
    for ids, gains in ((routes_ref, gain_ref[...]), (talker_routes_ref, talker_gain_ref[...] * live)):
        expert = lax.broadcasted_iota(jnp.int32, (experts, ids.shape[1]), 0)
        dense = jnp.zeros(expert.shape, jnp.float32)
        for choice in range(ids.shape[0]):
            dense += jnp.where(
                ids[choice : choice + 1, :] == expert, gains[choice : choice + 1, :], 0.0
            )
        high = dense.astype(jnp.bfloat16).astype(jnp.float32)
        stack += [high, dense - high]
    stack.append(jnp.zeros((LANES - 4 * experts, live.shape[1]), jnp.float32))
    lanes[...] = jnp.concatenate(stack, axis=0).T
    first = pl.multiple_of(where_ref[2] * rows, rows)
    out_ref[...] = lanes[pl.ds(first, rows), :].astype(jnp.bfloat16)


def gain_lanes(where, experts, routes, gain, live, talker_routes, talker_gain):
    count = routes.shape[0]
    inputs = [routes.T, gain.T, live[None], talker_routes.T, talker_gain.T]
    return pl.pallas_call(
        functools.partial(lanes_kernel, experts),
        out_shape=jax.ShapeDtypeStruct((count // 2, LANES), jnp.bfloat16),
        in_specs=[pl.BlockSpec(memory_space=pltpu.SMEM)]
        + [pl.BlockSpec(memory_space=pltpu.VMEM)] * len(inputs),
        out_specs=pl.BlockSpec(memory_space=pltpu.VMEM),
        scratch_shapes=[pltpu.VMEM((count, LANES), jnp.float32)],
        compiler_params=pltpu.CompilerParams(vmem_limit_bytes=4 * 1024 * 1024),
        cost_estimate=pl.CostEstimate(
            flops=1 << 30, bytes_accessed=64 * count * LANES, transcendentals=0
        ),
    )(where, *inputs)


def row_kernel(where_ref, hidden_ref, other_ref, lanes_ref, out_ref):
    rows, width = other_ref.shape
    first = pl.multiple_of(where_ref[2] * rows, rows)
    out_ref[:, :width] = hidden_ref[pl.ds(first, rows), :]
    out_ref[:, width : 2 * width] = other_ref[...]
    out_ref[:, 2 * width :] = lanes_ref[...]


def build_row(where, hidden_in, other, lanes):
    rows, width = other.shape
    return pl.pallas_call(
        row_kernel,
        out_shape=jax.ShapeDtypeStruct((rows, 2 * width + LANES), jnp.bfloat16),
        in_specs=[pl.BlockSpec(memory_space=pltpu.SMEM)]
        + [pl.BlockSpec(memory_space=pltpu.VMEM)] * 3,
        out_specs=pl.BlockSpec(memory_space=pltpu.VMEM),
        compiler_params=pltpu.CompilerParams(vmem_limit_bytes=4 * 1024 * 1024),
        cost_estimate=pl.CostEstimate(flops=0, bytes_accessed=8 * rows * width, transcendentals=0),
    )(where, hidden_in, other, lanes)


def load(pairs, sems):
    copies = [
        pltpu.make_async_copy(source, destination, sems.at[index])
        for index, (source, destination) in enumerate(pairs)
    ]
    for copy in copies:
        copy.start()
    return copies


def chunk_pairs(chunks, place, first_row=0):
    pairs, row = [], first_row
    for chunk in chunks:
        pairs.append((chunk, place.at[pl.ds(row, chunk.shape[0])]))
        row += chunk.shape[0]
    return pairs


def gated(summed, lanes, first_lane, experts, where_ref, order):
    half = summed.shape[1] // 2
    expert = where_ref[0] * 2 + (where_ref[1] + order) % 2
    offset = lax.broadcasted_iota(jnp.int32, lanes.shape, 1) - first_lane - expert
    gain = jnp.sum(
        jnp.where((offset == 0) | (offset == experts), lanes, 0.0), axis=1, keepdims=True
    )
    return (jax.nn.silu(summed[:, :half]) * summed[:, half:] * gain).astype(jnp.bfloat16)


def early_kernel(blocks, where_ref, *refs):
    row_refs, refs = refs[:blocks], refs[blocks:]
    own_ref, near_refs, far_ref, sums_ref, late_ref, lanes_ref, rows, weights, sems = (
        refs[0], refs[1:3], *refs[3:]
    )
    width, late = own_ref.shape[1], late_ref.shape[1]
    early = rows.shape[1] - late
    group = where_ref[1]
    pairs = chunk_pairs([ref.at[:, pl.ds(0, 2 * width)] for ref in row_refs], rows)
    pairs += chunk_pairs([ref.at[:, pl.ds(2 * width, LANES)] for ref in row_refs], lanes_ref)
    pairs += chunk_pairs([own_ref.at[group], *near_refs], weights.at[0])
    pairs += chunk_pairs([own_ref.at[1 - group], far_ref], weights.at[1])
    for copy in load(pairs, sems):
        copy.wait()
    late_ref[...] = rows[:, early:]
    near = early + near_refs[1].shape[0]
    padded = weights.shape[1]
    if padded > near:
        weights[0, near:] = jnp.zeros((padded - near, weights.shape[2]), jnp.bfloat16)
    for order, depth in enumerate((padded, early)):
        sums_ref[order] = jnp.dot(
            rows[:, :depth], weights[order, :depth], preferred_element_type=jnp.float32
        )


def run_early(where, row_blocks, own, near, far):
    blocks, count = len(row_blocks), sum(block.shape[0] for block in row_blocks)
    _, width, columns = own.shape
    chunk = far.shape[0]
    late = width - chunk
    inputs = [*row_blocks, own, *near, far]
    return pl.pallas_call(
        functools.partial(early_kernel, blocks),
        out_shape=(
            jax.ShapeDtypeStruct((2, count, columns), jnp.float32),
            jax.ShapeDtypeStruct((count, late), jnp.bfloat16),
            jax.ShapeDtypeStruct((count, LANES), jnp.bfloat16),
        ),
        in_specs=[pl.BlockSpec(memory_space=pltpu.SMEM)]
        + [pl.BlockSpec(memory_space=pltpu.HBM)] * len(inputs),
        out_specs=(pl.BlockSpec(memory_space=pltpu.VMEM),) * 3,
        scratch_shapes=[
            pltpu.VMEM((count, 2 * width), jnp.bfloat16),
            pltpu.VMEM((2, pl.cdiv(width + chunk + near[1].shape[0], LANES) * LANES, columns), jnp.bfloat16),
            pltpu.SemaphoreType.DMA((2 * blocks + 5,)),
        ],
        compiler_params=pltpu.CompilerParams(vmem_limit_bytes=24 * 1024 * 1024),
        cost_estimate=pl.CostEstimate(
            flops=2 * count * (2 * width + 3 * chunk) * columns,
            bytes_accessed=4 * count * width + 2 * (2 * width + 3 * chunk) * columns,
            transcendentals=0,
        ),
    )(where, *inputs)


def late_kernel(experts, where_ref, sums_ref, late_ref, lanes_ref, far_ref, direct_ref, out_ref, weights, sems):
    chunk, rest = far_ref.shape[0], direct_ref.shape[1]
    half = sums_ref.shape[2] // 2
    group = where_ref[1]
    pairs = [
        (direct_ref.at[group], weights.at[0, pl.ds(chunk, rest)]),
        (far_ref, weights.at[1, pl.ds(0, chunk)]),
        (direct_ref.at[1 - group], weights.at[1, pl.ds(chunk, rest)]),
    ]
    copies = load(pairs, sems)
    aligned = chunk // LANES * LANES
    if chunk > aligned:
        weights[0, aligned:chunk] = jnp.zeros((chunk - aligned, weights.shape[2]), jnp.bfloat16)
    lanes = lanes_ref[...].astype(jnp.float32)
    for order, (first, needed) in enumerate(((aligned, copies[:1]), (0, copies[1:]))):
        for copy in needed:
            copy.wait()
        summed = sums_ref[order] + jnp.dot(
            late_ref[:, first:], weights[order, first:], preferred_element_type=jnp.float32
        )
        out_ref[:, order * half : (order + 1) * half] = gated(
            summed, lanes, 0, experts, where_ref, order
        )


def run_late(where, early, far, direct, experts):
    sums, late, lanes = early
    _, count, columns = sums.shape
    return pl.pallas_call(
        functools.partial(late_kernel, experts),
        out_shape=jax.ShapeDtypeStruct((count, columns), jnp.bfloat16),
        in_specs=[pl.BlockSpec(memory_space=pltpu.SMEM)]
        + [pl.BlockSpec(memory_space=pltpu.VMEM)] * 3
        + [pl.BlockSpec(memory_space=pltpu.HBM)] * 2,
        out_specs=pl.BlockSpec(memory_space=pltpu.VMEM),
        scratch_shapes=[
            pltpu.VMEM((2, late.shape[1], columns), jnp.bfloat16),
            pltpu.SemaphoreType.DMA((3,)),
        ],
        compiler_params=pltpu.CompilerParams(vmem_limit_bytes=16 * 1024 * 1024),
        cost_estimate=pl.CostEstimate(
            flops=4 * count * late.shape[1] * columns,
            bytes_accessed=8 * count * columns,
            transcendentals=count * columns,
        ),
    )(where, sums, late, lanes, far, direct)


def hidden_kernel(blocks, gain_blocks, chunks, direct, first_lane, experts, where_ref, *refs):
    refs = list(refs)
    take = lambda count: [refs.pop(0) for _ in range(count)]
    row_refs, gain_refs = take(blocks), take(gain_blocks)
    (own_ref,) = take(1)
    chunk_refs = [take(chunks), take(chunks)]
    direct_refs = take(direct)
    out_ref, rows, gains, weights, sems = refs[-5:]
    width = own_ref.shape[1]
    half_hidden = own_ref.shape[2] // 2
    lane_refs = [ref.at[:, pl.ds(ref.shape[1] - LANES, LANES)] for ref in gain_refs or row_refs]
    row_refs = [ref.at[:, pl.ds(0, 2 * width)] for ref in row_refs]
    row_copies = load(chunk_pairs(row_refs, rows) + chunk_pairs(lane_refs, gains), sems.at[0])
    weight_copies = []
    for order in range(2):
        expert = (where_ref[1] + order) % 2
        parts = [own_ref.at[expert], *chunk_refs[order]]
        parts += [ref.at[expert] for ref in direct_refs]
        weight_copies.append(load(chunk_pairs(parts, weights.at[order]), sems.at[1 + order]))
    for copy in row_copies:
        copy.wait()
    lanes = gains[...].astype(jnp.float32)
    for order in range(2):
        for copy in weight_copies[order]:
            copy.wait()
        summed = jnp.dot(rows[...], weights[order], preferred_element_type=jnp.float32)
        hidden = gated(summed, lanes, first_lane, experts, where_ref, order)
        out_ref[:, order * half_hidden : (order + 1) * half_hidden] = hidden


def run_hidden(where, row_blocks, gain_blocks, own, near, far, direct, before, first_lane, experts):
    blocks = len(row_blocks)
    count = sum(block.shape[0] for block in row_blocks)
    _, width, columns = own.shape
    inputs = [*row_blocks, *gain_blocks, own, *near, *far, *direct, *before]
    return pl.pallas_call(
        functools.partial(
            hidden_kernel, blocks, len(gain_blocks), len(near), len(direct), first_lane, experts
        ),
        out_shape=jax.ShapeDtypeStruct((count, columns), jnp.bfloat16),
        in_specs=[pl.BlockSpec(memory_space=pltpu.SMEM)]
        + [pl.BlockSpec(memory_space=pltpu.HBM)] * len(inputs),
        out_specs=pl.BlockSpec(memory_space=pltpu.VMEM),
        scratch_shapes=[
            pltpu.VMEM((count, 2 * width), jnp.bfloat16),
            pltpu.VMEM((count, LANES), jnp.bfloat16),
            pltpu.VMEM((2, 2 * width, columns), jnp.bfloat16),
            pltpu.SemaphoreType.DMA((3, max(2 * blocks, 2 + len(near)))),
        ],
        compiler_params=pltpu.CompilerParams(vmem_limit_bytes=20 * 1024 * 1024),
        cost_estimate=pl.CostEstimate(
            flops=8 * count * width * columns,
            bytes_accessed=4 * width * (count + 2 * columns),
            transcendentals=count * columns,
        ),
    )(where, *inputs)


def down_kernel(halves, chunks, where_ref, hidden_ref, *refs):
    refs = list(refs)
    take = lambda count: [refs.pop(0) for _ in range(count)]
    chunk_refs = [take(chunks), take(chunks)]
    weights, sems = refs[-2:]
    out_refs, whole_refs = refs[-2 - len(halves) : -2], refs[: -2 - len(halves)]
    depth = weights.shape[0] // 2
    pairs = []
    for order in range(2):
        expert = (where_ref[1] + order) % 2
        parts = chunk_refs[order] + [ref.at[expert] for ref in whole_refs]
        pairs += chunk_pairs(parts, weights, order * depth)
    for copy in load(pairs, sems):
        copy.wait()
    rows = hidden_ref.shape[0] // 2
    for half, out_ref in zip(halves, out_refs):
        out_ref[...] = jnp.dot(
            hidden_ref[half * rows : (half + 1) * rows, :],
            weights[...],
            preferred_element_type=jnp.float32,
        ).astype(jnp.bfloat16)


def run_down(where, hidden, near, far, whole, halves=(0, 1)):
    count, depth = hidden.shape
    inputs = [*near, *far, *whole]
    columns = inputs[0].shape[-1]
    outs = len(halves)
    return pl.pallas_call(
        functools.partial(down_kernel, halves, len(near)),
        out_shape=(jax.ShapeDtypeStruct((count // 2, columns), jnp.bfloat16),) * outs,
        in_specs=[pl.BlockSpec(memory_space=pltpu.SMEM), pl.BlockSpec(memory_space=pltpu.VMEM)]
        + [pl.BlockSpec(memory_space=pltpu.HBM)] * len(inputs),
        out_specs=(pl.BlockSpec(memory_space=pltpu.VMEM),) * outs,
        scratch_shapes=[
            pltpu.VMEM((depth, columns), jnp.bfloat16),
            pltpu.SemaphoreType.DMA((2 * (len(near) + len(whole)),)),
        ],
        compiler_params=pltpu.CompilerParams(vmem_limit_bytes=16 * 1024 * 1024),
        cost_estimate=pl.CostEstimate(
            flops=outs * count * depth * columns,
            bytes_accessed=2 * depth * (count + columns) + outs * count * columns,
            transcendentals=0,
        ),
    )(where, hidden, *inputs)


def over_replica(array):
    return lax.ppermute(array, "replica", SWAP)


def over_groups(array):
    return lax.ppermute(array, "groups", SWAP)


def over_expert(array, distance):
    return lax.ppermute(
        array, "expert", [(at, at ^ distance) for at in range(lax.axis_size("expert"))]
    )


def after(array, *others):
    return lax.optimization_barrier((array, *others))[0] if others else array


def send(weights, group, first_row, rows, *before):
    piece = lax.dynamic_slice(weights, (group, first_row, 0), (1, rows, weights.shape[2]))[0]
    return over_replica(after(piece, *before))


def over_both(array, distance):
    owners = lax.axis_size("expert")
    pairs = [
        (2 * at + replica, 2 * (at ^ distance) + 1 - replica)
        for at in range(owners)
        for replica in range(2)
    ]
    return lax.ppermute(array, ("expert", "replica"), pairs)


def chip_sums(mine, other, cross=False):
    owners = lax.axis_size("expert")
    rows = mine.shape[0] // (owners // 2)
    terms = []
    for index in range(owners // 2):
        part = slice(index * rows, (index + 1) * rows)
        chip = mine[part].astype(jnp.float32) + other[part].astype(jnp.float32)
        if cross or index:
            chip = (over_both if cross else over_expert)(chip.astype(jnp.bfloat16), 2 * index)
        terms.append(chip)
    return terms


def spread_sums(mine, away, cross=False):
    return chip_sums(mine, over_expert(away, 1), cross)


def add_up(terms):
    return sum(term.astype(jnp.float32) for term in terms).astype(jnp.bfloat16)


def in_order(replica, own, other, axis):
    return jnp.concatenate(
        [jnp.where(replica == 0, own, other), jnp.where(replica == 0, other, own)], axis=axis
    )


def dense_on_device(
    hidden_in,
    routes,
    route_gain,
    w_in,
    w_out,
    handoff,
    speaking,
    talker_routes,
    talker_gain,
    talker_w_in,
    talker_w_out,
):
    replica, group = lax.axis_index("replica"), lax.axis_index("groups")
    where = jnp.stack([lax.axis_index("expert"), group, replica]).astype(jnp.int32)
    owners = lax.axis_size("expert")
    experts = w_in.shape[0] * owners
    rows = routes.shape[0] // 2
    distances = range(2, owners, 2)

    width = w_in.shape[1]
    ends = [0, width * 3 // 8, width * 13 // 16]

    lanes = gain_lanes(
        where, experts, routes, route_gain, speaking, talker_routes, talker_gain
    )
    give = lax.dynamic_slice_in_dim(hidden_in, (1 - replica) * rows, rows, 0)
    other = over_replica(give)
    near_in = [send(w_in, group, a, b - a, other) for a, b in zip(ends, ends[1:])]
    row = build_row(where, hidden_in, other, lanes)
    same = [row] + [over_expert(row, distance) for distance in distances]
    far_in = [over_groups(after(near_in[0], same[1]))]
    far_in.append(over_groups(near_in[1]))
    direct_in = over_replica(after(w_in[:, ends[2] :], near_in[0]))
    across = [over_expert(after(row, far_in[0]), 1), over_expert(jnp.concatenate(same[1:]), 1)]
    blocks = same + across
    early = run_early(where, blocks, w_in, near_in, far_in[0])
    hidden = run_late(where, early, far_in[1], direct_in, experts)
    other_hidden = over_replica(hidden)
    own = spread_sums(*run_down(where, hidden, [], [], [w_out]))
    other_hidden = after(other_hidden, *own[1:])
    (got_away,) = run_down(where, other_hidden, [], [], [w_out], (1,))
    other_hidden = after(other_hidden, got_away)
    (got_mine,) = run_down(where, other_hidden, [], [], [w_out], (0,))
    got_away = over_expert(got_away, 1)
    half = talker_w_in.shape[1] // 2
    near_talker_in = [send(talker_w_in, group, first, half, got_mine) for first in (0, half)]
    got = chip_sums(got_mine, got_away)
    far_talker_in = [over_groups(near_talker_in[0])]
    far_talker_in.append(over_groups(after(near_talker_in[1], far_talker_in[0])))
    got, own = add_up(got), add_up(own)
    thinker_out = in_order(replica, own, got, 0)

    def handed(array):
        return jnp.dot(array, handoff, preferred_element_type=jnp.float32)

    term = over_replica(handed(got).astype(jnp.bfloat16))
    direct_talker_out = over_replica(after(talker_w_out, term))
    talker_row = (handed(own) + term.astype(jnp.float32)).astype(jnp.bfloat16)
    parts = jnp.split(talker_row, 2, axis=1)
    talker_row = in_order(replica, parts[0], parts[1], 1)
    same = [talker_row] + [over_expert(talker_row, distance) for distance in distances]
    rest = after(jnp.concatenate(same[1:]), far_talker_in[1])
    talker_blocks = same + [over_expert(talker_row, 1), over_expert(rest, 1)]
    hidden = run_hidden(
        where,
        talker_blocks,
        blocks,
        talker_w_in,
        near_talker_in,
        far_talker_in,
        [],
        [],
        2 * experts,
        experts,
    )
    give = run_down(where, hidden, [], [], [direct_talker_out])
    got = add_up(spread_sums(*give, cross=True))
    own = run_down(where, after(hidden, *give), [], [], [talker_w_out])
    own = add_up(spread_sums(*own))
    return (thinker_out, in_order(replica, own, got, 0))


def on_device(*arrays):
    token_count, top_count = arrays[1].shape
    local_experts = arrays[3].shape[0]
    experts = local_experts * lax.axis_size("expert")
    dense = (
        token_count * top_count * 2 // experts >= token_count
        and 4 * experts <= LANES
        and lax.axis_size("replica") == lax.axis_size("groups") == local_experts == 2
        and lax.axis_size("expert") in (2, 4, 8, 16)
    )
    return (dense_on_device if dense else routed_on_device)(*arrays)


def solution(mesh):
    return jax.shard_map(
        on_device,
        mesh=mesh,
        in_specs=(
            P(("groups", "expert"), "replica"),
            P(("groups", "expert"), None),
            P(("groups", "expert"), None),
            P("expert", "replica", None),
            P("expert", None, "replica"),
            P("replica", None),
            P(("groups", "expert")),
            P(("groups", "expert"), None),
            P(("groups", "expert"), None),
            P("expert", "replica", None),
            P("expert", None, "replica"),
        ),
        out_specs=(P(("groups", "expert"), "replica"), P(("groups", "expert"), "replica")),
        check_vma=False,
    )
```

```python
import functools

import jax
import jax.numpy as jnp
from jax import lax
from jax.experimental import pallas as pl
from jax.experimental.pallas import tpu as pltpu
from jax.sharding import PartitionSpec as P

LANES = 128
SWAP = [(0, 1), (1, 0)]


def place_rows(tok_rows, flat_ids, live_rows, experts, capacity):
    onehot = (flat_ids[:, None] == lax.iota(jnp.int32, experts)[None, :]).astype(
        jnp.int32
    ) * live_rows[:, None]
    before = jnp.cumsum(onehot, axis=0) - onehot
    slot_rank = jnp.sum(before * onehot, axis=1)
    slot_index = jnp.where(live_rows > 0, flat_ids * capacity + slot_rank, experts * capacity)
    buffer = (
        jnp.zeros((experts * capacity, tok_rows.shape[1]), tok_rows.dtype)
        .at[slot_index]
        .set(tok_rows, mode="drop")
    )
    return (buffer, slot_index)


def activate(gate_sum, up_sum):
    return (jax.nn.silu(gate_sum) * up_sum).astype(jnp.bfloat16)


def down_rows(second_weights, piece):
    return jnp.einsum("lrf,lfd->lrd", piece, second_weights, preferred_element_type=jnp.float32)


def routed_on_device(
    hidden_in,
    routes,
    route_gain,
    w_in,
    w_out,
    handoff,
    speaking,
    talker_routes,
    talker_gain,
    talker_w_in,
    talker_w_out,
):
    owners = lax.axis_size("expert")
    token_count, top_count = routes.shape
    local_experts = w_in.shape[0]
    experts = local_experts * owners
    capacity = max(2, token_count * top_count * 2 // experts)
    talker_capacity = max(2, capacity * 3 // 4)
    flat_ids = routes.reshape(-1)
    all_rows = jnp.ones_like(flat_ids)
    spread = jnp.repeat(hidden_in, top_count, axis=0)
    buffer, slot_index = place_rows(spread, flat_ids, all_rows, experts, capacity)
    arrived = lax.all_to_all(
        buffer.reshape(owners, local_experts, capacity, -1),
        "expert",
        split_axis=0,
        concat_axis=2,
        tiled=True,
    )
    partial_value = jnp.einsum("lrd,ldf->lrf", arrived[0], w_in, preferred_element_type=jnp.float32)
    hidden_width = w_in.shape[2] // 2
    share_sum = lax.psum_scatter(
        partial_value.astype(jnp.bfloat16), "replica", scatter_dimension=1, tiled=True
    ).astype(jnp.float32)
    hidden = activate(share_sum[:, :, :hidden_width], share_sum[:, :, hidden_width:])
    expert_out = down_rows(w_out, lax.all_gather(hidden, "replica", axis=1, tiled=True))
    returned = lax.all_to_all(
        expert_out.astype(jnp.bfloat16)[None], "expert", split_axis=2, concat_axis=0, tiled=True
    )
    returned = returned.reshape(experts * capacity, -1)
    picked = returned[slot_index].astype(jnp.float32).reshape(token_count, top_count, -1)
    thinker_out = jnp.sum(picked * route_gain[:, :, None], axis=1).astype(jnp.bfloat16)
    handoff_terms = jnp.dot(thinker_out, handoff, preferred_element_type=jnp.float32)
    talker_in = lax.psum_scatter(
        handoff_terms.astype(jnp.bfloat16), "replica", scatter_dimension=1, tiled=True
    )
    talker_ids = talker_routes.reshape(-1)
    speak_rows = jnp.repeat(speaking, top_count)
    talker_spread = jnp.repeat(talker_in, top_count, axis=0)
    talker_buffer, talker_slots = place_rows(
        talker_spread, talker_ids, speak_rows, experts, talker_capacity
    )
    talker_arrived = lax.all_to_all(
        talker_buffer.reshape(owners, local_experts, talker_capacity, -1),
        "expert",
        split_axis=0,
        concat_axis=2,
        tiled=True,
    )
    talker_partial = jnp.einsum(
        "lrd,ldf->lrf", talker_arrived[0], talker_w_in, preferred_element_type=jnp.float32
    )
    talker_hidden_width = talker_w_in.shape[2] // 2
    talker_share = lax.psum_scatter(
        talker_partial.astype(jnp.bfloat16), "replica", scatter_dimension=1, tiled=True
    ).astype(jnp.float32)
    talker_hidden = activate(
        talker_share[:, :, :talker_hidden_width], talker_share[:, :, talker_hidden_width:]
    )
    talker_expert_out = down_rows(
        talker_w_out, lax.all_gather(talker_hidden, "replica", axis=1, tiled=True)
    )
    talker_returned = lax.all_to_all(
        talker_expert_out.astype(jnp.bfloat16)[None],
        "expert",
        split_axis=2,
        concat_axis=0,
        tiled=True,
    )
    talker_returned = talker_returned.reshape(experts * talker_capacity, -1)
    safe_slots = jnp.minimum(talker_slots, experts * talker_capacity - 1)
    talker_picked = (
        talker_returned[safe_slots].astype(jnp.float32).reshape(token_count, top_count, -1)
    )
    talker_weights = talker_gain * speak_rows.reshape(token_count, top_count).astype(jnp.float32)
    talker_out = jnp.sum(talker_picked * talker_weights[:, :, None], axis=1).astype(jnp.bfloat16)
    return (thinker_out, talker_out)


def lanes_kernel(experts, where_ref, *refs):
    sources, out_ref, places, (lanes, sems) = refs[:5], refs[5], refs[6:11], refs[11:]
    for copy in load(list(zip(sources, places)), sems):
        copy.wait()
    routes_ref, gain_ref, live_ref, talker_routes_ref, talker_gain_ref = places
    rows = out_ref.shape[0]
    stack = []
    live = live_ref[...].astype(jnp.float32)
    for ids, gains in ((routes_ref, gain_ref[...]), (talker_routes_ref, talker_gain_ref[...] * live)):
        expert = lax.broadcasted_iota(jnp.int32, (experts, ids.shape[1]), 0)
        dense = jnp.zeros(expert.shape, jnp.float32)
        for choice in range(ids.shape[0]):
            dense += jnp.where(
                ids[choice : choice + 1, :] == expert, gains[choice : choice + 1, :], 0.0
            )
        high = dense.astype(jnp.bfloat16).astype(jnp.float32)
        stack += [high, dense - high]
    stack.append(jnp.zeros((LANES - 4 * experts, live.shape[1]), jnp.float32))
    lanes[...] = jnp.concatenate(stack, axis=0).T
    first = pl.multiple_of(where_ref[2] * rows, rows)
    out_ref[...] = lanes[pl.ds(first, rows), :].astype(jnp.bfloat16)


def gain_lanes(where, experts, routes, gain, live, talker_routes, talker_gain):
    count = routes.shape[0]
    inputs = [routes.T, gain.T, live[None], talker_routes.T, talker_gain.T]
    return pl.pallas_call(
        functools.partial(lanes_kernel, experts),
        out_shape=jax.ShapeDtypeStruct((count // 2, LANES), jnp.bfloat16),
        in_specs=[pl.BlockSpec(memory_space=pltpu.SMEM)]
        + [pl.BlockSpec(memory_space=pltpu.HBM)] * len(inputs),
        out_specs=pl.BlockSpec(memory_space=pltpu.VMEM),
        scratch_shapes=[pltpu.VMEM(array.shape, array.dtype) for array in inputs]
        + [pltpu.VMEM((count, LANES), jnp.float32), pltpu.SemaphoreType.DMA((len(inputs),))],
        compiler_params=pltpu.CompilerParams(vmem_limit_bytes=4 * 1024 * 1024),
        cost_estimate=pl.CostEstimate(
            flops=1 << 30, bytes_accessed=64 * count * LANES, transcendentals=0
        ),
    )(where, *inputs)


def row_kernel(where_ref, hidden_ref, other_ref, lanes_ref, out_ref):
    rows, width = other_ref.shape
    first = pl.multiple_of(where_ref[2] * rows, rows)
    out_ref[:, :width] = hidden_ref[pl.ds(first, rows), :]
    out_ref[:, width : 2 * width] = other_ref[...]
    out_ref[:, 2 * width :] = lanes_ref[...]


def build_row(where, hidden_in, other, lanes):
    rows, width = other.shape
    return pl.pallas_call(
        row_kernel,
        out_shape=jax.ShapeDtypeStruct((rows, 2 * width + LANES), jnp.bfloat16),
        in_specs=[pl.BlockSpec(memory_space=pltpu.SMEM)]
        + [pl.BlockSpec(memory_space=pltpu.VMEM)] * 3,
        out_specs=pl.BlockSpec(memory_space=pltpu.VMEM),
        compiler_params=pltpu.CompilerParams(vmem_limit_bytes=4 * 1024 * 1024),
        cost_estimate=pl.CostEstimate(flops=0, bytes_accessed=8 * rows * width, transcendentals=0),
    )(where, hidden_in, other, lanes)


def load(pairs, sems):
    copies = [
        pltpu.make_async_copy(source, destination, sems.at[index])
        for index, (source, destination) in enumerate(pairs)
    ]
    for copy in copies:
        copy.start()
    return copies


def chunk_pairs(chunks, place, first_row=0):
    pairs, row = [], first_row
    for chunk in chunks:
        pairs.append((chunk, place.at[pl.ds(row, chunk.shape[0])]))
        row += chunk.shape[0]
    return pairs


def gated(summed, lanes, first_lane, experts, where_ref, order):
    half = summed.shape[1] // 2
    expert = where_ref[0] * 2 + (where_ref[1] + order) % 2
    offset = lax.broadcasted_iota(jnp.int32, lanes.shape, 1) - first_lane - expert
    gain = jnp.sum(
        jnp.where((offset == 0) | (offset == experts), lanes, 0.0), axis=1, keepdims=True
    )
    return (jax.nn.silu(summed[:, :half]) * summed[:, half:] * gain).astype(jnp.bfloat16)


def early_kernel(blocks, where_ref, *refs):
    row_refs, refs = refs[:blocks], refs[blocks:]
    own_ref, near_refs, far_ref, sums_ref, late_ref, lanes_ref, rows, weights, sems = (
        refs[0], refs[1:3], *refs[3:]
    )
    width, late = own_ref.shape[1], late_ref.shape[1]
    early = rows.shape[1] - late
    group = where_ref[1]
    pairs = chunk_pairs([ref.at[:, pl.ds(0, 2 * width)] for ref in row_refs], rows)
    pairs += chunk_pairs([ref.at[:, pl.ds(2 * width, LANES)] for ref in row_refs], lanes_ref)
    pairs += chunk_pairs([own_ref.at[group], *near_refs], weights.at[0])
    pairs += chunk_pairs([own_ref.at[1 - group], far_ref], weights.at[1])
    for copy in load(pairs, sems):
        copy.wait()
    late_ref[...] = rows[:, early:]
    near = early + near_refs[1].shape[0]
    padded = weights.shape[1]
    if padded > near:
        weights[0, near:] = jnp.zeros((padded - near, weights.shape[2]), jnp.bfloat16)
    for order, depth in enumerate((padded, early)):
        sums_ref[order] = jnp.dot(
            rows[:, :depth], weights[order, :depth], preferred_element_type=jnp.float32
        )


def run_early(where, row_blocks, own, near, far):
    blocks, count = len(row_blocks), sum(block.shape[0] for block in row_blocks)
    _, width, columns = own.shape
    chunk = far.shape[0]
    late = width - chunk
    inputs = [*row_blocks, own, *near, far]
    return pl.pallas_call(
        functools.partial(early_kernel, blocks),
        out_shape=(
            jax.ShapeDtypeStruct((2, count, columns), jnp.float32),
            jax.ShapeDtypeStruct((count, late), jnp.bfloat16),
            jax.ShapeDtypeStruct((count, LANES), jnp.bfloat16),
        ),
        in_specs=[pl.BlockSpec(memory_space=pltpu.SMEM)]
        + [pl.BlockSpec(memory_space=pltpu.HBM)] * len(inputs),
        out_specs=(pl.BlockSpec(memory_space=pltpu.VMEM),) * 3,
        scratch_shapes=[
            pltpu.VMEM((count, 2 * width), jnp.bfloat16),
            pltpu.VMEM((2, pl.cdiv(width + chunk + near[1].shape[0], LANES) * LANES, columns), jnp.bfloat16),
            pltpu.SemaphoreType.DMA((2 * blocks + 5,)),
        ],
        compiler_params=pltpu.CompilerParams(vmem_limit_bytes=18 * 1024 * 1024),
        cost_estimate=pl.CostEstimate(
            flops=2 * count * (2 * width + 3 * chunk) * columns,
            bytes_accessed=4 * count * width + 2 * (2 * width + 3 * chunk) * columns,
            transcendentals=0,
        ),
    )(where, *inputs)


def late_kernel(experts, where_ref, sums_ref, late_ref, lanes_ref, far_ref, direct_ref, out_ref, weights, sems):
    chunk, rest = far_ref.shape[0], direct_ref.shape[1]
    half = sums_ref.shape[2] // 2
    group = where_ref[1]
    pairs = [
        (direct_ref.at[group], weights.at[0, pl.ds(chunk, rest)]),
        (far_ref, weights.at[1, pl.ds(0, chunk)]),
        (direct_ref.at[1 - group], weights.at[1, pl.ds(chunk, rest)]),
    ]
    copies = load(pairs, sems)
    aligned = chunk // LANES * LANES
    if chunk > aligned:
        weights[0, aligned:chunk] = jnp.zeros((chunk - aligned, weights.shape[2]), jnp.bfloat16)
    lanes = lanes_ref[...].astype(jnp.float32)
    for order, (first, needed) in enumerate(((aligned, copies[:1]), (0, copies[1:]))):
        for copy in needed:
            copy.wait()
        summed = sums_ref[order] + jnp.dot(
            late_ref[:, first:], weights[order, first:], preferred_element_type=jnp.float32
        )
        out_ref[:, order * half : (order + 1) * half] = gated(
            summed, lanes, 0, experts, where_ref, order
        )


def run_late(where, early, far, direct, experts):
    sums, late, lanes = early
    _, count, columns = sums.shape
    return pl.pallas_call(
        functools.partial(late_kernel, experts),
        out_shape=jax.ShapeDtypeStruct((count, columns), jnp.bfloat16),
        in_specs=[pl.BlockSpec(memory_space=pltpu.SMEM)]
        + [pl.BlockSpec(memory_space=pltpu.VMEM)] * 3
        + [pl.BlockSpec(memory_space=pltpu.HBM)] * 2,
        out_specs=pl.BlockSpec(memory_space=pltpu.VMEM),
        scratch_shapes=[
            pltpu.VMEM((2, late.shape[1], columns), jnp.bfloat16),
            pltpu.SemaphoreType.DMA((3,)),
        ],
        compiler_params=pltpu.CompilerParams(vmem_limit_bytes=10 * 1024 * 1024),
        cost_estimate=pl.CostEstimate(
            flops=4 * count * late.shape[1] * columns,
            bytes_accessed=8 * count * columns,
            transcendentals=count * columns,
        ),
    )(where, sums, late, lanes, far, direct)


def hidden_kernel(blocks, gain_blocks, chunks, direct, first_lane, experts, where_ref, *refs):
    refs = list(refs)
    take = lambda count: [refs.pop(0) for _ in range(count)]
    row_refs, gain_refs = take(blocks), take(gain_blocks)
    (own_ref,) = take(1)
    chunk_refs = [take(chunks), take(chunks)]
    direct_refs = take(direct)
    out_ref, rows, gains, weights, sems = refs[-5:]
    width = own_ref.shape[1]
    half_hidden = own_ref.shape[2] // 2
    lane_refs = [ref.at[:, pl.ds(ref.shape[1] - LANES, LANES)] for ref in gain_refs or row_refs]
    row_refs = [ref.at[:, pl.ds(0, 2 * width)] for ref in row_refs]
    row_copies = load(chunk_pairs(row_refs, rows) + chunk_pairs(lane_refs, gains), sems.at[0])
    weight_copies = []
    for order in range(2):
        expert = (where_ref[1] + order) % 2
        parts = [own_ref.at[expert], *chunk_refs[order]]
        parts += [ref.at[expert] for ref in direct_refs]
        weight_copies.append(load(chunk_pairs(parts, weights.at[order]), sems.at[1 + order]))
    for copy in row_copies:
        copy.wait()
    lanes = gains[...].astype(jnp.float32)
    for order in range(2):
        for copy in weight_copies[order]:
            copy.wait()
        summed = jnp.dot(rows[...], weights[order], preferred_element_type=jnp.float32)
        hidden = gated(summed, lanes, first_lane, experts, where_ref, order)
        out_ref[:, order * half_hidden : (order + 1) * half_hidden] = hidden


def run_hidden(where, row_blocks, gain_blocks, own, near, far, direct, before, first_lane, experts):
    blocks = len(row_blocks)
    count = sum(block.shape[0] for block in row_blocks)
    _, width, columns = own.shape
    inputs = [*row_blocks, *gain_blocks, own, *near, *far, *direct, *before]
    return pl.pallas_call(
        functools.partial(
            hidden_kernel, blocks, len(gain_blocks), len(near), len(direct), first_lane, experts
        ),
        out_shape=jax.ShapeDtypeStruct((count, columns), jnp.bfloat16),
        in_specs=[pl.BlockSpec(memory_space=pltpu.SMEM)]
        + [pl.BlockSpec(memory_space=pltpu.HBM)] * len(inputs),
        out_specs=pl.BlockSpec(memory_space=pltpu.VMEM),
        scratch_shapes=[
            pltpu.VMEM((count, 2 * width), jnp.bfloat16),
            pltpu.VMEM((count, LANES), jnp.bfloat16),
            pltpu.VMEM((2, 2 * width, columns), jnp.bfloat16),
            pltpu.SemaphoreType.DMA((3, max(2 * blocks, 2 + len(near)))),
        ],
        compiler_params=pltpu.CompilerParams(vmem_limit_bytes=12 * 1024 * 1024),
        cost_estimate=pl.CostEstimate(
            flops=8 * count * width * columns,
            bytes_accessed=4 * width * (count + 2 * columns),
            transcendentals=count * columns,
        ),
    )(where, *inputs)


def down_kernel(halves, chunks, where_ref, hidden_ref, *refs):
    refs = list(refs)
    take = lambda count: [refs.pop(0) for _ in range(count)]
    chunk_refs = [take(chunks), take(chunks)]
    weights, sems = refs[-2:]
    out_refs, whole_refs = refs[-2 - len(halves) : -2], refs[: -2 - len(halves)]
    depth = weights.shape[0] // 2
    pairs = []
    for order in range(2):
        expert = (where_ref[1] + order) % 2
        parts = chunk_refs[order] + [ref.at[expert] for ref in whole_refs]
        pairs += chunk_pairs(parts, weights, order * depth)
    for copy in load(pairs, sems):
        copy.wait()
    rows = hidden_ref.shape[0] // 2
    for half, out_ref in zip(halves, out_refs):
        out_ref[...] = jnp.dot(
            hidden_ref[half * rows : (half + 1) * rows, :],
            weights[...],
            preferred_element_type=jnp.float32,
        ).astype(jnp.bfloat16)


def run_down(where, hidden, near, far, whole, halves=(0, 1)):
    count, depth = hidden.shape
    inputs = [*near, *far, *whole]
    columns = inputs[0].shape[-1]
    outs = len(halves)
    return pl.pallas_call(
        functools.partial(down_kernel, halves, len(near)),
        out_shape=(jax.ShapeDtypeStruct((count // 2, columns), jnp.bfloat16),) * outs,
        in_specs=[pl.BlockSpec(memory_space=pltpu.SMEM), pl.BlockSpec(memory_space=pltpu.VMEM)]
        + [pl.BlockSpec(memory_space=pltpu.HBM)] * len(inputs),
        out_specs=(pl.BlockSpec(memory_space=pltpu.VMEM),) * outs,
        scratch_shapes=[
            pltpu.VMEM((depth, columns), jnp.bfloat16),
            pltpu.SemaphoreType.DMA((2 * (len(near) + len(whole)),)),
        ],
        compiler_params=pltpu.CompilerParams(vmem_limit_bytes=8 * 1024 * 1024),
        cost_estimate=pl.CostEstimate(
            flops=outs * count * depth * columns,
            bytes_accessed=2 * depth * (count + columns) + outs * count * columns,
            transcendentals=0,
        ),
    )(where, hidden, *inputs)


def over_replica(array):
    return lax.ppermute(array, "replica", SWAP)


def over_groups(array):
    return lax.ppermute(array, "groups", SWAP)


def over_expert(array, distance):
    return lax.ppermute(
        array, "expert", [(at, at ^ distance) for at in range(lax.axis_size("expert"))]
    )


def after(array, *others):
    return lax.optimization_barrier((array, *others))[0] if others else array


def send(weights, group, first_row, rows, *before):
    piece = lax.dynamic_slice(weights, (group, first_row, 0), (1, rows, weights.shape[2]))[0]
    return over_replica(after(piece, *before))


def over_both(array, distance):
    owners = lax.axis_size("expert")
    pairs = [
        (2 * at + replica, 2 * (at ^ distance) + 1 - replica)
        for at in range(owners)
        for replica in range(2)
    ]
    return lax.ppermute(array, ("expert", "replica"), pairs)


def chip_sums(mine, other, cross=False):
    owners = lax.axis_size("expert")
    rows = mine.shape[0] // (owners // 2)
    terms = []
    for index in range(owners // 2):
        part = slice(index * rows, (index + 1) * rows)
        chip = mine[part].astype(jnp.float32) + other[part].astype(jnp.float32)
        if cross or index:
            chip = (over_both if cross else over_expert)(chip.astype(jnp.bfloat16), 2 * index)
        terms.append(chip)
    return terms


def spread_sums(mine, away, cross=False):
    return chip_sums(mine, over_expert(away, 1), cross)


def add_up(terms):
    return sum(term.astype(jnp.float32) for term in terms).astype(jnp.bfloat16)


def gather_blocks(row, *hold):
    blocks, step = {0: row}, lax.axis_size("expert") // 2
    while step > 1:
        for at, block in list(blocks.items()):
            blocks[at + step] = over_expert(after(block, *hold) if at else block, step)
        step //= 2
    return [blocks[at] for at in sorted(blocks)]


def in_order(replica, own, other, axis):
    return jnp.concatenate(
        [jnp.where(replica == 0, own, other), jnp.where(replica == 0, other, own)], axis=axis
    )


def dense_on_device(
    hidden_in,
    routes,
    route_gain,
    w_in,
    w_out,
    handoff,
    speaking,
    talker_routes,
    talker_gain,
    talker_w_in,
    talker_w_out,
):
    replica, group = lax.axis_index("replica"), lax.axis_index("groups")
    where = jnp.stack([lax.axis_index("expert"), group, replica]).astype(jnp.int32)
    owners = lax.axis_size("expert")
    experts = w_in.shape[0] * owners
    rows = routes.shape[0] // 2
    distances = range(2, owners, 2)

    width = w_in.shape[1]
    ends = [0, width * 3 // 8, width * 13 // 16]

    lanes = gain_lanes(
        where, experts, routes, route_gain, speaking, talker_routes, talker_gain
    )
    give = lax.dynamic_slice_in_dim(hidden_in, (1 - replica) * rows, rows, 0)
    other = over_replica(give)
    near_in = [send(w_in, group, 0, ends[1], other)]
    row = build_row(where, hidden_in, other, lanes)
    near_in.append(send(w_in, group, ends[1], ends[2] - ends[1], row))
    same = gather_blocks(row, near_in[0])
    far_in = [over_groups(after(near_in[0], row))]
    far_in.append(over_groups(near_in[1]))
    direct_in = over_replica(after(w_in[:, ends[2] :], near_in[0]))
    rest = after(jnp.concatenate(same[1:]), near_in[1])
    across = [over_expert(after(row, far_in[0]), 1), over_expert(rest, 1)]
    blocks = same + across
    early = run_early(where, blocks, w_in, near_in, far_in[0])
    hidden = run_late(where, early, far_in[1], direct_in, experts)
    other_hidden = over_replica(hidden)
    own = spread_sums(*run_down(where, hidden, [], [], [w_out]))
    other_hidden = after(other_hidden, *own[1:])
    (got_away,) = run_down(where, other_hidden, [], [], [w_out], (1,))
    other_hidden = after(other_hidden, got_away)
    (got_mine,) = run_down(where, other_hidden, [], [], [w_out], (0,))
    got_away = over_expert(got_away, 1)
    half = talker_w_in.shape[1] // 2
    near_talker_in = [send(talker_w_in, group, first, half, got_mine) for first in (0, half)]
    got = chip_sums(got_mine, got_away)
    far_talker_in = [over_groups(near_talker_in[0])]
    far_talker_in.append(over_groups(after(near_talker_in[1], far_talker_in[0])))
    got, own = add_up(got), add_up(own)
    thinker_out = in_order(replica, own, got, 0)

    def handed(array):
        return jnp.dot(array, handoff, preferred_element_type=jnp.float32)

    term = over_replica(handed(got).astype(jnp.bfloat16))
    direct_talker_out = over_replica(after(talker_w_out, term))
    talker_row = (handed(own) + term.astype(jnp.float32)).astype(jnp.bfloat16)
    parts = jnp.split(talker_row, 2, axis=1)
    talker_row = in_order(replica, parts[0], parts[1], 1)
    same = [talker_row] + [over_expert(talker_row, distance) for distance in distances]
    rest = after(jnp.concatenate(same[1:]), far_talker_in[1])
    talker_blocks = same + [over_expert(talker_row, 1), over_expert(rest, 1)]
    hidden = run_hidden(
        where,
        talker_blocks,
        blocks,
        talker_w_in,
        near_talker_in,
        far_talker_in,
        [],
        [],
        2 * experts,
        experts,
    )
    give = run_down(where, hidden, [], [], [direct_talker_out])
    got = add_up(spread_sums(*give, cross=True))
    own = run_down(where, after(hidden, *give), [], [], [talker_w_out])
    own = add_up(spread_sums(*own))
    return (thinker_out, in_order(replica, own, got, 0))


def on_device(*arrays):
    token_count, top_count = arrays[1].shape
    local_experts = arrays[3].shape[0]
    experts = local_experts * lax.axis_size("expert")
    dense = (
        token_count * top_count * 2 // experts >= token_count
        and 4 * experts <= LANES
        and lax.axis_size("replica") == lax.axis_size("groups") == local_experts == 2
        and lax.axis_size("expert") in (2, 4, 8, 16)
    )
    return (dense_on_device if dense else routed_on_device)(*arrays)


def solution(mesh):
    return jax.shard_map(
        on_device,
        mesh=mesh,
        in_specs=(
            P(("groups", "expert"), "replica"),
            P(("groups", "expert"), None),
            P(("groups", "expert"), None),
            P("expert", "replica", None),
            P("expert", None, "replica"),
            P("replica", None),
            P(("groups", "expert")),
            P(("groups", "expert"), None),
            P(("groups", "expert"), None),
            P("expert", "replica", None),
            P("expert", None, "replica"),
        ),
        out_specs=(P(("groups", "expert"), "replica"), P(("groups", "expert"), "replica")),
        check_vma=False,
    )
```

```python
import functools

import jax
import jax.numpy as jnp
from jax import lax
from jax.experimental import pallas as pl
from jax.experimental.pallas import tpu as pltpu
from jax.sharding import PartitionSpec as P

LANES = 128
SWAP = [(0, 1), (1, 0)]


def place_rows(tok_rows, flat_ids, live_rows, experts, capacity):
    onehot = (flat_ids[:, None] == lax.iota(jnp.int32, experts)[None, :]).astype(
        jnp.int32
    ) * live_rows[:, None]
    before = jnp.cumsum(onehot, axis=0) - onehot
    slot_rank = jnp.sum(before * onehot, axis=1)
    slot_index = jnp.where(live_rows > 0, flat_ids * capacity + slot_rank, experts * capacity)
    buffer = (
        jnp.zeros((experts * capacity, tok_rows.shape[1]), tok_rows.dtype)
        .at[slot_index]
        .set(tok_rows, mode="drop")
    )
    return (buffer, slot_index)


def activate(gate_sum, up_sum):
    return (jax.nn.silu(gate_sum) * up_sum).astype(jnp.bfloat16)


def down_rows(second_weights, piece):
    return jnp.einsum("lrf,lfd->lrd", piece, second_weights, preferred_element_type=jnp.float32)


def routed_on_device(
    hidden_in,
    routes,
    route_gain,
    w_in,
    w_out,
    handoff,
    speaking,
    talker_routes,
    talker_gain,
    talker_w_in,
    talker_w_out,
):
    owners = lax.axis_size("expert")
    token_count, top_count = routes.shape
    local_experts = w_in.shape[0]
    experts = local_experts * owners
    capacity = max(2, token_count * top_count * 2 // experts)
    talker_capacity = max(2, capacity * 3 // 4)
    flat_ids = routes.reshape(-1)
    all_rows = jnp.ones_like(flat_ids)
    spread = jnp.repeat(hidden_in, top_count, axis=0)
    buffer, slot_index = place_rows(spread, flat_ids, all_rows, experts, capacity)
    arrived = lax.all_to_all(
        buffer.reshape(owners, local_experts, capacity, -1),
        "expert",
        split_axis=0,
        concat_axis=2,
        tiled=True,
    )
    partial_value = jnp.einsum("lrd,ldf->lrf", arrived[0], w_in, preferred_element_type=jnp.float32)
    hidden_width = w_in.shape[2] // 2
    share_sum = lax.psum_scatter(
        partial_value.astype(jnp.bfloat16), "replica", scatter_dimension=1, tiled=True
    ).astype(jnp.float32)
    hidden = activate(share_sum[:, :, :hidden_width], share_sum[:, :, hidden_width:])
    expert_out = down_rows(w_out, lax.all_gather(hidden, "replica", axis=1, tiled=True))
    returned = lax.all_to_all(
        expert_out.astype(jnp.bfloat16)[None], "expert", split_axis=2, concat_axis=0, tiled=True
    )
    returned = returned.reshape(experts * capacity, -1)
    picked = returned[slot_index].astype(jnp.float32).reshape(token_count, top_count, -1)
    thinker_out = jnp.sum(picked * route_gain[:, :, None], axis=1).astype(jnp.bfloat16)
    handoff_terms = jnp.dot(thinker_out, handoff, preferred_element_type=jnp.float32)
    talker_in = lax.psum_scatter(
        handoff_terms.astype(jnp.bfloat16), "replica", scatter_dimension=1, tiled=True
    )
    talker_ids = talker_routes.reshape(-1)
    speak_rows = jnp.repeat(speaking, top_count)
    talker_spread = jnp.repeat(talker_in, top_count, axis=0)
    talker_buffer, talker_slots = place_rows(
        talker_spread, talker_ids, speak_rows, experts, talker_capacity
    )
    talker_arrived = lax.all_to_all(
        talker_buffer.reshape(owners, local_experts, talker_capacity, -1),
        "expert",
        split_axis=0,
        concat_axis=2,
        tiled=True,
    )
    talker_partial = jnp.einsum(
        "lrd,ldf->lrf", talker_arrived[0], talker_w_in, preferred_element_type=jnp.float32
    )
    talker_hidden_width = talker_w_in.shape[2] // 2
    talker_share = lax.psum_scatter(
        talker_partial.astype(jnp.bfloat16), "replica", scatter_dimension=1, tiled=True
    ).astype(jnp.float32)
    talker_hidden = activate(
        talker_share[:, :, :talker_hidden_width], talker_share[:, :, talker_hidden_width:]
    )
    talker_expert_out = down_rows(
        talker_w_out, lax.all_gather(talker_hidden, "replica", axis=1, tiled=True)
    )
    talker_returned = lax.all_to_all(
        talker_expert_out.astype(jnp.bfloat16)[None],
        "expert",
        split_axis=2,
        concat_axis=0,
        tiled=True,
    )
    talker_returned = talker_returned.reshape(experts * talker_capacity, -1)
    safe_slots = jnp.minimum(talker_slots, experts * talker_capacity - 1)
    talker_picked = (
        talker_returned[safe_slots].astype(jnp.float32).reshape(token_count, top_count, -1)
    )
    talker_weights = talker_gain * speak_rows.reshape(token_count, top_count).astype(jnp.float32)
    talker_out = jnp.sum(talker_picked * talker_weights[:, :, None], axis=1).astype(jnp.bfloat16)
    return (thinker_out, talker_out)


def lanes_kernel(experts, where_ref, *refs):
    sources, out_ref, places, (lanes, sems) = refs[:5], refs[5], refs[6:11], refs[11:]
    for copy in load(list(zip(sources, places)), sems):
        copy.wait()
    routes_ref, gain_ref, live_ref, talker_routes_ref, talker_gain_ref = places
    rows = out_ref.shape[0]
    stack = []
    live = live_ref[...].astype(jnp.float32)
    for ids, gains in ((routes_ref, gain_ref[...]), (talker_routes_ref, talker_gain_ref[...] * live)):
        expert = lax.broadcasted_iota(jnp.int32, (experts, ids.shape[1]), 0)
        dense = jnp.zeros(expert.shape, jnp.float32)
        for choice in range(ids.shape[0]):
            dense += jnp.where(
                ids[choice : choice + 1, :] == expert, gains[choice : choice + 1, :], 0.0
            )
        high = dense.astype(jnp.bfloat16).astype(jnp.float32)
        stack += [high, dense - high]
    stack.append(jnp.zeros((LANES - 4 * experts, live.shape[1]), jnp.float32))
    lanes[...] = jnp.concatenate(stack, axis=0).T
    first = pl.multiple_of(where_ref[2] * rows, rows)
    out_ref[...] = lanes[pl.ds(first, rows), :].astype(jnp.bfloat16)


def gain_lanes(where, experts, routes, gain, live, talker_routes, talker_gain):
    count = routes.shape[0]
    inputs = [routes.T, gain.T, live[None], talker_routes.T, talker_gain.T]
    return pl.pallas_call(
        functools.partial(lanes_kernel, experts),
        out_shape=jax.ShapeDtypeStruct((count // 2, LANES), jnp.bfloat16),
        in_specs=[pl.BlockSpec(memory_space=pltpu.SMEM)]
        + [pl.BlockSpec(memory_space=pltpu.HBM)] * len(inputs),
        out_specs=pl.BlockSpec(memory_space=pltpu.VMEM),
        scratch_shapes=[pltpu.VMEM(array.shape, array.dtype) for array in inputs]
        + [pltpu.VMEM((count, LANES), jnp.float32), pltpu.SemaphoreType.DMA((len(inputs),))],
        compiler_params=pltpu.CompilerParams(vmem_limit_bytes=4 * 1024 * 1024),
        cost_estimate=pl.CostEstimate(
            flops=1 << 30, bytes_accessed=64 * count * LANES, transcendentals=0
        ),
    )(where, *inputs)


def row_kernel(where_ref, hidden_ref, other_ref, lanes_ref, out_ref):
    rows, width = other_ref.shape
    first = pl.multiple_of(where_ref[2] * rows, rows)
    out_ref[:, :width] = hidden_ref[pl.ds(first, rows), :]
    out_ref[:, width : 2 * width] = other_ref[...]
    out_ref[:, 2 * width :] = lanes_ref[...]


def build_row(where, hidden_in, other, lanes):
    rows, width = other.shape
    return pl.pallas_call(
        row_kernel,
        out_shape=jax.ShapeDtypeStruct((rows, 2 * width + LANES), jnp.bfloat16),
        in_specs=[pl.BlockSpec(memory_space=pltpu.SMEM)]
        + [pl.BlockSpec(memory_space=pltpu.VMEM)] * 3,
        out_specs=pl.BlockSpec(memory_space=pltpu.VMEM),
        compiler_params=pltpu.CompilerParams(vmem_limit_bytes=4 * 1024 * 1024),
        cost_estimate=pl.CostEstimate(flops=0, bytes_accessed=8 * rows * width, transcendentals=0),
    )(where, hidden_in, other, lanes)


def load(pairs, sems):
    copies = [
        pltpu.make_async_copy(source, destination, sems.at[index])
        for index, (source, destination) in enumerate(pairs)
    ]
    for copy in copies:
        copy.start()
    return copies


def chunk_pairs(chunks, place, first_row=0):
    pairs, row = [], first_row
    for chunk in chunks:
        pairs.append((chunk, place.at[pl.ds(row, chunk.shape[0])]))
        row += chunk.shape[0]
    return pairs


def gated(summed, lanes, first_lane, experts, where_ref, order):
    half = summed.shape[1] // 2
    expert = where_ref[0] * 2 + (where_ref[1] + order) % 2
    offset = lax.broadcasted_iota(jnp.int32, lanes.shape, 1) - first_lane - expert
    gain = jnp.sum(
        jnp.where((offset == 0) | (offset == experts), lanes, 0.0), axis=1, keepdims=True
    )
    return (jax.nn.silu(summed[:, :half]) * summed[:, half:] * gain).astype(jnp.bfloat16)


def early_kernel(blocks, where_ref, *refs):
    row_refs, refs = refs[:blocks], refs[blocks:]
    own_ref, near_refs, far_ref, sums_ref, late_ref, lanes_ref, rows, weights, sems = (
        refs[0], refs[1:3], *refs[3:]
    )
    width, late = own_ref.shape[1], late_ref.shape[1]
    early = rows.shape[1] - late
    group = where_ref[1]
    pairs = chunk_pairs([ref.at[:, pl.ds(0, 2 * width)] for ref in row_refs], rows)
    pairs += chunk_pairs([ref.at[:, pl.ds(2 * width, LANES)] for ref in row_refs], lanes_ref)
    pairs += chunk_pairs([own_ref.at[group], *near_refs], weights.at[0])
    pairs += chunk_pairs([own_ref.at[1 - group], far_ref], weights.at[1])
    for copy in load(pairs, sems):
        copy.wait()
    late_ref[...] = rows[:, early:]
    near = early + near_refs[1].shape[0]
    padded = weights.shape[1]
    if padded > near:
        weights[0, near:] = jnp.zeros((padded - near, weights.shape[2]), jnp.bfloat16)
    for order, depth in enumerate((padded, early)):
        sums_ref[order] = jnp.dot(
            rows[:, :depth], weights[order, :depth], preferred_element_type=jnp.float32
        )


def run_early(where, row_blocks, own, near, far):
    blocks, count = len(row_blocks), sum(block.shape[0] for block in row_blocks)
    _, width, columns = own.shape
    chunk = far.shape[0]
    late = width - chunk
    inputs = [*row_blocks, own, *near, far]
    return pl.pallas_call(
        functools.partial(early_kernel, blocks),
        out_shape=(
            jax.ShapeDtypeStruct((2, count, columns), jnp.float32),
            jax.ShapeDtypeStruct((count, late), jnp.bfloat16),
            jax.ShapeDtypeStruct((count, LANES), jnp.bfloat16),
        ),
        in_specs=[pl.BlockSpec(memory_space=pltpu.SMEM)]
        + [pl.BlockSpec(memory_space=pltpu.HBM)] * len(inputs),
        out_specs=(pl.BlockSpec(memory_space=pltpu.VMEM),) * 3,
        scratch_shapes=[
            pltpu.VMEM((count, 2 * width), jnp.bfloat16),
            pltpu.VMEM((2, pl.cdiv(width + chunk + near[1].shape[0], LANES) * LANES, columns), jnp.bfloat16),
            pltpu.SemaphoreType.DMA((2 * blocks + 5,)),
        ],
        compiler_params=pltpu.CompilerParams(vmem_limit_bytes=18 * 1024 * 1024),
        cost_estimate=pl.CostEstimate(
            flops=2 * count * (2 * width + 3 * chunk) * columns,
            bytes_accessed=4 * count * width + 2 * (2 * width + 3 * chunk) * columns,
            transcendentals=0,
        ),
    )(where, *inputs)


def late_kernel(experts, where_ref, sums_ref, late_ref, lanes_ref, far_ref, direct_ref, out_ref, weights, sems):
    chunk, rest = far_ref.shape[0], direct_ref.shape[1]
    half = sums_ref.shape[2] // 2
    group = where_ref[1]
    pairs = [
        (direct_ref.at[group], weights.at[0, pl.ds(chunk, rest)]),
        (far_ref, weights.at[1, pl.ds(0, chunk)]),
        (direct_ref.at[1 - group], weights.at[1, pl.ds(chunk, rest)]),
    ]
    copies = load(pairs, sems)
    aligned = chunk // LANES * LANES
    if chunk > aligned:
        weights[0, aligned:chunk] = jnp.zeros((chunk - aligned, weights.shape[2]), jnp.bfloat16)
    lanes = lanes_ref[...].astype(jnp.float32)
    for order, (first, needed) in enumerate(((aligned, copies[:1]), (0, copies[1:]))):
        for copy in needed:
            copy.wait()
        summed = sums_ref[order] + jnp.dot(
            late_ref[:, first:], weights[order, first:], preferred_element_type=jnp.float32
        )
        out_ref[:, order * half : (order + 1) * half] = gated(
            summed, lanes, 0, experts, where_ref, order
        )


def run_late(where, early, far, direct, experts):
    sums, late, lanes = early
    _, count, columns = sums.shape
    return pl.pallas_call(
        functools.partial(late_kernel, experts),
        out_shape=jax.ShapeDtypeStruct((count, columns), jnp.bfloat16),
        in_specs=[pl.BlockSpec(memory_space=pltpu.SMEM)]
        + [pl.BlockSpec(memory_space=pltpu.VMEM)] * 3
        + [pl.BlockSpec(memory_space=pltpu.HBM)] * 2,
        out_specs=pl.BlockSpec(memory_space=pltpu.VMEM),
        scratch_shapes=[
            pltpu.VMEM((2, late.shape[1], columns), jnp.bfloat16),
            pltpu.SemaphoreType.DMA((3,)),
        ],
        compiler_params=pltpu.CompilerParams(vmem_limit_bytes=10 * 1024 * 1024),
        cost_estimate=pl.CostEstimate(
            flops=4 * count * late.shape[1] * columns,
            bytes_accessed=8 * count * columns,
            transcendentals=count * columns,
        ),
    )(where, sums, late, lanes, far, direct)


def hidden_kernel(blocks, gain_blocks, chunks, direct, first_lane, experts, where_ref, *refs):
    refs = list(refs)
    take = lambda count: [refs.pop(0) for _ in range(count)]
    row_refs, gain_refs = take(blocks), take(gain_blocks)
    (own_ref,) = take(1)
    chunk_refs = [take(chunks), take(chunks)]
    direct_refs = take(direct)
    out_ref, rows, gains, weights, sems = refs[-5:]
    width = own_ref.shape[1]
    half_hidden = own_ref.shape[2] // 2
    lane_refs = [ref.at[:, pl.ds(ref.shape[1] - LANES, LANES)] for ref in gain_refs or row_refs]
    row_refs = [ref.at[:, pl.ds(0, 2 * width)] for ref in row_refs]
    row_copies = load(chunk_pairs(row_refs, rows) + chunk_pairs(lane_refs, gains), sems.at[0])
    weight_copies = []
    for order in range(2):
        expert = (where_ref[1] + order) % 2
        parts = [own_ref.at[expert], *chunk_refs[order]]
        parts += [ref.at[expert] for ref in direct_refs]
        weight_copies.append(load(chunk_pairs(parts, weights.at[order]), sems.at[1 + order]))
    for copy in row_copies:
        copy.wait()
    lanes = gains[...].astype(jnp.float32)
    for order in range(2):
        for copy in weight_copies[order]:
            copy.wait()
        summed = jnp.dot(rows[...], weights[order], preferred_element_type=jnp.float32)
        hidden = gated(summed, lanes, first_lane, experts, where_ref, order)
        out_ref[:, order * half_hidden : (order + 1) * half_hidden] = hidden


def run_hidden(where, row_blocks, gain_blocks, own, near, far, direct, before, first_lane, experts):
    blocks = len(row_blocks)
    count = sum(block.shape[0] for block in row_blocks)
    _, width, columns = own.shape
    inputs = [*row_blocks, *gain_blocks, own, *near, *far, *direct, *before]
    return pl.pallas_call(
        functools.partial(
            hidden_kernel, blocks, len(gain_blocks), len(near), len(direct), first_lane, experts
        ),
        out_shape=jax.ShapeDtypeStruct((count, columns), jnp.bfloat16),
        in_specs=[pl.BlockSpec(memory_space=pltpu.SMEM)]
        + [pl.BlockSpec(memory_space=pltpu.HBM)] * len(inputs),
        out_specs=pl.BlockSpec(memory_space=pltpu.VMEM),
        scratch_shapes=[
            pltpu.VMEM((count, 2 * width), jnp.bfloat16),
            pltpu.VMEM((count, LANES), jnp.bfloat16),
            pltpu.VMEM((2, 2 * width, columns), jnp.bfloat16),
            pltpu.SemaphoreType.DMA((3, max(2 * blocks, 2 + len(near)))),
        ],
        compiler_params=pltpu.CompilerParams(vmem_limit_bytes=12 * 1024 * 1024),
        cost_estimate=pl.CostEstimate(
            flops=8 * count * width * columns,
            bytes_accessed=4 * width * (count + 2 * columns),
            transcendentals=count * columns,
        ),
    )(where, *inputs)


def down_kernel(halves, chunks, where_ref, hidden_ref, *refs):
    refs = list(refs)
    take = lambda count: [refs.pop(0) for _ in range(count)]
    chunk_refs = [take(chunks), take(chunks)]
    weights, sems = refs[-2:]
    out_refs, whole_refs = refs[-2 - len(halves) : -2], refs[: -2 - len(halves)]
    depth = weights.shape[0] // 2
    pairs = []
    for order in range(2):
        expert = (where_ref[1] + order) % 2
        parts = chunk_refs[order] + [ref.at[expert] for ref in whole_refs]
        pairs += chunk_pairs(parts, weights, order * depth)
    for copy in load(pairs, sems):
        copy.wait()
    rows = hidden_ref.shape[0] // 2
    for half, out_ref in zip(halves, out_refs):
        out_ref[...] = jnp.dot(
            hidden_ref[half * rows : (half + 1) * rows, :],
            weights[...],
            preferred_element_type=jnp.float32,
        ).astype(jnp.bfloat16)


def run_down(where, hidden, near, far, whole, halves=(0, 1)):
    count, depth = hidden.shape
    inputs = [*near, *far, *whole]
    columns = inputs[0].shape[-1]
    outs = len(halves)
    return pl.pallas_call(
        functools.partial(down_kernel, halves, len(near)),
        out_shape=(jax.ShapeDtypeStruct((count // 2, columns), jnp.bfloat16),) * outs,
        in_specs=[pl.BlockSpec(memory_space=pltpu.SMEM), pl.BlockSpec(memory_space=pltpu.VMEM)]
        + [pl.BlockSpec(memory_space=pltpu.HBM)] * len(inputs),
        out_specs=(pl.BlockSpec(memory_space=pltpu.VMEM),) * outs,
        scratch_shapes=[
            pltpu.VMEM((depth, columns), jnp.bfloat16),
            pltpu.SemaphoreType.DMA((2 * (len(near) + len(whole)),)),
        ],
        compiler_params=pltpu.CompilerParams(vmem_limit_bytes=8 * 1024 * 1024),
        cost_estimate=pl.CostEstimate(
            flops=outs * count * depth * columns,
            bytes_accessed=2 * depth * (count + columns) + outs * count * columns,
            transcendentals=0,
        ),
    )(where, hidden, *inputs)


def over_replica(array):
    return lax.ppermute(array, "replica", SWAP)


def over_groups(array):
    return lax.ppermute(array, "groups", SWAP)


def over_expert(array, distance):
    return lax.ppermute(
        array, "expert", [(at, at ^ distance) for at in range(lax.axis_size("expert"))]
    )


def after(array, *others):
    return lax.optimization_barrier((array, *others))[0] if others else array


def send(weights, group, first_row, rows, *before):
    piece = lax.dynamic_slice(weights, (group, first_row, 0), (1, rows, weights.shape[2]))[0]
    return over_replica(after(piece, *before))


def over_both(array, distance):
    owners = lax.axis_size("expert")
    pairs = [
        (2 * at + replica, 2 * (at ^ distance) + 1 - replica)
        for at in range(owners)
        for replica in range(2)
    ]
    return lax.ppermute(array, ("expert", "replica"), pairs)


def chip_sums(mine, other, cross=False):
    owners = lax.axis_size("expert")
    rows = mine.shape[0] // (owners // 2)
    terms = []
    for index in range(owners // 2):
        part = slice(index * rows, (index + 1) * rows)
        chip = mine[part].astype(jnp.float32) + other[part].astype(jnp.float32)
        if cross or index:
            chip = (over_both if cross else over_expert)(chip.astype(jnp.bfloat16), 2 * index)
        terms.append(chip)
    return terms


def spread_sums(mine, away, cross=False):
    return chip_sums(mine, over_expert(away, 1), cross)


def add_up(terms):
    return sum(term.astype(jnp.float32) for term in terms).astype(jnp.bfloat16)


def in_order(replica, own, other, axis):
    return jnp.concatenate(
        [jnp.where(replica == 0, own, other), jnp.where(replica == 0, other, own)], axis=axis
    )


def dense_on_device(
    hidden_in,
    routes,
    route_gain,
    w_in,
    w_out,
    handoff,
    speaking,
    talker_routes,
    talker_gain,
    talker_w_in,
    talker_w_out,
):
    replica, group = lax.axis_index("replica"), lax.axis_index("groups")
    where = jnp.stack([lax.axis_index("expert"), group, replica]).astype(jnp.int32)
    owners = lax.axis_size("expert")
    experts = w_in.shape[0] * owners
    rows = routes.shape[0] // 2
    distances = range(2, owners, 2)

    width = w_in.shape[1]
    ends = [0, width * 3 // 8, width * 13 // 16]

    lanes = gain_lanes(
        where, experts, routes, route_gain, speaking, talker_routes, talker_gain
    )
    give = lax.dynamic_slice_in_dim(hidden_in, (1 - replica) * rows, rows, 0)
    other = over_replica(give)
    near_in = [send(w_in, group, a, b - a, other, lanes) for a, b in zip(ends, ends[1:])]
    row = build_row(where, hidden_in, other, lanes)
    same = [row] + [over_expert(row, distance) for distance in distances]
    far_in = [over_groups(after(near_in[0], same[1])), over_groups(near_in[1])]
    direct_in = over_replica(after(w_in[:, ends[2] :], near_in[0]))
    across = [over_expert(after(row, far_in[0]), 1), over_expert(jnp.concatenate(same[1:]), 1)]
    blocks = same + across
    early = run_early(where, blocks, w_in, near_in, far_in[0])
    hidden = run_late(where, early, far_in[1], direct_in, experts)
    other_hidden = over_replica(hidden)
    own = spread_sums(*run_down(where, hidden, [], [], [w_out]))
    other_hidden = after(other_hidden, *own[1:])
    (got_away,) = run_down(where, other_hidden, [], [], [w_out], (1,))
    other_hidden = after(other_hidden, got_away)
    (got_mine,) = run_down(where, other_hidden, [], [], [w_out], (0,))
    got_away = over_expert(got_away, 1)
    half = talker_w_in.shape[1] // 2
    near_talker_in = [send(talker_w_in, group, first, half, got_mine) for first in (0, half)]
    got = chip_sums(got_mine, got_away)
    far_talker_in = [over_groups(near_talker_in[0])]
    far_talker_in.append(over_groups(after(near_talker_in[1], far_talker_in[0])))
    got, own = add_up(got), add_up(own)
    thinker_out = in_order(replica, own, got, 0)

    def handed(array):
        return jnp.dot(array, handoff, preferred_element_type=jnp.float32)

    term = over_replica(handed(got).astype(jnp.bfloat16))
    direct_talker_out = over_replica(after(talker_w_out, term))
    talker_row = (handed(own) + term.astype(jnp.float32)).astype(jnp.bfloat16)
    parts = jnp.split(talker_row, 2, axis=1)
    talker_row = in_order(replica, parts[0], parts[1], 1)
    same = [talker_row] + [over_expert(talker_row, distance) for distance in distances]
    rest = after(jnp.concatenate(same[1:]), far_talker_in[1])
    talker_blocks = same + [over_expert(talker_row, 1), over_expert(rest, 1)]
    hidden = run_hidden(
        where,
        talker_blocks,
        blocks,
        talker_w_in,
        near_talker_in,
        far_talker_in,
        [],
        [],
        2 * experts,
        experts,
    )
    give = run_down(where, hidden, [], [], [direct_talker_out])
    got = add_up(spread_sums(*give, cross=True))
    own = run_down(where, after(hidden, *give), [], [], [talker_w_out])
    own = add_up(spread_sums(*own))
    return (thinker_out, in_order(replica, own, got, 0))


def on_device(*arrays):
    token_count, top_count = arrays[1].shape
    local_experts = arrays[3].shape[0]
    experts = local_experts * lax.axis_size("expert")
    dense = (
        token_count * top_count * 2 // experts >= token_count
        and 4 * experts <= LANES
        and lax.axis_size("replica") == lax.axis_size("groups") == local_experts == 2
        and lax.axis_size("expert") in (2, 4, 8, 16)
    )
    return (dense_on_device if dense else routed_on_device)(*arrays)


def solution(mesh):
    return jax.shard_map(
        on_device,
        mesh=mesh,
        in_specs=(
            P(("groups", "expert"), "replica"),
            P(("groups", "expert"), None),
            P(("groups", "expert"), None),
            P("expert", "replica", None),
            P("expert", None, "replica"),
            P("replica", None),
            P(("groups", "expert")),
            P(("groups", "expert"), None),
            P(("groups", "expert"), None),
            P("expert", "replica", None),
            P("expert", None, "replica"),
        ),
        out_specs=(P(("groups", "expert"), "replica"), P(("groups", "expert"), "replica")),
        check_vma=False,
    )
```
